32 devices in a mesh: dp: 4 (over z), ctx: 8 (over y, x, core).
Axes of the slice: x: 2, y: 2, z: 4, core: 2. Of those that a mesh axis runs over, the one named last changes fastest.
Arguments:
- tokens: bfloat16 [4, 1024, 2048], P('dp', 'ctx'), may hold values from -6 to 6
- routes: int32 [4, 1024, 8], P('dp', 'ctx'), may hold values from 0 to 15, all different within a row; in each aligned block of 128 rows (0 to 127, 128 to 255, ..., all dimensions but the last counted through in order) at most 96 rows name the same one
- cotangent: bfloat16 [4, 1024, 2048], P('dp', 'ctx'), may hold values from -6 to 6
- attn_gain: bfloat16 [2048], P(('dp', 'ctx')), may hold values from 0.099609375 to 1.8984375
- query_weight: bfloat16 [2048, 2048], P(('dp', 'ctx')), may hold values from -0.125 to 0.125
- key_weight: bfloat16 [2048, 2048], P(('dp', 'ctx')), may hold values from -0.125 to 0.125
- value_weight: bfloat16 [2048, 2048], P(('dp', 'ctx')), may hold values from -0.125 to 0.125
- query_gain: bfloat16 [2048], P(('dp', 'ctx')), may hold values from 0.099609375 to 1.8984375
- key_gain: bfloat16 [2048], P(('dp', 'ctx')), may hold values from 0.099609375 to 1.8984375
- out_weight: bfloat16 [2048, 2048], P(('dp', 'ctx')), may hold values from -2 to 2
- mlp_gain: bfloat16 [2048], P(('dp', 'ctx')), may hold values from 0.099609375 to 1.8984375
- router_weight: bfloat16 [2048, 16], P(('dp', 'ctx')), may hold values from -0.0625 to 0.0625
- gate_weight: bfloat16 [32, 2048, 512], P(('dp', 'ctx')), may hold values from -0.125 to 0.125
- up_weight: bfloat16 [32, 2048, 512], P(('dp', 'ctx')), may hold values from -0.125 to 0.125
- down_weight: bfloat16 [32, 512, 2048], P(('dp', 'ctx')), may hold values from -2.5 to 2.5
Outputs:
- layer_out: bfloat16 [4, 1024, 2048], P('dp', 'ctx')
- grad_tokens: bfloat16 [4, 1024, 2048], P('dp', 'ctx')
- grad_attn_gain: float32 [2048], P(('dp', 'ctx'))
- grad_query_weight: float32 [2048, 2048], P(('dp', 'ctx'))
- grad_key_weight: float32 [2048, 2048], P(('dp', 'ctx'))
- grad_value_weight: float32 [2048, 2048], P(('dp', 'ctx'))
- grad_query_gain: float32 [2048], P(('dp', 'ctx'))
- grad_key_gain: float32 [2048], P(('dp', 'ctx'))
- grad_out_weight: float32 [2048, 2048], P(('dp', 'ctx'))
- grad_mlp_gain: float32 [2048], P(('dp', 'ctx'))
- grad_router_weight: float32 [2048, 16], P(('dp', 'ctx'))
- grad_gate_weight: float32 [32, 2048, 512], P(('dp', 'ctx'))
- grad_up_weight: float32 [32, 2048, 512], P(('dp', 'ctx'))
- grad_down_weight: float32 [32, 512, 2048], P(('dp', 'ctx'))
The draws below stay inside these ranges and needn't reach their ends.
Inputs may be any that keep to these rules, and one draw needn't show every extreme that they name: `routes`: within the 128 rows of one device at most 96 rows name the same expert, a bound that some block reaches of them; a row names 8 different experts.
All inputs are finite; a program needn't handle non-finite values.
Results may differ from the reference program's by a relative error of at most 0.028.
Values may be sent and summed in bfloat16 or wider, within the bound.
No kernel may reach another device: no remote copies, remote signals or barrier semaphores. Data moves between devices by JAX's collectives and lax.ppermute only.
A program may use at most 320 MiB of HBM per device.

```python
import math
import jax
import jax.numpy as jnp
import numpy as np
from jax import lax

D = 2048
HEADS = 16
HEAD_DIM = 128
FF = 1024
TOP = 8
TOK_DEV = 128
BLOCK = 64
SEQ = 1024
SEQS = 4
EXPERTS = 16
HALF = 512
HALVES = 32
CAP = 96
N_CTX = 8


def levels(key, shape, split, low, largest):
    loudness = 1.0
    for dim, blocks in split:
        heights = jax.random.uniform(jax.random.fold_in(jax.random.fold_in(key, 6), dim), (blocks,), jnp.float32, low / len(split), largest / len(split))
        loudness = loudness * jnp.repeat(jnp.exp(heights), shape[dim] // blocks).reshape((-1,) + (1,) * (len(shape) - 1 - dim))
    return loudness


def deal_out(key, own, number, rows, amount, top, most, skew):
    order = jax.random.permutation(key, amount)
    heavy_load, usual = load_shares(amount, rows * top, most, skew, True), load_shares(amount, rows * top, most, skew, False)
    places = jnp.arange(amount)

    def named(tallies, turn):
        used = int((tallies > 0).sum())
        fixed = max(1, used // 4)
        shifted = fixed + (places - fixed + turn * (used - fixed)) % max(1, amount - fixed)
        return jnp.zeros((amount,), jnp.int32).at[order[jnp.where(places < fixed, places, shifted)]].set(jnp.asarray(tallies, jnp.int32))

    tallies = jnp.where(number % 4 == 0, named(heavy_load, number // 4), named(usual, number - number // 4 - 1))
    mixed = jax.random.permutation(jax.random.fold_in(own, 3), amount)
    donor, taker = mixed[0:amount // 2 * 2:2], mixed[1:amount // 2 * 2:2]
    slack = jnp.minimum(tallies[donor] - 1, most - tallies[taker]) // 2
    slack = jnp.where((donor == order[0]) | (taker == order[0]) | (tallies[taker] == 0), 0, jnp.maximum(slack, 0))
    shifted = jax.random.randint(jax.random.fold_in(own, 4), (amount // 2,), 0, 1 << 20) % (slack + 1)
    tallies = tallies.at[donor].add(-shifted).at[taker].add(shifted)
    items = jnp.searchsorted(jnp.cumsum(tallies), jnp.arange(rows * top), side="right").astype(jnp.int32)
    grid = items.reshape(top, rows).T
    grid = grid[jax.random.permutation(jax.random.fold_in(own, 1), rows)]
    turn = jax.random.randint(jax.random.fold_in(own, 2), (rows, 1), 0, top)
    return jnp.take_along_axis(grid, (jnp.arange(top)[None, :] + turn) % top, axis=1)


def load_shares(amount, total, reach, skew, full):
    portions = [(1 << 20) // math.isqrt(standing ** skew) + 1 for standing in range(1, amount + 1)]
    largest = reach if full else min(reach, max(-(-total // amount), total * portions[0] // sum(portions)))
    least = 1 if total - largest >= amount - 1 else 0
    counts, rest = [largest] + [least] * (amount - 1), total - largest - least * (amount - 1)
    while rest > 0:
        movable = [i for i in range(1, amount) if counts[i] < largest] or [i for i in range(1, amount) if counts[i] < reach]
        mass, left = sum([portions[i] for i in movable]), rest
        for i in movable:
            more = min(reach - counts[i], max(1, left * portions[i] // mass), rest)
            counts[i] = counts[i] + more
            rest = rest - more
    return np.array(counts)


def bell_draw(stream_key, shape, scale, most, split=(), kind=jnp.bfloat16):
    factor_of = levels(stream_key, shape, split, -0.22, 0.18) if split else 1.0
    entries = jax.random.normal(stream_key, shape, jnp.float32) * scale * factor_of
    return jnp.minimum(jnp.maximum(entries, -most), most).astype(kind)


def setup_inputs(seed: int = 0) -> dict:
    keys = jax.random.split(jax.random.key(seed), 16)
    tokens = bell_draw(keys[0], (SEQS, SEQ, D), 1.0, 6.0, ((0, 4), (1, 8)))
    routes_keys = jax.random.split(jax.random.fold_in(keys[1], 1), SEQS * SEQ // TOK_DEV)
    routes_turns = jax.random.permutation(jax.random.fold_in(keys[1], 3), SEQS * SEQ // TOK_DEV)
    routes = jax.vmap(lambda own, number: deal_out(jax.random.fold_in(keys[1], 2), own, number, TOK_DEV, EXPERTS, TOP, CAP, 1))(routes_keys, routes_turns).reshape((SEQS, SEQ, TOP))
    cotangent = bell_draw(keys[2], (SEQS, SEQ, D), 1.0, 6.0, ((0, 4), (1, 8)))
    attn_gain = jnp.clip(1.0 + 0.18 * jax.random.normal(keys[3], (D,), jnp.float32), 0.099609375, 1.8984375).astype(jnp.bfloat16)
    query_weight = bell_draw(keys[4], (D, D), D ** -0.5, 0.125, ((0, 32),))
    key_weight = bell_draw(keys[5], (D, D), D ** -0.5, 0.125, ((0, 32),))
    value_weight = bell_draw(keys[6], (D, D), D ** -0.5, 0.125, ((0, 32),))
    query_gain = jnp.clip(1.0 + 0.18 * jax.random.normal(keys[7], (D,), jnp.float32), 0.099609375, 1.8984375).astype(jnp.bfloat16)
    key_gain = jnp.clip(1.0 + 0.18 * jax.random.normal(keys[8], (D,), jnp.float32), 0.099609375, 1.8984375).astype(jnp.bfloat16)
    out_weight = bell_draw(keys[9], (D, D), (max(1, 4 * D // SEQ)) ** -0.5, 2.0, ((0, 32),))
    mlp_gain = jnp.clip(1.0 + 0.18 * jax.random.normal(keys[10], (D,), jnp.float32), 0.099609375, 1.8984375).astype(jnp.bfloat16)
    router_weight = bell_draw(keys[11], (D, EXPERTS), (4 * D) ** -0.5, 0.0625, ((0, 32),))
    gate_weight = bell_draw(keys[12], (HALVES, D, HALF), D ** -0.5, 0.125, ((0, 32),))
    up_weight = bell_draw(keys[13], (HALVES, D, HALF), D ** -0.5, 0.125, ((0, 32),))
    down_weight = bell_draw(keys[14], (HALVES, HALF, D), (max(1, 3 * FF // (2 * EXPERTS * EXPERTS))) ** -0.5, 2.5, ((0, 32),))
    return dict(tokens=tokens, routes=routes, cotangent=cotangent, attn_gain=attn_gain, query_weight=query_weight, key_weight=key_weight, value_weight=value_weight, query_gain=query_gain, key_gain=key_gain, out_weight=out_weight, mlp_gain=mlp_gain, router_weight=router_weight, gate_weight=gate_weight, up_weight=up_weight, down_weight=down_weight)


@jax.custom_vjp
def low(v):
    return lax.optimization_barrier(v.astype(jnp.bfloat16)).astype(jnp.float32)

@jax.custom_vjp
def low_back(v):
    return v

def low_keep(v):
    return (low(v), None)

def low_pass(kept, grad):
    return (grad,)

def back_keep(v):
    return (v, None)

def back_low(kept, grad):
    return (low(grad),)
low.defvjp(low_keep, low_pass)
low_back.defvjp(back_keep, back_low)
EPSILON = 1e-05
HIGH = lax.Precision.HIGHEST
NEG_LARGE = -1e+30

def rms_scale(tensor, gain_vec):
    return tensor * lax.rsqrt(lax.optimization_barrier(jnp.mean(tensor * tensor, axis=-1, keepdims=True)) + EPSILON) * gain_vec

def layout_positions():
    row_index = jnp.arange(SEQ, dtype=jnp.int32)
    device = row_index // TOK_DEV
    within = row_index % TOK_DEV
    return jnp.where(within < BLOCK, device * BLOCK + within, (2 * N_CTX - 1 - device) * BLOCK + within - BLOCK)

def rotary_tables(position):
    freq_index = jnp.arange(HEAD_DIM // 2, dtype=jnp.float32)
    inverse = jnp.exp(freq_index * (-2.0 * math.log(10000.0) / HEAD_DIM))
    angles = position.astype(jnp.float32)[:, None] * inverse[None, :]
    return (jnp.cos(angles), jnp.sin(angles))

def rotate(tensor, cosine, sine_table):
    half_dim = tensor.shape[-1] // 2
    first_half = tensor[..., :half_dim]
    second_half = tensor[..., half_dim:]
    cos_part = cosine[:, None, :]
    sin_part = sine_table[:, None, :]
    return jnp.concatenate([first_half * cos_part - second_half * sin_part, second_half * cos_part + first_half * sin_part], axis=-1)

def attention(query_rot, key_rot, value_heads, position):
    query_block = min(512, SEQ)
    block_count = SEQ // query_block
    score_scale = 1.0 / math.sqrt(HEAD_DIM)

    @jax.checkpoint
    def one_block(block_index):
        first_row = block_index * query_block
        queries = lax.dynamic_slice_in_dim(query_rot, first_row, query_block, 0)
        query_pos = lax.dynamic_slice_in_dim(position, first_row, query_block, 0)
        scores = low_back(jnp.einsum('qhd,khd->hqk', queries, key_rot, precision=HIGH) * score_scale)
        allowed = position[None, None, :] <= query_pos[None, :, None]
        masked = jnp.where(allowed, scores, NEG_LARGE)
        weights = jax.nn.softmax(masked, axis=-1)
        return jnp.einsum('hqk,khd->qhd', low(weights), value_heads, precision=HIGH)
    blocks = lax.map(one_block, jnp.arange(block_count, dtype=jnp.int32))
    return blocks.reshape(SEQ, HEADS * HEAD_DIM)

def experts(normed_two, weights_dense, gate_weight, up_weight, down_weight):

    @jax.checkpoint
    def one_half(running, inputs):
        gate_part, up_part, down_part, half_index = inputs
        expert_id = half_index // 2
        copied = low_back(normed_two)
        gate_pre = low_back(jnp.dot(copied, gate_part, precision=HIGH))
        up_pre = low_back(jnp.dot(copied, up_part, precision=HIGH))
        hidden = low(jax.nn.silu(gate_pre) * up_pre)
        half_out = low(low_back(jnp.dot(hidden, down_part, precision=HIGH)))
        column = lax.dynamic_slice_in_dim(weights_dense, expert_id, 1, 1)
        return (running + column * half_out, None)
    running, ignored = lax.scan(one_half, jnp.zeros_like(normed_two), (gate_weight, up_weight, down_weight, jnp.arange(HALVES, dtype=jnp.int32)))
    return running

def sequence_forward(params, tokens_seq, routes_seq):
    attn_gain, query_weight, key_weight, value_weight, query_gain, key_gain, out_weight, mlp_gain, router_weight, gate_weight, up_weight, down_weight = params
    normed = low(rms_scale(tokens_seq, attn_gain))
    query_pre = low_back(jnp.dot(normed, query_weight, precision=HIGH))
    key_pre = low_back(jnp.dot(normed, key_weight, precision=HIGH))
    value_rows = low(low_back(jnp.dot(normed, value_weight, precision=HIGH)))
    position = layout_positions()
    cosine, sine_table = rotary_tables(position)
    query_rot = low(rotate(rms_scale(query_pre, query_gain).reshape(SEQ, HEADS, HEAD_DIM), cosine, sine_table))
    key_rot = low(rotate(rms_scale(key_pre, key_gain).reshape(SEQ, HEADS, HEAD_DIM), cosine, sine_table))
    attended = attention(query_rot, key_rot, value_rows.reshape(SEQ, HEADS, HEAD_DIM), position)
    attended = low(low_back(attended))
    branch = low_back(jnp.dot(attended, out_weight, precision=HIGH))
    middle = tokens_seq + branch
    normed_two = low(rms_scale(middle, mlp_gain))
    logits = low_back(jnp.dot(normed_two, router_weight, precision=HIGH))
    router_probs = jax.nn.softmax(logits, axis=-1)
    chosen = routes_seq[:, :, None] == jnp.arange(EXPERTS, dtype=jnp.int32)[None, None, :]
    weights_dense = router_probs * lax.optimization_barrier(jnp.sum(chosen.astype(router_probs.dtype), axis=1))
    mixture = experts(normed_two, weights_dense, gate_weight, up_weight, down_weight)
    return middle + mixture

def reference(tokens, routes, cotangent, attn_gain, query_weight, key_weight, value_weight, query_gain, key_gain, out_weight, mlp_gain, router_weight, gate_weight, up_weight, down_weight):
    params = tuple((weight.astype(jnp.float32) for weight in (attn_gain, query_weight, key_weight, value_weight, query_gain, key_gain, out_weight, mlp_gain, router_weight, gate_weight, up_weight, down_weight)))
    tokens_f = tokens.astype(jnp.float32)

    def forward(tokens_all, weights_all):

        @jax.checkpoint
        def per_sequence(inputs):
            return sequence_forward(weights_all, inputs[0], inputs[1])
        return lax.map(per_sequence, (tokens_all, routes))
    result, pullback = jax.vjp(forward, tokens_f, params)
    grad_tokens, grads = pullback(cotangent.astype(jnp.float32))
    return (result.astype(jnp.bfloat16), grad_tokens.astype(jnp.bfloat16), grads[0], grads[1], grads[2], grads[3], grads[4], grads[5], grads[6], grads[7], grads[8], grads[9], grads[10], grads[11])
```

```python
import math

import jax
import jax.numpy as jnp
import numpy as np
from jax import lax
from jax.sharding import PartitionSpec as P

HEADS = 16
HEAD_DIM = 128
TOP = 8

EPSILON = 1e-05
NEG_LARGE = -1e30
BF = jnp.bfloat16
F32 = jnp.float32
ALL = ("dp", "ctx")


def dot(left, right):
    return jnp.dot(left, right, preferred_element_type=F32)


def contract_rows(left, right):
    return lax.dot_general(left, right, (((0,), (0,)), ((), ())), preferred_element_type=F32)


def times_transposed(left, right):
    return lax.dot_general(left, right, (((1,), (1,)), ((), ())), preferred_element_type=F32)


def rotary_tables(position, head_dim):
    freq_index = jnp.arange(head_dim // 2, dtype=F32)
    inverse = jnp.exp(freq_index * (-2.0 * math.log(10000.0) / head_dim))
    angles = position.astype(F32)[:, None] * inverse[None, :]
    return (jnp.cos(angles), jnp.sin(angles))


def rotate(tensor, cosine, sine_table, direction):
    half_dim = tensor.shape[-1] // 2
    first_half = tensor[..., :half_dim]
    second_half = tensor[..., half_dim:]
    cos_part = cosine[:, None, :]
    sin_part = sine_table[:, None, :] * direction
    return jnp.concatenate(
        [
            first_half * cos_part - second_half * sin_part,
            second_half * cos_part + first_half * sin_part,
        ],
        axis=-1,
    )


def inverse_rms(tensor):
    return lax.rsqrt(jnp.mean(tensor * tensor, axis=-1, keepdims=True) + EPSILON)


def norm_backward(tensor, inverse, gain_vec, grad_in):
    scaled = grad_in * gain_vec
    grad_gain = jnp.sum(grad_in * tensor * inverse, axis=0)
    grad_tensor = inverse * scaled - tensor * (inverse * inverse * inverse) * jnp.mean(
        scaled * tensor, axis=-1, keepdims=True
    )
    return (grad_tensor, grad_gain)


class Layout:
    def __init__(self, rb):
        self.nz = lax.axis_size("dp")
        self.nc = lax.axis_size("ctx")
        self.dz = lax.axis_index("dp")
        self.cx = lax.axis_index("ctx")
        nz, nc = self.nz, self.nc
        order = [0] + list(range(1, nz, 2)) + list(range(nz - 2 + nz % 2, 0, -2))
        self.order = np.array(order, np.int32)
        place = np.zeros(nz, np.int32)
        place[self.order] = np.arange(nz)
        self.place = place
        self.ring = [(order[i], order[(i + 1) % nz]) for i in range(nz)]
        self.pos = jnp.asarray(place)[self.dz]
        bits = [1 << b for b in range(1, (nc - 1).bit_length())]
        self.bits = (bits + [1], bits[::-1] + [1])
        self.slots = []
        for steps in self.bits:
            held = [0]
            for bit in steps:
                held = held + [h ^ bit for h in held]
            self.slots.append(np.array(held, np.int32))
        self.where = []
        for held in self.slots:
            inv = np.zeros(nc, np.int32)
            inv[held] = np.arange(nc)
            self.where.append(inv)
        self.hpd = HEADS // nc
        self.cols = self.hpd * HEAD_DIM
        self.group = HEAD_DIM // rb
        self.rb = rb

    def swap(self, value, bit):
        return lax.ppermute(value, "ctx", [(i, i ^ bit) for i in range(self.nc)])

    def ring_step(self, value):
        return lax.ppermute(value, "dp", self.ring)

    def layer_at(self, step):
        return jnp.asarray(self.order)[(self.pos - step) % self.nz]

    def gather_ring(self, block):
        blocks = [block]
        for _ in range(self.nz - 1):
            blocks.append(self.ring_step(blocks[-1]))
        return blocks

    def assemble_ring(self, blocks):
        rows = blocks[0].shape[0]
        whole = jnp.zeros((self.nz * rows,) + blocks[0].shape[1:], blocks[0].dtype)
        for step, block in enumerate(blocks):
            whole = lax.dynamic_update_slice_in_dim(whole, block, self.layer_at(step) * rows, 0)
        return whole

    def gather_ctx(self, value):
        half = value.shape[0] // 2
        outs = []
        for color in (0, 1):
            held = value[color * half : (color + 1) * half][None]
            for bit in self.bits[color]:
                held = jnp.concatenate([held, self.swap(held, bit)], axis=0)
            outs.append(held)
        return outs

    def reduce_ctx(self, value, color):
        for bit in self.bits[color][::-1]:
            keep = value.shape[0] // 2
            other = self.swap(value[keep:], bit)
            value = (value[:keep].astype(F32) + other.astype(F32)).astype(BF)
        return value[0]

    def reduce_ring(self, parts):
        total = parts(1)
        for step in list(range(2, self.nz)) + [0]:
            total = (self.ring_step(total).astype(F32) + parts(step).astype(F32)).astype(BF)
        return total

    def slots_to_devices(self, value):
        devices = jnp.arange(self.nc) ^ self.cx
        return jnp.stack([value[k][jnp.asarray(self.where[k])[devices]] for k in (0, 1)])

    def devices_to_slots(self, value):
        return jnp.stack([value[k][jnp.asarray(self.slots[k]) ^ self.cx] for k in (0, 1)])

    def head_blocks(self, value):
        rows = value.shape[0]
        split = value.reshape(rows, self.group, self.hpd, self.nc // self.group, HEAD_DIM)
        return split.transpose(3, 1, 0, 2, 4).reshape(self.nc, rows, self.cols)

    def head_rows(self, value):
        rows = value.shape[1]
        split = value.reshape(self.nc // self.group, self.group, rows, self.hpd, HEAD_DIM)
        return split.transpose(2, 1, 3, 0, 4).reshape(rows, self.nc * self.cols)

    def own_heads(self, vector):
        return self.head_blocks(vector[None])[self.cx, 0]

    def all_heads(self, vector):
        whole = jnp.zeros((self.nc, 1, self.cols), vector.dtype)
        whole = lax.dynamic_update_slice(whole, vector[None, None], (self.cx, 0, 0))
        return self.head_rows(whole)[0]


def a2a(value, axes):
    return lax.all_to_all(value, axes, split_axis=0, concat_axis=0, tiled=True)


def experts_gathered(lay, mlp_normed, routes, router_probs, dy_all, gate_w, up_w, down_w):
    nz, nc = lay.nz, lay.nc
    devices = nz * nc
    tok_rows, width = mlp_normed.shape
    half = tok_rows // 2
    expert_count = router_probs.shape[1]
    chosen = jnp.any(routes[:, :, None] == jnp.arange(expert_count, dtype=jnp.int32), axis=1)
    combine = jnp.where(chosen, router_probs, 0.0)
    gates = a2a(jnp.repeat(combine.T, 2, axis=0), ALL)
    layers = jnp.stack([lay.layer_at(step) for step in range(nz)])
    gates = gates.reshape(nz, nc, 2, half)[layers]
    gates = jnp.stack(
        [gates[:, jnp.asarray(lay.slots[k]) ^ lay.cx, k] for k in (0, 1)], axis=1
    ).reshape(devices * tok_rows, 1)
    dy = dy_all.reshape(nz, nc, 2, half, width)[layers]
    dy = jnp.stack(
        [dy[:, jnp.asarray(lay.slots[k]) ^ lay.cx, k] for k in (0, 1)], axis=1
    ).reshape(devices * tok_rows, width)
    chunks = []
    for block in lay.gather_ring(mlp_normed):
        chunks += lay.gather_ctx(block)
    rows = jnp.concatenate(chunks, axis=0).reshape(devices * tok_rows, width)
    gate_pre = dot(rows, gate_w)
    up_pre = dot(rows, up_w)
    sigmoid_val = jax.nn.sigmoid(gate_pre)
    silu = gate_pre * sigmoid_val
    hidden_f = silu * up_pre
    hidden = hidden_f.astype(BF)
    partial_out = (gates * dot(hidden, down_w)).astype(BF)
    grad_hidden = times_transposed(dy, down_w)
    weighted = jnp.sum(grad_hidden * hidden.astype(F32), axis=-1) * gates[:, 0]
    grad_hidden = grad_hidden * gates
    grad_gate_pre = (
        grad_hidden * up_pre * sigmoid_val * (1.0 + gate_pre * (1.0 - sigmoid_val))
    ).astype(BF)
    grad_up_pre = (grad_hidden * silu).astype(BF)
    grad_copy = (
        times_transposed(grad_gate_pre, gate_w) + times_transposed(grad_up_pre, up_w)
    ).astype(BF)
    grad_down_w = contract_rows((hidden.astype(F32) * gates).astype(BF), dy)
    grad_gate_w = contract_rows(rows, grad_gate_pre)
    grad_up_w = contract_rows(rows, grad_up_pre)

    def reduce_all(value):
        value = value.reshape(nz, 2, nc, half, width)

        def parts(step):
            return jnp.concatenate([lay.reduce_ctx(value[step, k], k) for k in (0, 1)], axis=0)

        return lay.reduce_ring(parts).astype(F32)

    places = jnp.asarray(lay.place)
    weighted = weighted.reshape(nz, 2, nc, half)[(lay.pos - places) % nz]
    flip = jnp.arange(nc) ^ lay.cx
    weighted = jnp.concatenate(
        [weighted[:, k][:, jnp.asarray(lay.where[k])[flip]] for k in (0, 1)], axis=-1
    ).reshape(devices, tok_rows)
    weighted = a2a(weighted, ALL).reshape(expert_count, 2, tok_rows).sum(1).T
    grad_sum = reduce_all(grad_copy)
    mixture = reduce_all(partial_out)
    return (mixture, grad_sum, weighted, grad_gate_w, grad_up_w, grad_down_w)


def experts_sent(lay, mlp_normed, routes, router_probs, grad_result, gate_w, up_w, down_w):
    tok_rows, width = mlp_normed.shape
    expert_count = router_probs.shape[1]
    capacity = 3 * tok_rows * TOP // (2 * expert_count)
    flat_routes = routes.reshape(tok_rows * TOP)
    onehot = (flat_routes[:, None] == jnp.arange(expert_count, dtype=jnp.int32)[None, :]).astype(
        jnp.int32
    )
    slot_index = jnp.sum((jnp.cumsum(onehot, axis=0) - onehot) * onehot, axis=1)
    chosen = onehot.reshape(tok_rows, TOP, expert_count).astype(F32)
    gate_values = jnp.einsum("tke,te->tk", chosen, router_probs)

    def dispatch(rows_in):
        sent = jnp.zeros((expert_count, capacity, width), BF).at[flat_routes, slot_index].set(rows_in)
        return a2a(jnp.repeat(sent, 2, axis=0), ALL)

    def collect(buffer):
        even_rows = buffer[2 * flat_routes, slot_index].astype(F32)
        odd_rows = buffer[2 * flat_routes + 1, slot_index].astype(F32)
        return (even_rows + odd_rows).reshape(tok_rows, TOP, width)

    received = dispatch(jnp.repeat(mlp_normed, TOP, axis=0))
    flat_in = received.reshape(-1, width)
    gate_pre = dot(flat_in, gate_w)
    up_pre = dot(flat_in, up_w)
    hidden = (jax.nn.silu(gate_pre) * up_pre).astype(BF)
    half_out = dot(hidden, down_w).astype(BF).reshape(received.shape)
    expert_rows = collect(a2a(half_out, ALL))
    mixture = jnp.einsum("tk,tkd->td", gate_values, expert_rows)
    grad_gates = jnp.einsum("td,tkd->tk", grad_result, expert_rows)
    grad_rows = (
        (gate_values[:, :, None] * grad_result[:, None, :])
        .astype(BF)
        .reshape(tok_rows * TOP, width)
    )
    grad_flat = dispatch(grad_rows).reshape(-1, width)
    grad_down_w = contract_rows(hidden, grad_flat)
    grad_hidden = times_transposed(grad_flat, down_w)
    sigmoid_val = jax.nn.sigmoid(gate_pre)
    grad_gate_pre = (
        grad_hidden * up_pre * sigmoid_val * (1.0 + gate_pre * (1.0 - sigmoid_val))
    ).astype(BF)
    grad_up_pre = (grad_hidden * jax.nn.silu(gate_pre)).astype(BF)
    grad_gate_w = contract_rows(flat_in, grad_gate_pre)
    grad_up_w = contract_rows(flat_in, grad_up_pre)
    grad_copy = (
        (times_transposed(grad_gate_pre, gate_w) + times_transposed(grad_up_pre, up_w))
        .astype(BF)
        .reshape(received.shape)
    )
    grad_sum = jnp.sum(collect(a2a(grad_copy, ALL)), axis=1)
    weighted = router_probs * jnp.einsum("tk,tke->te", grad_gates, chosen)
    return (mixture, grad_sum, weighted, grad_gate_w, grad_up_w, grad_down_w)


def body(
    tokens,
    routes,
    cotangent,
    attn_gain,
    query_weight,
    key_weight,
    value_weight,
    query_gain,
    key_gain,
    out_weight,
    mlp_gain,
    router_weight,
    gate_weight,
    up_weight,
    down_weight,
):
    rb = query_weight.shape[0]
    lay = Layout(rb)
    nz, nc, cx = lay.nz, lay.nc, lay.cx
    tok_rows = tokens.shape[1]
    width = tokens.shape[2]
    half = tok_rows // 2
    seq_rows = tok_rows * nc
    expert_count = router_weight.shape[1]
    hpd, cols = lay.hpd, lay.cols
    devices = nz * nc
    score_scale = 1.0 / math.sqrt(HEAD_DIM)
    capacity = 3 * tok_rows * TOP // (2 * expert_count)
    gathered = devices * tok_rows <= 4 * expert_count * capacity

    lanes = -(-(expert_count + 4) // 128) * 128
    small = jnp.concatenate(
        [router_weight]
        + [g[:, None] for g in (attn_gain, query_gain, key_gain, mlp_gain)]
        + [jnp.zeros((rb, lanes - expert_count - 4), BF)],
        axis=1,
    )
    small = lax.all_gather(small, ALL, axis=0, tiled=True)
    router_w = small[:, :expert_count]
    attn_gain_f, qgain_f, kgain_f, mlp_gain_f = (
        small[:, expert_count + k].astype(F32) for k in range(4)
    )
    sent = jnp.concatenate(
        [lay.head_blocks(w) for w in (query_weight, key_weight, value_weight)], axis=-1
    )
    block = a2a(sent, "ctx").reshape(nc * rb, 3 * cols)
    qkv_w = lay.assemble_ring(lay.gather_ring(block))
    inputs_all = jnp.concatenate(lay.gather_ctx(tokens[0]), axis=0).reshape(seq_rows, width)
    out_w = lax.all_gather(out_weight, ALL, axis=0, tiled=True)
    dy_all = lax.all_gather(cotangent[0], ALL, axis=0, tiled=True) if gathered else None

    inputs_all = inputs_all.astype(F32)
    attn_inv_all = inverse_rms(inputs_all)
    normed = (inputs_all * attn_inv_all * attn_gain_f).astype(BF)
    qkv = dot(normed, qkv_w)
    query_pre, key_pre = qkv[:, :cols], qkv[:, cols : 2 * cols]
    value_rows = qkv[:, 2 * cols :].astype(BF).reshape(seq_rows, hpd, HEAD_DIM)

    def sum_heads(first, second):
        stats = jnp.stack([jnp.sum(first, axis=-1), jnp.sum(second, axis=-1)], axis=-1)
        stats = lay.slots_to_devices(stats.reshape(2, nc, half, 2))
        stats = stats.reshape(2 * nc * half * 2 // 128, 128)
        stats = lax.all_gather(stats, "ctx", axis=0).sum(0)
        stats = lay.devices_to_slots(stats.reshape(2, nc, half, 2)).reshape(seq_rows, 2)
        return stats[:, :1] / width, stats[:, 1:] / width

    query_ms, key_ms = sum_heads(query_pre * query_pre, key_pre * key_pre)
    query_inv, key_inv = lax.rsqrt(query_ms + EPSILON), lax.rsqrt(key_ms + EPSILON)
    own_qgain, own_kgain = lay.own_heads(qgain_f), lay.own_heads(kgain_f)
    row = jnp.arange(half, dtype=jnp.int32)
    owners = [jnp.asarray(lay.slots[k]) ^ cx for k in (0, 1)]
    positions = jnp.concatenate(
        [
            (owners[0][:, None] * half + row).reshape(-1),
            ((2 * nc - 1 - owners[1])[:, None] * half + row).reshape(-1),
        ]
    )
    cosine, sine = rotary_tables(positions, HEAD_DIM)
    query_rot = rotate(
        (query_pre * query_inv * own_qgain).reshape(seq_rows, hpd, HEAD_DIM), cosine, sine, 1.0
    ).astype(BF)
    key_rot = rotate(
        (key_pre * key_inv * own_kgain).reshape(seq_rows, hpd, HEAD_DIM), cosine, sine, 1.0
    ).astype(BF)

    allowed = positions[None, None, :] <= positions[None, :, None]
    scores = jnp.einsum("qhd,khd->hqk", query_rot, key_rot, preferred_element_type=F32) * score_scale
    masked = jnp.where(allowed, scores, NEG_LARGE)
    top = jnp.max(masked, axis=-1, keepdims=True)
    unnormed = jnp.exp(masked - top)
    total = jnp.sum(unnormed, axis=-1, keepdims=True)
    probs_f = unnormed / total
    probs_b = probs_f.astype(BF)
    attended_f = jnp.einsum("hqk,khd->qhd", probs_b, value_rows, preferred_element_type=F32)
    attended_b = attended_f.reshape(seq_rows, cols).astype(BF)

    def rows_to_devices(value):
        value = lay.slots_to_devices(value.reshape(2, nc, half, cols))
        return a2a(value.transpose(1, 0, 2, 3).reshape(nc, tok_rows, cols), "ctx")

    attended_own = lay.head_rows(rows_to_devices(attended_b))
    inputs_f = tokens[0].astype(F32)
    middle = inputs_f + dot(attended_own, out_w)
    mlp_inv = inverse_rms(middle)
    mlp_normed = (middle * mlp_inv * mlp_gain_f).astype(BF)
    router_probs = jax.nn.softmax(dot(mlp_normed, router_w), axis=-1)
    grad_result = cotangent[0].astype(F32)
    if gathered:
        moe = experts_gathered(
            lay, mlp_normed, routes[0], router_probs, dy_all, gate_weight[0], up_weight[0], down_weight[0]
        )
    else:
        moe = experts_sent(
            lay, mlp_normed, routes[0], router_probs, grad_result, gate_weight[0], up_weight[0], down_weight[0]
        )
    mixture, grad_mlp_normed, weighted, grad_gate_w, grad_up_w, grad_down_w = moe
    result = middle + mixture
    grad_logits = (weighted - router_probs * jnp.sum(weighted, axis=-1, keepdims=True)).astype(BF)
    grad_router_w = contract_rows(mlp_normed, grad_logits)
    grad_mlp_normed = grad_mlp_normed + times_transposed(grad_logits, router_w)
    grad_middle_norm, grad_mlp_gain = norm_backward(middle, mlp_inv, mlp_gain_f, grad_mlp_normed)
    grad_middle = grad_result + grad_middle_norm
    grad_branch = grad_middle.astype(BF)
    grad_attended = times_transposed(grad_branch, out_w).astype(BF)
    grad_heads = a2a(lay.head_blocks(grad_attended), "ctx").reshape(nc, 2, half, cols)
    grad_heads = lay.devices_to_slots(grad_heads.transpose(1, 0, 2, 3))
    grad_heads = grad_heads.reshape(seq_rows, hpd, HEAD_DIM)

    branch_all = jnp.concatenate(lay.gather_ctx(grad_branch), axis=0).reshape(seq_rows, width)
    grad_out = contract_rows(attended_b, branch_all).astype(BF).reshape(hpd, lay.group, rb, width)
    share = cx % lay.group
    terms = []
    for k in range(lay.group):
        term = lax.dynamic_index_in_dim(grad_out, share ^ k, 1, keepdims=False)
        terms.append(lay.swap(term, k) if k else term)
    terms = jnp.stack(terms)

    def out_part(step):
        layer = lay.layer_at(step)
        return terms[(layer // hpd) ^ share, layer % hpd]

    grad_out_w = lay.reduce_ring(out_part).astype(F32)

    row_delta = jnp.einsum("qhd,qhd->hq", grad_heads.astype(F32), attended_f)
    grad_probs = jnp.einsum("qhd,khd->hqk", grad_heads, value_rows, preferred_element_type=F32)
    grad_scores = (probs_f * (grad_probs - row_delta[..., None])).astype(BF)
    grad_query_rot = jnp.einsum("hqk,khd->qhd", grad_scores, key_rot, preferred_element_type=F32)
    grad_key_rot = jnp.einsum("hqk,qhd->khd", grad_scores, query_rot, preferred_element_type=F32)
    grad_value = jnp.einsum("hqk,qhd->khd", probs_b, grad_heads, preferred_element_type=F32)
    grad_query_norm = rotate(grad_query_rot * score_scale, cosine, sine, -1.0).reshape(seq_rows, cols)
    grad_key_norm = rotate(grad_key_rot * score_scale, cosine, sine, -1.0).reshape(seq_rows, cols)
    grad_query_gain = jnp.sum(grad_query_norm * query_pre * query_inv, axis=0)
    grad_key_gain = jnp.sum(grad_key_norm * key_pre * key_inv, axis=0)
    scaled_q, scaled_k = grad_query_norm * own_qgain, grad_key_norm * own_kgain
    query_dot, key_dot = sum_heads(scaled_q * query_pre, scaled_k * key_pre)
    grad_query_pre = query_inv * scaled_q - query_pre * (query_inv * query_inv * query_inv) * query_dot
    grad_key_pre = key_inv * scaled_k - key_pre * (key_inv * key_inv * key_inv) * key_dot
    grad_pre = jnp.concatenate(
        [
            grad_query_pre.astype(BF),
            grad_key_pre.astype(BF),
            grad_value.reshape(seq_rows, cols).astype(BF),
        ],
        axis=-1,
    )
    grad_qkv = contract_rows(normed, grad_pre).astype(BF)
    layer_rows = nc * rb

    def qkv_part(step):
        return lax.dynamic_slice_in_dim(grad_qkv, lay.layer_at(step) * layer_rows, layer_rows, 0)

    grad_qkv = a2a(lay.reduce_ring(qkv_part).reshape(nc, rb, 3 * cols), "ctx").astype(F32)
    grad_query_w, grad_key_w, grad_value_w = (
        lay.head_rows(grad_qkv[:, :, k * cols : (k + 1) * cols]) for k in range(3)
    )
    grad_normed = times_transposed(grad_pre, qkv_w).astype(BF).reshape(2, nc, half, width)
    grad_normed = jnp.concatenate([lay.reduce_ctx(grad_normed[k], k) for k in (0, 1)], axis=0)
    attn_inv = inverse_rms(inputs_f)
    grad_inputs_norm, grad_attn_gain = norm_backward(
        inputs_f, attn_inv, attn_gain_f, grad_normed.astype(F32)
    )
    grad_inputs = grad_middle + grad_inputs_norm

    packed = jnp.concatenate(
        [grad_router_w]
        + [
            g[:, None]
            for g in (
                grad_attn_gain,
                lay.all_heads(grad_query_gain),
                lay.all_heads(grad_key_gain),
                grad_mlp_gain,
            )
        ],
        axis=1,
    )
    packed = a2a(packed.reshape(devices, rb * (expert_count + 4)), ALL)
    packed = packed.sum(0).reshape(rb, expert_count + 4)
    gains = [packed[:, expert_count + k] for k in range(4)]
    return (
        result.astype(BF)[None],
        grad_inputs.astype(BF)[None],
        gains[0],
        grad_query_w,
        grad_key_w,
        grad_value_w,
        gains[1],
        gains[2],
        grad_out_w,
        gains[3],
        packed[:, :expert_count],
        grad_gate_w[None],
        grad_up_w[None],
        grad_down_w[None],
    )


def solution(mesh):
    both = ("dp", "ctx")
    in_specs = (
        P("dp", "ctx", None),
        P("dp", "ctx", None),
        P("dp", "ctx", None),
        P(both),
        P(both, None),
        P(both, None),
        P(both, None),
        P(both),
        P(both),
        P(both, None),
        P(both),
        P(both, None),
        P(both, None, None),
        P(both, None, None),
        P(both, None, None),
    )
    out_specs = (
        P("dp", "ctx", None),
        P("dp", "ctx", None),
        P(both),
        P(both, None),
        P(both, None),
        P(both, None),
        P(both),
        P(both),
        P(both, None),
        P(both),
        P(both, None),
        P(both, None, None),
        P(both, None, None),
        P(both, None, None),
    )
    return jax.shard_map(body, mesh=mesh, in_specs=in_specs, out_specs=out_specs, check_vma=False)
```

```python
import functools
import math

import jax
import jax.numpy as jnp
import numpy as np
from jax import lax
from jax.experimental import pallas as pl
from jax.experimental.pallas import tpu as pltpu
from jax.sharding import PartitionSpec as P

HEADS = 16
HEAD_DIM = 128
TOP = 8

EPSILON = 1e-05
NEG_LARGE = -1e30
NOTES = 128
BF = jnp.bfloat16
F32 = jnp.float32
ALL = ("dp", "ctx")


def dot(left, right):
    return jnp.dot(left, right, preferred_element_type=F32)


def contract_rows(left, right):
    return lax.dot_general(left, right, (((0,), (0,)), ((), ())), preferred_element_type=F32)


def times_transposed(left, right):
    return lax.dot_general(left, right, (((1,), (1,)), ((), ())), preferred_element_type=F32)


def inverse_rms(tensor):
    return lax.rsqrt(jnp.mean(tensor * tensor, axis=-1, keepdims=True) + EPSILON)


def norm_backward(tensor, inverse, gain_vec, grad_in):
    scaled = grad_in * gain_vec
    grad_gain = jnp.sum(grad_in * tensor * inverse, axis=0)
    grad_tensor = inverse * scaled - tensor * (inverse * inverse * inverse) * jnp.mean(
        scaled * tensor, axis=-1, keepdims=True
    )
    return (grad_tensor, grad_gain)


class Layout:
    def __init__(self, rb):
        self.nz = lax.axis_size("dp")
        self.nc = lax.axis_size("ctx")
        self.dz = lax.axis_index("dp")
        self.cx = lax.axis_index("ctx")
        nz, nc = self.nz, self.nc
        order = [0] + list(range(1, nz, 2)) + list(range(nz - 2 + nz % 2, 0, -2))
        self.ring = [(order[i], order[(i + 1) % nz]) for i in range(nz)]
        odd = self.dz % 2 == 1
        self.pos = jnp.where(odd, (self.dz + 1) // 2, jnp.where(self.dz == 0, 0, nz - self.dz // 2))
        self.bits = [1 << b for b in range(1, (nc - 1).bit_length())]
        self.flips = list(range(2, nc, 2))
        self.hpd = HEADS // nc
        self.cols = self.hpd * HEAD_DIM
        self.group = HEAD_DIM // rb
        self.rb = rb

    def swap(self, value, bit):
        return lax.ppermute(value, "ctx", [(i, i ^ bit) for i in range(self.nc)])

    def ring_step(self, value):
        return lax.ppermute(value, "dp", self.ring)

    def layer_at(self, step):
        place = (self.pos - step) % self.nz
        back = jnp.where(place == 0, 0, 2 * (self.nz - place))
        return jnp.where((place > 0) & (place <= self.nz // 2), 2 * place - 1, back)

    def gather_ring(self, block):
        blocks = [block]
        for _ in range(self.nz - 1):
            blocks.append(self.ring_step(blocks[-1]))
        return blocks

    def gather_near(self, value):
        return jnp.concatenate([value] + [self.swap(value, flip) for flip in self.flips], axis=0)

    def gather_ctx(self, value):
        near = self.gather_near(value)
        return (near, self.swap(near, 1))

    def reduce_ctx(self, near, far):
        total = (near.astype(F32) + self.swap(far, 1).astype(F32)).astype(BF)
        return self.reduce_chips(total)

    def reduce_chips(self, total):
        blocks = total.reshape((self.nc // 2, -1) + total.shape[1:])
        half = blocks.shape[1] // 2
        outs = []
        for color in (0, 1):
            part = blocks[:, color * half : (color + 1) * half]
            held = list(range(self.nc // 2))
            for bit in self.bits[::-1] if color == 0 else self.bits:
                keep = np.array([n for n, h in enumerate(held) if not 2 * h & bit])
                send = np.array([n for n, h in enumerate(held) if 2 * h & bit])
                other = self.swap(jnp.stack([part[n] for n in send]), bit)
                part = (jnp.stack([part[n] for n in keep]).astype(F32) + other.astype(F32)).astype(BF)
                held = [held[n] for n in keep]
            outs.append(part[0])
        return jnp.concatenate(outs, axis=0)

    def reduce_ring(self, parts):
        total = parts(1)
        for step in list(range(2, self.nz)) + [0]:
            total = (self.ring_step(total).astype(F32) + parts(step).astype(F32)).astype(BF)
        return total

    def arrival(self):
        flips = np.array([2 * n + core for core in (0, 1) for n in range(self.nc // 2)], np.int32)
        return jnp.asarray(flips) ^ self.cx

    def arrival_place(self):
        flips = jnp.arange(self.nc) ^ self.cx
        return (flips % 2) * (self.nc // 2) + flips // 2

    def head_blocks(self, value):
        rows = value.shape[0]
        split = value.reshape(rows, self.group, self.hpd, self.nc // self.group, HEAD_DIM)
        return split.transpose(3, 1, 0, 2, 4).reshape(self.nc, rows, self.cols)

    def head_rows(self, value):
        rows = value.shape[1]
        split = value.reshape(self.nc // self.group, self.group, rows, self.hpd, HEAD_DIM)
        return split.transpose(2, 1, 3, 0, 4).reshape(rows, self.nc * self.cols)

    def head_at(self, device, n):
        return ((device % self.group) * self.hpd + n) * (self.nc // self.group) + device // self.group

    def weight_rows(self, grads, weights):
        count, rows = len(weights), weights[0].shape[0]
        width = weights[0].shape[1]

        def kernel(grads, *refs):
            sums = 0.0
            for device in range(self.nc):
                for w in range(count):
                    for n in range(self.hpd):
                        head = slice(self.head_at(device, n) * HEAD_DIM, (self.head_at(device, n) + 1) * HEAD_DIM)
                        start = w * self.cols + n * HEAD_DIM
                        part = grads[device, :, start : start + HEAD_DIM].astype(F32)
                        refs[count + w][:, head] = part
                        sums += part * refs[w][:, head].astype(F32)
            refs[-1][...] = as_row(jnp.sum(sums, axis=-1, keepdims=True))

        shape = jax.ShapeDtypeStruct((rows, width), F32)
        return pl.pallas_call(
            kernel,
            out_shape=[shape] * count + [jax.ShapeDtypeStruct((1, rows), F32)],
            compiler_params=pltpu.CompilerParams(vmem_limit_bytes=24 * 2**20),
        )(grads, *weights)

    def own_heads(self, vector):
        return self.head_blocks(vector[None])[self.cx, 0]

    def all_heads(self, vector):
        whole = jnp.zeros((self.nc, 1, self.cols), vector.dtype)
        whole = lax.dynamic_update_slice(whole, vector[None, None], (self.cx, 0, 0))
        return self.head_rows(whole)[0]


def sync(*values):
    return lax.optimization_barrier(values)


def after(value, *deps):
    return lax.optimization_barrier((value,) + deps)[0]


def a2a(value, axes):
    return lax.all_to_all(value, axes, split_axis=0, concat_axis=0, tiled=True)


def column(row):
    return jnp.broadcast_to(row, (row.shape[1], row.shape[1])).T[:, :1]


def as_row(col):
    return jnp.broadcast_to(col, (col.shape[0], col.shape[0])).T[:1]


def lane_pick(notes, *lanes):
    lane = lax.broadcasted_iota(jnp.int32, notes.shape, 1)
    keep = functools.reduce(jnp.logical_or, [lane == n for n in lanes])
    return jnp.sum(jnp.where(keep, notes.astype(F32), 0.0), axis=-1, keepdims=True)


def pick_kernel(capacity, count, expert_ref, block, *outs):
    rows = block.shape[0]
    width = outs[0].shape[1]
    start = block.shape[1] - NOTES
    before = lax.broadcasted_iota(jnp.int32, (rows, rows), 0) < lax.broadcasted_iota(jnp.int32, (rows, rows), 1)
    before = jnp.where(before, 1.0, 0.0).astype(BF)
    for n in range(count):
        named = lane_pick(block[:, start:], expert_ref[n])
        named = jnp.broadcast_to(named, (rows, rows)).T[:capacity]
        slot = dot(named.astype(BF), before)
        mine = lax.broadcasted_iota(jnp.int32, slot.shape, 0).astype(F32)
        choose = jnp.where((slot == mine) & (named > 0.5), 1.0, 0.0).astype(BF)
        picked = dot(choose, block[:, :width]).astype(BF)
        if len(outs) == 1:
            outs[0][n * capacity : (n + 1) * capacity] = picked
        else:
            outs[n][...] = picked


def pick_rows(block, experts, capacity, width, joined):
    rows, wide = block.shape
    count = experts.shape[0]
    shapes = [(count * capacity, width)] if joined else [(capacity, width)] * count
    return pl.pallas_call(
        functools.partial(pick_kernel, capacity, count),
        grid_spec=pltpu.PrefetchScalarGridSpec(
            num_scalar_prefetch=1,
            grid=(1,),
            in_specs=[pl.BlockSpec((rows, wide), lambda n, experts: (0, 0))],
            out_specs=[pl.BlockSpec(shape, lambda n, experts: (0, 0)) for shape in shapes],
        ),
        out_shape=[jax.ShapeDtypeStruct(shape, BF) for shape in shapes],
        compiler_params=pltpu.CompilerParams(vmem_limit_bytes=24 * 2**20),
        cost_estimate=pl.CostEstimate(
            flops=2 * count * rows * capacity * width, bytes_accessed=4 * count * rows * width, transcendentals=0
        ),
    )(experts, block)


def spread_kernel(capacity, has_sum, expert_ref, notes, *refs):
    out = refs[-1]
    parts = refs[: -2 if has_sum else -1]
    rows = notes.shape[0]
    after_it = lax.broadcasted_iota(jnp.int32, (rows, rows), 1) < lax.broadcasted_iota(jnp.int32, (rows, rows), 0)
    after_it = jnp.where(after_it, 1.0, 0.0).astype(BF)
    total = refs[-2][...].astype(F32) if has_sum else 0.0
    n = 0
    for part in parts:
        for place in range(0, part.shape[0], capacity):
            named = jnp.broadcast_to(lane_pick(notes[...], expert_ref[n]), (rows, capacity))
            slot = dot(after_it, named.astype(BF))
            mine = lax.broadcasted_iota(jnp.int32, slot.shape, 1).astype(F32)
            choose = jnp.where((slot == mine) & (named > 0.5), 1.0, 0.0).astype(BF)
            total += dot(choose, part[place : place + capacity])
            n += 1
    out[...] = total.astype(BF)


def spread_rows(block, experts, parts, total, capacity):
    rows = block.shape[0]
    width = parts[0].shape[1]
    place = block.shape[1] // NOTES - 1
    row = pl.BlockSpec((rows, width), lambda n, experts: (0, 0))
    return pl.pallas_call(
        functools.partial(spread_kernel, capacity, total is not None),
        grid_spec=pltpu.PrefetchScalarGridSpec(
            num_scalar_prefetch=1,
            grid=(1,),
            in_specs=[pl.BlockSpec((rows, NOTES), lambda n, experts: (0, place))]
            + [pl.BlockSpec(p.shape, lambda n, experts: (0, 0)) for p in parts]
            + ([row] if total is not None else []),
            out_specs=row,
        ),
        out_shape=jax.ShapeDtypeStruct((rows, width), BF),
        compiler_params=pltpu.CompilerParams(vmem_limit_bytes=24 * 2**20),
        cost_estimate=pl.CostEstimate(
            flops=8 * rows * rows * width, bytes_accessed=16 * rows * width, transcendentals=0
        ),
    )(experts, block, *parts, *([total] if total is not None else []))


def expert_kernel(
    kinds, expert_ref, near, far, dy_near, dy_far, gate_w, up_w, down_w,
    out_near, out_far, grad_near, grad_far, hidden_near, hidden_far, gate_near, gate_far, up_near, up_far,
):
    tile = near.shape[0]
    width = dy_near.shape[1]
    expert = expert_ref[0]
    rows = jnp.concatenate([near[:, :width], far[:, :width]], axis=0)
    notes = jnp.concatenate([near[:, width:], far[:, width:]], axis=0)
    dy = jnp.concatenate([dy_near[...], dy_far[...]], axis=0)
    gate_col = lane_pick(notes, expert + kinds, expert + 2 * kinds)
    gate_pre = dot(rows, gate_w[...])
    up_pre = dot(rows, up_w[...])
    sigmoid_val = jax.nn.sigmoid(gate_pre)
    silu = gate_pre * sigmoid_val
    hidden_f = silu * up_pre
    out = (dot(hidden_f.astype(BF), down_w[...]) * gate_col).astype(BF)
    out_near[...] = out[:tile]
    out_far[...] = out[tile:]
    grad_hidden = times_transposed(dy, down_w[...])
    weighted = jnp.sum(grad_hidden * hidden_f, axis=-1, keepdims=True) * gate_col
    lane = lax.broadcasted_iota(jnp.int32, (2 * tile, NOTES), 1)
    weighted = jnp.where(lane == expert, weighted, 0.0).astype(BF)
    grad_near[:, width:] = weighted[:tile]
    grad_far[:, width:] = weighted[tile:]
    grad_hidden = grad_hidden * gate_col
    grad_gate_pre = (
        grad_hidden * up_pre * (sigmoid_val * (1.0 + gate_pre * (1.0 - sigmoid_val)))
    ).astype(BF)
    grad_up_pre = (grad_hidden * silu).astype(BF)
    hidden = (hidden_f * gate_col).astype(BF)
    hidden_near[...] = hidden[:tile]
    hidden_far[...] = hidden[tile:]
    gate_near[...] = grad_gate_pre[:tile]
    gate_far[...] = grad_gate_pre[tile:]
    up_near[...] = grad_up_pre[:tile]
    up_far[...] = grad_up_pre[tile:]
    grad = (
        times_transposed(grad_gate_pre, gate_w[...]) + times_transposed(grad_up_pre, up_w[...])
    ).astype(BF)
    grad_near[:, :width] = grad[:tile]
    grad_far[:, :width] = grad[tile:]


def expert_chunk(kinds, expert, near, far, dy_near, dy_far, gate_w, up_w, down_w, tile=128):
    rows, width = dy_near.shape
    units = gate_w.shape[1]

    def row(cols):
        return pl.BlockSpec((tile, cols), lambda i, expert: (i, 0))

    def whole(array):
        return pl.BlockSpec(array.shape, lambda i, expert: (0, 0), pipeline_mode=pl.Buffered(1))

    def shape(cols):
        return jax.ShapeDtypeStruct((rows, cols), BF)

    wide = near.shape[1]
    outs = [width, width, wide, wide] + [units] * 6
    return pl.pallas_call(
        functools.partial(expert_kernel, kinds),
        grid_spec=pltpu.PrefetchScalarGridSpec(
            num_scalar_prefetch=1,
            grid=(rows // tile,),
            in_specs=[row(wide), row(wide), row(width), row(width), whole(gate_w), whole(up_w), whole(down_w)],
            out_specs=[row(cols) for cols in outs],
        ),
        out_shape=[shape(cols) for cols in outs],
        compiler_params=pltpu.CompilerParams(vmem_limit_bytes=56 * 2**20),
        cost_estimate=pl.CostEstimate(
            flops=24 * rows * width * units,
            bytes_accessed=16 * rows * width,
            transcendentals=2 * rows * units,
        ),
    )(expert, near, far, dy_near, dy_far, gate_w, up_w, down_w)


def contract_kernel(count, *refs):
    total = 0.0
    for left, right in zip(refs[:count], refs[count:-1]):
        total += contract_rows(left[...], right[...])
    refs[-1][...] = total


def contract_many(lefts, rights, rows, cols, tile=256):
    count = len(lefts)
    depth = lefts[0].shape[0]
    tall = rows >= cols
    strip = pl.BlockSpec((depth, tile), lambda i: (0, i))
    held = pl.BlockSpec((depth, min(rows, cols)), lambda i: (0, 0), pipeline_mode=pl.Buffered(1))
    return pl.pallas_call(
        functools.partial(contract_kernel, count),
        grid=(max(rows, cols) // tile,),
        in_specs=[strip if tall else held] * count + [held if tall else strip] * count,
        out_specs=pl.BlockSpec((tile, cols), lambda i: (i, 0)) if tall else pl.BlockSpec((rows, tile), lambda i: (0, i)),
        out_shape=jax.ShapeDtypeStruct((rows, cols), F32),
        compiler_params=pltpu.CompilerParams(vmem_limit_bytes=56 * 2**20),
        cost_estimate=pl.CostEstimate(
            flops=2 * depth * count * rows * cols,
            bytes_accessed=2 * depth * count * (rows + cols) + 4 * rows * cols,
            transcendentals=0,
        ),
    )(*lefts, *rights)


def columns(rows):
    count = rows.shape[1] // 128
    return jnp.concatenate([column(rows[:, n * 128 : (n + 1) * 128]) for n in range(count)], axis=0)


def as_rows(cols):
    count = cols.shape[0] // 128
    return jnp.concatenate([as_row(cols[n * 128 : (n + 1) * 128]) for n in range(count)], axis=1)


def norm_kernel(place_ref, near, far, gain, out):
    n = pl.program_id(0)
    steps = pl.num_programs(0)
    rows = jnp.where(place_ref[n] < steps // 2, near[...], far[...]).astype(F32)
    out[...] = (rows * inverse_rms(rows) * gain[...]).astype(BF)


def norm_in_order(place, near, far, gain, half):
    steps = place.shape[0]
    width = near.shape[1]
    return pl.pallas_call(
        norm_kernel,
        grid_spec=pltpu.PrefetchScalarGridSpec(
            num_scalar_prefetch=1,
            grid=(steps,),
            in_specs=[
                pl.BlockSpec((half, width), lambda n, place: (jnp.minimum(place[n], steps // 2 - 1), 0)),
                pl.BlockSpec((half, width), lambda n, place: (jnp.maximum(place[n] - steps // 2, 0), 0)),
                pl.BlockSpec((1, width), lambda n, place: (0, 0)),
            ],
            out_specs=pl.BlockSpec((half, width), lambda n, place: (n, 0)),
        ),
        out_shape=jax.ShapeDtypeStruct((steps * half, width), BF),
        compiler_params=pltpu.CompilerParams(vmem_limit_bytes=16 * 2**20),
        cost_estimate=pl.CostEstimate(
            flops=4 * steps * half * width, bytes_accessed=6 * steps * half * width, transcendentals=0
        ),
    )(place, near, far, gain)


def project_kernel(count, cols, layer_ref, rows, *refs):
    total = 0.0
    for n in range(count):
        depth = refs[n].shape[0]
        start = pl.multiple_of(layer_ref[n] * depth, depth)
        total += dot(rows[:, pl.ds(start, depth)], refs[n][...])
    out, squares = refs[count:]
    out[...] = total
    for n in range(2):
        part = total[:, n * cols : (n + 1) * cols]
        squares[n : n + 1] = as_rows(jnp.sum(part * part, axis=-1, keepdims=True))


def project(layers, rows, weights, cols, tile=256):
    count = len(weights)
    total, width = rows.shape
    wide = weights[0].shape[1]
    held = pl.BlockSpec(weights[0].shape, lambda n, layers: (0, 0), pipeline_mode=pl.Buffered(1))
    return pl.pallas_call(
        functools.partial(project_kernel, count, cols),
        grid_spec=pltpu.PrefetchScalarGridSpec(
            num_scalar_prefetch=1,
            grid=(total // tile,),
            in_specs=[pl.BlockSpec((tile, width), lambda n, layers: (n, 0))] + [held] * count,
            out_specs=[
                pl.BlockSpec((tile, wide), lambda n, layers: (n, 0)),
                pl.BlockSpec((2, tile), lambda n, layers: (0, n)),
            ],
        ),
        out_shape=[jax.ShapeDtypeStruct((total, wide), F32), jax.ShapeDtypeStruct((2, total), F32)],
        compiler_params=pltpu.CompilerParams(vmem_limit_bytes=40 * 2**20),
        cost_estimate=pl.CostEstimate(
            flops=2 * total * width * wide, bytes_accessed=2 * total * width + 6 * total * wide, transcendentals=0
        ),
    )(layers, rows, *weights)


def project_back_kernel(count, half, layer_ref, block_ref, grads, *refs):
    near, far = refs[count:]
    step = pl.program_id(0)
    blocks = near.shape[0] // half
    for side, out in enumerate((near, far)):
        first = (side * pl.num_programs(0) + step) * blocks
        rows = jnp.concatenate(
            [grads[pl.ds(pl.multiple_of(block_ref[first + n] * half, half), half)] for n in range(blocks)], axis=0
        )
        for n in range(count):
            depth = refs[n].shape[0]
            start = pl.multiple_of(layer_ref[n] * depth, depth)
            out[:, pl.ds(start, depth)] = times_transposed(rows, refs[n][...]).astype(BF)


def project_back(layers, blocks, grads, weights, half, tile=256):
    count = len(weights)
    total, wide = grads.shape
    width = count * weights[0].shape[0]
    held = pl.BlockSpec(weights[0].shape, lambda n, *refs: (0, 0), pipeline_mode=pl.Buffered(1))
    out = jax.ShapeDtypeStruct((total // 2, width), BF)
    return pl.pallas_call(
        functools.partial(project_back_kernel, count, half),
        grid_spec=pltpu.PrefetchScalarGridSpec(
            num_scalar_prefetch=2,
            grid=(total // 2 // tile,),
            in_specs=[pl.BlockSpec((total, wide), lambda n, *refs: (0, 0), pipeline_mode=pl.Buffered(1))]
            + [held] * count,
            out_specs=[pl.BlockSpec((tile, width), lambda n, *refs: (n, 0))] * 2,
        ),
        out_shape=[out, out],
        compiler_params=pltpu.CompilerParams(vmem_limit_bytes=40 * 2**20),
        cost_estimate=pl.CostEstimate(
            flops=2 * total * width * wide, bytes_accessed=2 * total * (width + wide), transcendentals=0
        ),
    )(layers, blocks, grads, *weights)


def turn(value, cosine, sine):
    return value * cosine + pltpu.roll(value, HEAD_DIM // 2, 1) * sine


def half_blocks(rows, half):
    count = rows // half
    return [(2 * n if n < count // 2 else 2 * (count - 1 - n) + 1) * half for n in range(count)]


def masked_scores(queries, keys, first, score_scale):
    scores = times_transposed(queries, keys) * score_scale
    row = lax.broadcasted_iota(jnp.int32, scores.shape, 0) + first
    col = lax.broadcasted_iota(jnp.int32, scores.shape, 1)
    return scores, col <= row


def attention_kernel(
    half, tile, score_scale, q_pre, k_pre, v_pre, inv, gains, cosine, sine,
    sent, attended, lse, query_rot, key_rot, value,
):
    rows = q_pre.shape[0]
    cos, sin = cosine[...], sine[...]
    query_rot[...] = turn(q_pre[...] * columns(inv[0:1]) * gains[0:1], cos, sin).astype(BF)
    key_rot[...] = turn(k_pre[...] * columns(inv[1:2]) * gains[1:2], cos, sin).astype(BF)
    value[...] = v_pre[...].astype(BF)
    for n in range(rows // tile):
        first = n * tile
        end = first + tile
        scores, allowed = masked_scores(query_rot[first:end], key_rot[:end], first, score_scale)
        scores = jnp.where(allowed, scores, NEG_LARGE)
        top = jnp.max(scores, axis=-1, keepdims=True)
        probs = jnp.exp(scores - top)
        total = jnp.sum(probs, axis=-1, keepdims=True)
        lse[first:end] = jnp.broadcast_to(top + jnp.log(total), (tile, HEAD_DIM))
        attended[first:end] = dot((probs / total).astype(BF), value[:end])
    for n, place in enumerate(half_blocks(rows, half)):
        sent[place : place + half] = attended[n * half : (n + 1) * half].astype(BF)


def attention_grad_kernel(
    half, tile, score_scale, sent_grad, attended, lse, query_rot, key_rot, value, q_pre, k_pre, inv, gains,
    cosine, sine, scaled_q, scaled_k, grad_value, dots, grad_gains, grad_heads, key_sum, value_sum, query_sum,
):
    rows = q_pre.shape[0]
    for n, place in enumerate(half_blocks(rows, half)):
        grad_heads[n * half : (n + 1) * half] = sent_grad[place : place + half]
    key_sum[...] = jnp.zeros_like(key_sum)
    value_sum[...] = jnp.zeros_like(value_sum)
    for n in range(rows // tile):
        first = n * tile
        end = first + tile
        grads = grad_heads[first:end]
        queries = query_rot[first:end]
        delta = jnp.sum(grads.astype(F32) * attended[first:end], axis=-1, keepdims=True)
        scores, allowed = masked_scores(queries, key_rot[:end], first, score_scale)
        probs = jnp.where(allowed, jnp.exp(scores - lse[first:end][:, :1]), 0.0)
        grad_scores = (probs * (times_transposed(grads, value[:end]) - delta)).astype(BF)
        query_sum[first:end] = dot(grad_scores, key_rot[:end])
        key_sum[:end] += contract_rows(grad_scores, queries)
        value_sum[:end] += contract_rows(probs.astype(BF), grads)
    grad_value[...] = value_sum[...].astype(BF)
    cos, sin = cosine[...], -sine[...]
    for n, (total, pre, scaled) in enumerate(((query_sum, q_pre, scaled_q), (key_sum, k_pre, scaled_k))):
        grad = turn(total[...] * score_scale, cos, sin)
        grad_gains[n : n + 1] = jnp.sum(grad * pre[...] * columns(inv[n : n + 1]), axis=0, keepdims=True)
        grad = grad * gains[n : n + 1]
        scaled[...] = grad
        dots[n : n + 1] = as_rows(jnp.sum(grad * pre[...], axis=-1, keepdims=True))


class Attention:
    def __init__(self, rows, half, hpd):
        self.rows, self.half, self.hpd = rows, half, hpd
        self.tile = min(256, rows)
        position = np.arange(rows, dtype=np.float32)
        freq = np.exp(np.arange(HEAD_DIM // 2, dtype=np.float32) * np.float32(-2.0 * math.log(10000.0) / HEAD_DIM))
        angles = position[:, None] * freq[None, :].astype(np.float32)
        self.cosine = jnp.asarray(np.concatenate([np.cos(angles)] * 2, axis=1), F32)
        self.sine = jnp.asarray(np.concatenate([-np.sin(angles), np.sin(angles)], axis=1), F32)
        self.head = pl.BlockSpec((rows, HEAD_DIM), lambda h: (0, h))
        self.keys = pl.BlockSpec((rows, HEAD_DIM), lambda h: (0, h + hpd))
        self.values = pl.BlockSpec((rows, HEAD_DIM), lambda h: (0, h + 2 * hpd))
        self.stat = pl.BlockSpec((2, rows), lambda h: (0, 0))
        self.gain = pl.BlockSpec((2, HEAD_DIM), lambda h: (0, h))
        self.table = pl.BlockSpec((rows, HEAD_DIM), lambda h: (0, 0))
        self.args = (half, self.tile, 1.0 / math.sqrt(HEAD_DIM))
        self.params = pltpu.CompilerParams(vmem_limit_bytes=48 * 2**20)

    def shape(self, dtype):
        return jax.ShapeDtypeStruct((self.rows, self.hpd * HEAD_DIM), dtype)

    def cost(self, products):
        area = self.hpd * self.rows * self.rows
        return pl.CostEstimate(
            flops=products * area * HEAD_DIM, bytes_accessed=self.hpd * self.rows * HEAD_DIM * 24, transcendentals=area
        )

    def forward(self, qkv, inv, gains):
        return pl.pallas_call(
            functools.partial(attention_kernel, *self.args),
            grid=(self.hpd,),
            in_specs=[self.head, self.keys, self.values, self.stat, self.gain, self.table, self.table],
            out_specs=[self.head] * 6,
            out_shape=[self.shape(t) for t in (BF, F32, F32, BF, BF, BF)],
            compiler_params=self.params,
            cost_estimate=self.cost(3),
        )(qkv, qkv, qkv, inv, gains, self.cosine, self.sine)

    def backward(self, sent_grad, kept, qkv, inv, gains):
        rows, hpd = self.rows, self.hpd
        line = pl.BlockSpec((None, 2, rows), lambda h: (h, 0, 0))
        return pl.pallas_call(
            functools.partial(attention_grad_kernel, *self.args),
            grid=(hpd,),
            in_specs=[self.head] * 6 + [self.head, self.keys, self.stat, self.gain, self.table, self.table],
            out_specs=[self.head] * 3 + [line, self.gain],
            out_shape=[self.shape(F32), self.shape(F32), self.shape(BF)]
            + [jax.ShapeDtypeStruct((hpd, 2, rows), F32), jax.ShapeDtypeStruct((2, hpd * HEAD_DIM), F32)],
            scratch_shapes=[pltpu.VMEM((rows, HEAD_DIM), BF)] + [pltpu.VMEM((rows, HEAD_DIM), F32)] * 3,
            compiler_params=self.params,
            cost_estimate=self.cost(6),
        )(sent_grad, *kept, qkv, qkv, inv, gains, self.cosine, self.sine)


class Gathered:
    def __init__(self, lay, routes, expert_count, capacity, width):
        self.lay, self.kinds, self.capacity, self.width = lay, expert_count, capacity, width
        self.tok_rows = routes.shape[0]
        chosen = routes[:, :, None] == jnp.arange(expert_count, dtype=jnp.int32)
        self.chosen = jnp.any(chosen, axis=1)
        first = lay.dz * (lay.nc // 2)
        flipped = first + (lay.cx ^ jnp.array([0] + lay.flips, jnp.int32)) // 2
        self.flipped = flipped.astype(jnp.int32)
        self.own = self.flipped[:1]
        self.straight = (first + jnp.arange(lay.nc // 2)).astype(jnp.int32)

    def experts(self, step):
        return self.straight if step else self.flipped

    def noted(self, rows, *notes):
        notes = [self.chosen.astype(BF)] + list(notes)
        rest = NOTES - self.kinds * len(notes)
        return jnp.concatenate([rows] + notes + [jnp.zeros((self.tok_rows, rest), BF)], axis=1)

    def offer(self, step, block, width=None):
        return pick_rows(block, self.experts(step), self.capacity, width or block.shape[1], step > 0)

    def exchange(self, parts):
        if len(parts) > 1:
            return [parts[0]] + [self.lay.swap(p, flip) for p, flip in zip(parts[1:], self.lay.flips)]
        groups = [list(range(core, self.lay.nc, 2)) for core in (0, 1)]
        return [
            lax.all_to_all(parts[0], "ctx", split_axis=0, concat_axis=0, tiled=True, axis_index_groups=groups)
        ]

    def joined(self, parts):
        return jnp.concatenate(parts, axis=0) if len(parts) > 1 else parts[0]

    def give_back(self, step, near, far):
        sums = (near.astype(F32) + far.astype(F32)).astype(BF)
        if step:
            return self.exchange([sums])
        count = len(self.lay.flips) + 1
        return self.exchange([sums[n * self.capacity : (n + 1) * self.capacity] for n in range(count)])

    def spread(self, step, parts, total):
        return spread_rows(self.blocks[step], self.experts(step), parts, total, self.capacity)

    def run(self, block, dy, gate_w, up_w, down_w):
        lay, nz = self.lay, self.lay.nz
        self.blocks = blocks = [block]
        self.rows, self.done, self.dy = rows, done, dy = [], [], dy
        back, far_grads = {}, {}
        parts = self.exchange(self.offer(0, block))
        coming = lay.ring_step(block)
        coming, *parts = sync(coming, *parts)
        for step in range(nz):
            near = self.joined(parts)
            far = lay.swap(near, 1)
            if step:
                far_grads[step - 1] = lay.swap(done[-1][3], 1)
            if step + 1 < nz:
                blocks.append(coming)
                parts = self.exchange(self.offer(step + 1, coming))
                if step + 2 < nz:
                    coming = lay.ring_step(coming)
            for pair in dy[step + 1 : step + 2]:
                if len(pair) == 1:
                    pair.append(lay.swap(pair[0], 1))
            if step > 1:
                far, far_grads[step - 2] = sync(far, far_grads[step - 2])
                back[step - 2] = self.give_back(step - 2, done[step - 2][2], far_grads[step - 2])
            rows += [near, far]
            made = list(expert_chunk(self.kinds, self.own, near, far, *dy[step], gate_w, up_w, down_w))
            held = [made[3], coming] + (list(parts) if step + 1 < nz else [])
            if step:
                held.append(far_grads[step - 1])
            held = list(sync(*held))
            made[3], coming = held[:2]
            if step + 1 < nz:
                parts = held[2 : 2 + len(parts)]
            if step:
                far_grads[step - 1] = held[-1]
            done.append(made)
        last = nz - 1
        far_grads[last] = lay.swap(done[last][3], 1)
        back[last - 1] = self.give_back(last - 1, done[last - 1][2], far_grads[last - 1])
        far_outs = [lay.swap(after(d[1], done[last][3]), 1) for d in done]
        self.outs = [(d[0], other) for d, other in zip(done, far_outs)]
        total = None
        for step in list(range(1, nz)) + [0]:
            if total is not None:
                total = lay.ring_step(total)
            if step == last - 1:
                total, far_grads[last], *back[step] = sync(total, far_grads[last], *back[step])
                back[last] = self.give_back(last, done[last][2], far_grads[last])
            elif step == last:
                total, *back[step] = sync(total, *back[step])
            total = self.spread(step, back[step], total)
        total = total.astype(F32)
        self.tail = back[last][-1]
        return total[:, : self.width], total[:, self.width : self.width + self.kinds]

    def mixture_parts(self, step, dep):
        near, far = self.outs[step]
        return self.give_back(step, near, after(far, dep))

    def weight_grads(self, which, dep):
        near = 4 + 2 * which
        mids = [after(d[k], dep) for d in self.done for k in (near, near + 1)]
        units = mids[0].shape[1]
        if which == 0:
            return contract_many(mids, [d for pair in self.dy for d in pair], units, self.width)
        return contract_many(self.rows, mids, self.width, units)


def experts_sent(lay, mlp_normed, routes, router_probs, grad_result, gate_w, up_w, down_w):
    tok_rows, width = mlp_normed.shape
    expert_count = router_probs.shape[1]
    capacity = 3 * tok_rows * TOP // (2 * expert_count)
    flat_routes = routes.reshape(tok_rows * TOP)
    onehot = (flat_routes[:, None] == jnp.arange(expert_count, dtype=jnp.int32)[None, :]).astype(
        jnp.int32
    )
    slot_index = jnp.sum((jnp.cumsum(onehot, axis=0) - onehot) * onehot, axis=1)
    chosen = onehot.reshape(tok_rows, TOP, expert_count).astype(F32)
    gate_values = jnp.einsum("tke,te->tk", chosen, router_probs)

    def dispatch(rows_in):
        sent = jnp.zeros((expert_count, capacity, width), BF).at[flat_routes, slot_index].set(rows_in)
        return a2a(jnp.repeat(sent, 2, axis=0), ALL)

    def collect(buffer):
        even_rows = buffer[2 * flat_routes, slot_index].astype(F32)
        odd_rows = buffer[2 * flat_routes + 1, slot_index].astype(F32)
        return (even_rows + odd_rows).reshape(tok_rows, TOP, width)

    received = dispatch(jnp.repeat(mlp_normed, TOP, axis=0))
    flat_in = received.reshape(-1, width)
    gate_pre = dot(flat_in, gate_w)
    up_pre = dot(flat_in, up_w)
    hidden = (jax.nn.silu(gate_pre) * up_pre).astype(BF)
    half_out = dot(hidden, down_w).astype(BF).reshape(received.shape)
    expert_rows = collect(a2a(half_out, ALL))
    mixture = jnp.einsum("tk,tkd->td", gate_values, expert_rows)
    grad_gates = jnp.einsum("td,tkd->tk", grad_result, expert_rows)
    grad_rows = (
        (gate_values[:, :, None] * grad_result[:, None, :])
        .astype(BF)
        .reshape(tok_rows * TOP, width)
    )
    grad_flat = dispatch(grad_rows).reshape(-1, width)
    grad_down_w = contract_rows(hidden, grad_flat)
    grad_hidden = times_transposed(grad_flat, down_w)
    sigmoid_val = jax.nn.sigmoid(gate_pre)
    grad_gate_pre = (
        grad_hidden * up_pre * sigmoid_val * (1.0 + gate_pre * (1.0 - sigmoid_val))
    ).astype(BF)
    grad_up_pre = (grad_hidden * jax.nn.silu(gate_pre)).astype(BF)
    grad_gate_w = contract_rows(flat_in, grad_gate_pre)
    grad_up_w = contract_rows(flat_in, grad_up_pre)
    grad_copy = (
        (times_transposed(grad_gate_pre, gate_w) + times_transposed(grad_up_pre, up_w))
        .astype(BF)
        .reshape(received.shape)
    )
    grad_sum = jnp.sum(collect(a2a(grad_copy, ALL)), axis=1)
    weighted = router_probs * jnp.einsum("tk,tke->te", grad_gates, chosen)
    return (mixture, grad_sum, weighted, lambda which, dep: (grad_down_w, grad_gate_w, grad_up_w)[which])


def body(
    tokens,
    routes,
    cotangent,
    attn_gain,
    query_weight,
    key_weight,
    value_weight,
    query_gain,
    key_gain,
    out_weight,
    mlp_gain,
    router_weight,
    gate_weight,
    up_weight,
    down_weight,
):
    rb = query_weight.shape[0]
    lay = Layout(rb)
    nz, nc, cx = lay.nz, lay.nc, lay.cx
    tok_rows = tokens.shape[1]
    width = tokens.shape[2]
    half = tok_rows // 2
    seq_rows = tok_rows * nc
    expert_count = router_weight.shape[1]
    hpd, cols = lay.hpd, lay.cols
    devices = nz * nc
    capacity = 3 * tok_rows * TOP // (2 * expert_count)
    gathered = (
        devices * tok_rows <= 4 * expert_count * capacity and 3 * expert_count <= NOTES and capacity % 16 == 0
    )

    sent = jnp.concatenate(
        [lay.head_blocks(w) for w in (query_weight, key_weight, value_weight)], axis=-1
    )
    kinds = expert_count + 4
    small = jnp.concatenate(
        [router_weight] + [g[:, None] for g in (attn_gain, query_gain, key_gain, mlp_gain)], axis=1
    )
    small = jnp.broadcast_to(small.T.reshape(1, kinds * rb), (devices, kinds * rb))
    block = a2a(sent, "ctx").reshape(nc * rb, 3 * cols)
    parts = [tokens[0]] + [lay.swap(tokens[0], flip) for flip in lay.flips]
    if gathered:
        moe = Gathered(lay, routes[0], expert_count, capacity, width)
        dy_blocks = [moe.noted(cotangent[0])]
        dy_blocks.append(lay.ring_step(dy_blocks[0]))
        block, dy_blocks[1] = sync(block, dy_blocks[1])
    ring = [block]
    for step in range(1, nz):
        block = lay.ring_step(block)
        beside = []
        if step == 1:
            small = a2a(small, ALL)
            beside = [small] + parts[1:]
        elif step == 2:
            seq_near = jnp.concatenate(parts, axis=0)
            seq_far = lay.swap(seq_near, 1)
            beside = [seq_far]
            if gathered:
                dy0 = moe.exchange(moe.offer(0, after(dy_blocks[0], ring[-1]), width))
                beside += dy0[1:]
        elif step == 3:
            small = small.reshape(devices, kinds, rb).transpose(1, 0, 2).reshape(kinds, width)
            router_t = small[:expert_count]
            attn_gain_f, qgain_f, kgain_f, mlp_gain_f = (
                small[expert_count + k].astype(F32) for k in range(4)
            )
            places = lay.arrival_place()
            places = jnp.concatenate([places * 2, (places * 2 + 1)[::-1]]).astype(jnp.int32)
            normed = norm_in_order(places, seq_near, seq_far, attn_gain_f[None], half)
            beside = [normed]
            if gathered:
                dy = [[moe.joined(dy0)]]
                dy[0].append(lay.swap(dy[0][0], 1))
                dy1 = moe.exchange(moe.offer(1, after(dy_blocks[1], ring[-1]), width))
                beside += [dy[0][1]] + dy1
        block, *beside = sync(block, *beside)
        if step == 1:
            small, parts[1:] = beside[0], beside[1:]
        elif step == 2:
            seq_far = beside[0]
            if gathered:
                dy0[1:] = beside[1:]
        elif step == 3:
            normed = beside[0]
            if gathered:
                dy[0][1], dy1 = beside[1], beside[2:]
        ring.append(block)
    out_w = lax.all_gather(after(out_weight, ring[2]), ALL, axis=0, tiled=True)
    if gathered:
        dy_blocks.append(lay.ring_step(after(dy_blocks[1], ring[-1])))
    layers = jnp.stack([lay.layer_at(step) for step in range(nz)]).astype(jnp.int32)
    qkv, squares = project(layers, normed, ring, cols)
    query_pre, key_pre = qkv[:, :cols], qkv[:, cols : 2 * cols]

    def sum_heads(stats):
        stats = lax.all_gather(stats.reshape(2 * seq_rows // 128, 128), "ctx", axis=0).sum(0)
        return stats.reshape(2, seq_rows) / width

    inv = lax.rsqrt(sum_heads(squares) + EPSILON)
    own_gains = jnp.stack([lay.own_heads(qgain_f), lay.own_heads(kgain_f)])
    attention = Attention(seq_rows, half, hpd)
    if gathered:
        inv, dy_blocks[2] = sync(inv, dy_blocks[2])
        dy_blocks.append(lay.ring_step(dy_blocks[2]))
        dy.append([moe.joined(dy1)])
        dy.append(moe.exchange(moe.offer(2, dy_blocks[2], width)))
    attended_b, *kept = attention.forward(qkv, inv, own_gains)
    if gathered:
        attended_b, dy_blocks[3], *dy[2] = sync(attended_b, dy_blocks[3], *dy[2])
        for pair in dy[1:3]:
            pair.append(lay.swap(pair[0], 1))
        offered = moe.offer(3, dy_blocks[3], width)
    attended_own = a2a(attended_b.reshape(nc, tok_rows, cols), "ctx")
    if gathered:
        attended_own, dy[1][1], dy[2][1], *offered = sync(attended_own, dy[1][1], dy[2][1], *offered)
        dy.append(moe.exchange(offered))
    attended_own = lay.head_rows(attended_own)
    inputs_f = tokens[0].astype(F32)
    middle = inputs_f + dot(attended_own, out_w)
    mlp_inv = inverse_rms(middle)
    mlp_normed = (middle * mlp_inv * mlp_gain_f).astype(BF)
    router_probs = jax.nn.softmax(times_transposed(mlp_normed, router_t), axis=-1)
    grad_result = cotangent[0].astype(F32)
    if gathered:
        combine = jnp.where(moe.chosen, router_probs, 0.0)
        high = combine.astype(BF)
        mlp_normed, high, *dy[3] = sync(mlp_normed, high, *dy[3])
        block = moe.noted(mlp_normed, high, (combine - high.astype(F32)).astype(BF))
        grad_mlp_normed, weighted = moe.run(
            block, dy, gate_weight[0], up_weight[0], down_weight[0]
        )
        weight_grads = moe.weight_grads
    else:
        mixture, grad_mlp_normed, weighted, weight_grads = experts_sent(
            lay, mlp_normed, routes[0], router_probs, grad_result, gate_weight[0], up_weight[0], down_weight[0]
        )
    grad_logits = (weighted - router_probs * jnp.sum(weighted, axis=-1, keepdims=True)).astype(BF)
    grad_router_t = contract_rows(grad_logits, mlp_normed)
    grad_mlp_normed = grad_mlp_normed + dot(grad_logits, router_t)
    grad_middle_norm, grad_mlp_gain = norm_backward(middle, mlp_inv, mlp_gain_f, grad_mlp_normed)
    grad_middle = grad_result + grad_middle_norm
    grad_branch = grad_middle.astype(BF)
    grad_attended = times_transposed(grad_branch, out_w).astype(BF)
    grad_heads = a2a(lay.head_blocks(grad_attended), "ctx").reshape(seq_rows, cols)

    if gathered:
        mix = {1: moe.mixture_parts(1, moe.tail), 2: moe.mixture_parts(2, grad_heads)}
    scaled_q, scaled_k, grad_value, dots, grad_gains = attention.backward(grad_heads, kept, qkv, inv, own_gains)
    if gathered:
        dots, *mix[1] = sync(dots, *mix[1])
        mixture = lay.ring_step(moe.spread(1, mix[1], None))
    dots = sum_heads(dots.sum(0))

    def through_norm(scaled, pre, n):
        inverse = inv[n][:, None]
        return (inverse * scaled - pre * (inverse * inverse * inverse) * dots[n][:, None]).astype(BF)

    grad_pre = jnp.concatenate(
        [through_norm(scaled_q, query_pre, 0), through_norm(scaled_k, key_pre, 1), grad_value], axis=-1
    )
    grad_qkv = contract_rows(normed, grad_pre).astype(BF)
    layer_rows = nc * rb

    def qkv_part(step):
        return lax.dynamic_slice_in_dim(grad_qkv, lay.layer_at(step) * layer_rows, layer_rows, 0)

    packed = jnp.concatenate(
        [grad_router_t]
        + [g[None] for g in (lay.all_heads(grad_gains[0]), lay.all_heads(grad_gains[1]), grad_mlp_gain)],
        axis=0,
    )
    kinds = expert_count + 3
    packed = packed.reshape(kinds, devices, rb).transpose(1, 0, 2).reshape(devices, kinds * rb)
    packed = a2a(packed, ALL).sum(0).reshape(kinds, rb)
    halves = jnp.stack([lay.arrival(), 2 * nc - 1 - lay.arrival()], axis=1).reshape(-1).astype(jnp.int32)
    branch_all = jnp.concatenate(lay.gather_ctx(after(grad_branch, grad_pre)), axis=0)
    attended_arrival = attended_b.reshape(nc, tok_rows, cols)[lay.arrival()].reshape(seq_rows, cols)
    grad_out = contract_rows(attended_arrival, branch_all).astype(BF).reshape(hpd, lay.group, rb, width)
    share = cx % lay.group
    terms = []
    for k in range(lay.group):
        term = lax.dynamic_index_in_dim(grad_out, share ^ k, 1, keepdims=False)
        terms.append(lay.swap(term, k) if k else term)
    terms = jnp.stack(terms)

    def out_part(step):
        layer = lay.layer_at(step)
        return terms[(layer // hpd) ^ share, layer % hpd]

    total, out_total = qkv_part(1), out_part(1)
    expert_grads = []
    if gathered:
        mix.update({step: moe.mixture_parts(step, grad_pre) for step in (3, 0)})
    for n, step in enumerate(list(range(2, nz)) + [0]):
        total, out_total = lay.ring_step(total), lay.ring_step(out_total)
        beside = []
        if n < 3:
            expert_grads.append(weight_grads(n, total if n else grad_pre))
            beside.append(expert_grads[-1])
        if n == 0:
            near, far = project_back(layers, halves, grad_pre, ring, half)
            beside += [near, far]
            if gathered:
                mixture, *mix[2] = sync(mixture, *mix[2])
                mixture = moe.spread(2, mix[2], mixture)
                beside.append(mixture)
        elif n == 1:
            grad_normed = lay.reduce_ctx(near, far)
            if gathered:
                mixture = lay.ring_step(mixture)
                beside += [mixture] + mix[3]
        elif n == 2 and gathered:
            mixture = lay.ring_step(moe.spread(3, mix[3], mixture))
            beside.append(mixture)
        total, out_total, *beside = sync(total, out_total, *beside)
        if n < 3:
            expert_grads[-1] = beside.pop(0)
        if n == 0:
            near, far = beside[:2]
            if gathered:
                mixture = beside[2]
        elif n == 1 and gathered:
            mixture, mix[3] = beside[0], beside[1:]
        elif n == 2 and gathered:
            mixture = beside[0]
        total = (total.astype(F32) + qkv_part(step).astype(F32)).astype(BF)
        out_total = (out_total.astype(F32) + out_part(step).astype(F32)).astype(BF)
    grad_qkv = a2a(total.reshape(nc, rb, 3 * cols), "ctx")
    grad_out_w = out_total.astype(F32)
    grad_down_w, grad_gate_w, grad_up_w = expert_grads
    if gathered:
        mixture = moe.spread(0, mix[0], mixture).astype(F32)
    result = middle + mixture
    grad_query_w, grad_key_w, grad_value_w, grad_attn_gain = lay.weight_rows(
        grad_qkv, (query_weight, key_weight, value_weight)
    )
    grad_attn_gain = grad_attn_gain[0] / attn_gain.astype(F32)
    attn_inv = inverse_rms(inputs_f)
    grad_inputs_norm, _ = norm_backward(inputs_f, attn_inv, attn_gain_f, grad_normed.astype(F32))
    grad_inputs = grad_middle + grad_inputs_norm
    gains = [grad_attn_gain] + [packed[expert_count + k] for k in range(3)]
    return (
        result.astype(BF)[None],
        grad_inputs.astype(BF)[None],
        gains[0],
        grad_query_w,
        grad_key_w,
        grad_value_w,
        gains[1],
        gains[2],
        grad_out_w,
        gains[3],
        packed[:expert_count].T,
        grad_gate_w[None],
        grad_up_w[None],
        grad_down_w[None],
    )


def solution(mesh):
    both = ("dp", "ctx")
    in_specs = (
        P("dp", "ctx", None),
        P("dp", "ctx", None),
        P("dp", "ctx", None),
        P(both),
        P(both, None),
        P(both, None),
        P(both, None),
        P(both),
        P(both),
        P(both, None),
        P(both),
        P(both, None),
        P(both, None, None),
        P(both, None, None),
        P(both, None, None),
    )
    out_specs = (
        P("dp", "ctx", None),
        P("dp", "ctx", None),
        P(both),
        P(both, None),
        P(both, None),
        P(both, None),
        P(both),
        P(both),
        P(both, None),
        P(both),
        P(both, None),
        P(both, None, None),
        P(both, None, None),
        P(both, None, None),
    )
    return jax.shard_map(body, mesh=mesh, in_specs=in_specs, out_specs=out_specs, check_vma=False)
```

```python
import functools
import math

import jax
import jax.numpy as jnp
import numpy as np
from jax import lax
from jax.experimental import pallas as pl
from jax.experimental.pallas import tpu as pltpu
from jax.sharding import PartitionSpec as P

HEADS = 16
HEAD_DIM = 128
TOP = 8

EPSILON = 1e-05
NEG_LARGE = -1e30
NOTES = 128
BF = jnp.bfloat16
F32 = jnp.float32
ALL = ("dp", "ctx")


def dot(left, right):
    return jnp.dot(left, right, preferred_element_type=F32)


def contract_rows(left, right):
    return lax.dot_general(left, right, (((0,), (0,)), ((), ())), preferred_element_type=F32)


def times_transposed(left, right):
    return lax.dot_general(left, right, (((1,), (1,)), ((), ())), preferred_element_type=F32)


def inverse_rms(tensor):
    return lax.rsqrt(jnp.mean(tensor * tensor, axis=-1, keepdims=True) + EPSILON)


def norm_backward(tensor, inverse, gain_vec, grad_in):
    scaled = grad_in * gain_vec
    grad_gain = jnp.sum(grad_in * tensor * inverse, axis=0)
    grad_tensor = inverse * scaled - tensor * (inverse * inverse * inverse) * jnp.mean(
        scaled * tensor, axis=-1, keepdims=True
    )
    return (grad_tensor, grad_gain)


class Layout:
    def __init__(self, rb):
        self.nz = lax.axis_size("dp")
        self.nc = lax.axis_size("ctx")
        self.dz = lax.axis_index("dp")
        self.cx = lax.axis_index("ctx")
        nz, nc = self.nz, self.nc
        order = [0] + list(range(1, nz, 2)) + list(range(nz - 2 + nz % 2, 0, -2))
        self.ring = [(order[i], order[(i + 1) % nz]) for i in range(nz)]
        odd = self.dz % 2 == 1
        self.pos = jnp.where(odd, (self.dz + 1) // 2, jnp.where(self.dz == 0, 0, nz - self.dz // 2))
        self.bits = [1 << b for b in range(1, (nc - 1).bit_length())]
        self.flips = list(range(2, nc, 2))
        self.hpd = HEADS // nc
        self.cols = self.hpd * HEAD_DIM
        self.group = HEAD_DIM // rb
        self.rb = rb

    def swap(self, value, bit):
        return lax.ppermute(value, "ctx", [(i, i ^ bit) for i in range(self.nc)])

    def ring_step(self, value):
        return lax.ppermute(value, "dp", self.ring)

    def layer_at(self, step):
        place = (self.pos - step) % self.nz
        back = jnp.where(place == 0, 0, 2 * (self.nz - place))
        return jnp.where((place > 0) & (place <= self.nz // 2), 2 * place - 1, back)

    def gather_ring(self, block):
        blocks = [block]
        for _ in range(self.nz - 1):
            blocks.append(self.ring_step(blocks[-1]))
        return blocks

    def gather_near(self, value):
        return jnp.concatenate([value] + [self.swap(value, flip) for flip in self.flips], axis=0)

    def gather_ctx(self, value):
        near = self.gather_near(value)
        return (near, self.swap(near, 1))

    def reduce_ctx(self, near, far):
        total = (near.astype(F32) + self.swap(far, 1).astype(F32)).astype(BF)
        return self.reduce_chips(total)

    def reduce_chips(self, total):
        blocks = total.reshape((self.nc // 2, -1) + total.shape[1:])
        half = blocks.shape[1] // 2
        outs = []
        for color in (0, 1):
            part = blocks[:, color * half : (color + 1) * half]
            held = list(range(self.nc // 2))
            for bit in self.bits[::-1] if color == 0 else self.bits:
                keep = np.array([n for n, h in enumerate(held) if not 2 * h & bit])
                send = np.array([n for n, h in enumerate(held) if 2 * h & bit])
                other = self.swap(jnp.stack([part[n] for n in send]), bit)
                part = (jnp.stack([part[n] for n in keep]).astype(F32) + other.astype(F32)).astype(BF)
                held = [held[n] for n in keep]
            outs.append(part[0])
        return jnp.concatenate(outs, axis=0)

    def reduce_ring(self, parts):
        total = parts(1)
        for step in list(range(2, self.nz)) + [0]:
            total = (self.ring_step(total).astype(F32) + parts(step).astype(F32)).astype(BF)
        return total

    def arrival(self):
        flips = np.array([2 * n + core for core in (0, 1) for n in range(self.nc // 2)], np.int32)
        return jnp.asarray(flips) ^ self.cx

    def arrival_place(self):
        flips = jnp.arange(self.nc) ^ self.cx
        return (flips % 2) * (self.nc // 2) + flips // 2

    def head_blocks(self, value):
        rows = value.shape[0]
        split = value.reshape(rows, self.group, self.hpd, self.nc // self.group, HEAD_DIM)
        return split.transpose(3, 1, 0, 2, 4).reshape(self.nc, rows, self.cols)

    def head_rows(self, value):
        rows = value.shape[1]
        split = value.reshape(self.nc // self.group, self.group, rows, self.hpd, HEAD_DIM)
        return split.transpose(2, 1, 3, 0, 4).reshape(rows, self.nc * self.cols)

    def head_at(self, device, n):
        return ((device % self.group) * self.hpd + n) * (self.nc // self.group) + device // self.group

    def weight_rows(self, grads, weights, gain):
        count, rows = len(weights), weights[0].shape[0]
        width = weights[0].shape[1]

        def kernel(gain, grads, *refs):
            sums = 0.0
            gain_col = column(gain[...])
            for device in range(self.nc):
                for w in range(count):
                    for n in range(self.hpd):
                        head = slice(self.head_at(device, n) * HEAD_DIM, (self.head_at(device, n) + 1) * HEAD_DIM)
                        start = w * self.cols + n * HEAD_DIM
                        part = grads[device, :, start : start + HEAD_DIM].astype(F32)
                        refs[count + w][:, head] = part
                        sums += part * refs[w][:, head].astype(F32)
            refs[-1][...] = as_row(jnp.sum(sums, axis=-1, keepdims=True) / gain_col)

        shape = jax.ShapeDtypeStruct((rows, width), F32)
        return pl.pallas_call(
            kernel,
            out_shape=[shape] * count + [jax.ShapeDtypeStruct((1, rows), F32)],
            compiler_params=pltpu.CompilerParams(vmem_limit_bytes=24 * 2**20),
        )(gain.astype(F32)[None], grads, *weights)

    def slot_of(self, layer):
        place = jnp.where(layer % 2 == 1, (layer + 1) // 2, jnp.where(layer == 0, 0, self.nz - layer // 2))
        return (self.pos - place) % self.nz

    def head_weights(self, blocks):
        blocks = jnp.stack(blocks)
        share = self.cx % self.group
        rows = jnp.zeros((self.hpd, self.group) + blocks.shape[1:], blocks.dtype)
        for k in range(self.group):
            other = share ^ k
            part = jnp.stack(
                [
                    lax.dynamic_index_in_dim(blocks, self.slot_of(other * self.hpd + n), 0, keepdims=False)
                    for n in range(self.hpd)
                ]
            )
            part = self.swap(part, k) if k else part
            rows = lax.dynamic_update_slice(rows, part[:, None], (0, other, 0, 0))
        return rows.reshape(self.cols, blocks.shape[-1])

    def own_heads(self, vector):
        return self.head_blocks(vector[None])[self.cx, 0]

    def all_heads(self, vector):
        whole = jnp.zeros((self.nc, 1, self.cols), vector.dtype)
        whole = lax.dynamic_update_slice(whole, vector[None, None], (self.cx, 0, 0))
        return self.head_rows(whole)[0]


def sync(*values):
    return lax.optimization_barrier(values)


def after(value, *deps):
    return lax.optimization_barrier((value,) + deps)[0]


def a2a(value, axes):
    return lax.all_to_all(value, axes, split_axis=0, concat_axis=0, tiled=True)


def column(row):
    return jnp.broadcast_to(row, (row.shape[1], row.shape[1])).T[:, :1]


def as_row(col):
    return jnp.broadcast_to(col, (col.shape[0], col.shape[0])).T[:1]


def lane_pick(notes, *lanes):
    lane = lax.broadcasted_iota(jnp.int32, notes.shape, 1)
    keep = functools.reduce(jnp.logical_or, [lane == n for n in lanes])
    return jnp.sum(jnp.where(keep, notes.astype(F32), 0.0), axis=-1, keepdims=True)


def pick_kernel(capacity, count, expert_ref, block, out):
    rows = block.shape[0]
    width = out.shape[1]
    start = block.shape[1] - NOTES
    before = lax.broadcasted_iota(jnp.int32, (rows, rows), 0) < lax.broadcasted_iota(jnp.int32, (rows, rows), 1)
    before = jnp.where(before, 1.0, 0.0).astype(BF)
    for n in range(count):
        named = lane_pick(block[:, start:], expert_ref[n])
        named = jnp.broadcast_to(named, (rows, rows)).T[:capacity]
        slot = dot(named.astype(BF), before)
        mine = lax.broadcasted_iota(jnp.int32, slot.shape, 0).astype(F32)
        choose = jnp.where((slot == mine) & (named > 0.5), 1.0, 0.0).astype(BF)
        out[n * capacity : (n + 1) * capacity] = dot(choose, block[:, :width]).astype(BF)


def pick_rows(block, experts, capacity, width):
    rows, wide = block.shape
    count = experts.shape[0]
    return pl.pallas_call(
        functools.partial(pick_kernel, capacity, count),
        grid_spec=pltpu.PrefetchScalarGridSpec(
            num_scalar_prefetch=1,
            grid=(1,),
            in_specs=[pl.BlockSpec((rows, wide), lambda n, experts: (0, 0))],
            out_specs=pl.BlockSpec((count * capacity, width), lambda n, experts: (0, 0)),
        ),
        out_shape=jax.ShapeDtypeStruct((count * capacity, width), BF),
        compiler_params=pltpu.CompilerParams(vmem_limit_bytes=24 * 2**20),
        cost_estimate=pl.CostEstimate(
            flops=2 * count * rows * capacity * width, bytes_accessed=4 * count * rows * width, transcendentals=0
        ),
    )(experts, block)


def add_kernel(left, right, *refs):
    refs[-1][...] = (left[...].astype(F32) + right[...].astype(F32)).astype(BF)


def add_rows(left, right, *deps, tile=96):
    rows, width = left.shape
    row = pl.BlockSpec((tile, width), lambda n: (n, 0))
    return pl.pallas_call(
        add_kernel,
        grid=(rows // tile,),
        in_specs=[row, row] + [pl.BlockSpec(memory_space=pl.ANY)] * len(deps),
        out_specs=row,
        out_shape=jax.ShapeDtypeStruct((rows, width), BF),
        compiler_params=pltpu.CompilerParams(vmem_limit_bytes=40 * 2**20),
        cost_estimate=pl.CostEstimate(flops=rows * width, bytes_accessed=6 * rows * width, transcendentals=0),
    )(left, right, *deps)


def spread_kernel(capacity, has_sum, expert_ref, notes, *refs):
    out = refs[-1]
    parts = refs[: -2 if has_sum else -1]
    rows = notes.shape[0]
    after_it = lax.broadcasted_iota(jnp.int32, (rows, rows), 1) < lax.broadcasted_iota(jnp.int32, (rows, rows), 0)
    after_it = jnp.where(after_it, 1.0, 0.0).astype(BF)
    total = refs[-2][...].astype(F32) if has_sum else 0.0
    n = 0
    for part in parts:
        for place in range(0, part.shape[0], capacity):
            named = jnp.broadcast_to(lane_pick(notes[...], expert_ref[n]), (rows, capacity))
            slot = dot(after_it, named.astype(BF))
            mine = lax.broadcasted_iota(jnp.int32, slot.shape, 1).astype(F32)
            choose = jnp.where((slot == mine) & (named > 0.5), 1.0, 0.0).astype(BF)
            total += dot(choose, part[place : place + capacity])
            n += 1
    out[...] = total.astype(BF)


def spread_rows(block, experts, parts, total, capacity):
    rows = block.shape[0]
    width = parts[0].shape[1]
    place = block.shape[1] // NOTES - 1
    row = pl.BlockSpec((rows, width), lambda n, experts: (0, 0))
    return pl.pallas_call(
        functools.partial(spread_kernel, capacity, total is not None),
        grid_spec=pltpu.PrefetchScalarGridSpec(
            num_scalar_prefetch=1,
            grid=(1,),
            in_specs=[pl.BlockSpec((rows, NOTES), lambda n, experts: (0, place))]
            + [pl.BlockSpec(p.shape, lambda n, experts: (0, 0)) for p in parts]
            + ([row] if total is not None else []),
            out_specs=row,
        ),
        out_shape=jax.ShapeDtypeStruct((rows, width), BF),
        compiler_params=pltpu.CompilerParams(vmem_limit_bytes=24 * 2**20),
        cost_estimate=pl.CostEstimate(
            flops=8 * rows * rows * width, bytes_accessed=16 * rows * width, transcendentals=0
        ),
    )(experts, block, *parts, *([total] if total is not None else []))


def expert_kernel(
    kinds, expert_ref, near, far, dy_near, dy_far, gate_w, up_w, down_w, *refs,
):
    sides, mids, outs = refs[-10:-8], refs[-8:-2], refs[-2:]
    tile = near.shape[0]
    width = dy_near.shape[1]
    expert = expert_ref[0]
    rows = jnp.concatenate([near[:, :width], far[:, :width]], axis=0)
    notes = jnp.concatenate([near[:, width:], far[:, width:]], axis=0)
    dy = jnp.concatenate([dy_near[...], dy_far[...]], axis=0)

    def put(pair, start, value):
        pair[0][:, start : start + value.shape[1]] = value[:tile]
        pair[1][:, start : start + value.shape[1]] = value[tile:]

    gate_col = lane_pick(notes, expert + kinds, expert + 2 * kinds)
    gate_pre = dot(rows, gate_w[...])
    up_pre = dot(rows, up_w[...])
    sigmoid_val = jax.nn.sigmoid(gate_pre)
    silu = gate_pre * sigmoid_val
    hidden_f = silu * up_pre
    put(outs, 0, (dot(hidden_f.astype(BF), down_w[...]) * gate_col).astype(BF))
    grad_hidden = times_transposed(dy, down_w[...])
    weighted = jnp.sum(grad_hidden * hidden_f, axis=-1, keepdims=True) * gate_col
    lane = lax.broadcasted_iota(jnp.int32, (2 * tile, NOTES), 1)
    put(sides, width, jnp.where(lane == expert, weighted, 0.0).astype(BF))
    grad_hidden = grad_hidden * gate_col
    grad_gate_pre = (
        grad_hidden * up_pre * (sigmoid_val * (1.0 + gate_pre * (1.0 - sigmoid_val)))
    ).astype(BF)
    grad_up_pre = (grad_hidden * silu).astype(BF)
    for n, mid in enumerate(((hidden_f * gate_col).astype(BF), grad_gate_pre, grad_up_pre)):
        mids[2 * n][...] = mid[:tile]
        mids[2 * n + 1][...] = mid[tile:]
    put(
        sides,
        0,
        (
            times_transposed(grad_gate_pre, gate_w[...]) + times_transposed(grad_up_pre, up_w[...])
        ).astype(BF),
    )


def expert_chunk(kinds, expert, near, far, dy_near, dy_far, gate_w, up_w, down_w, *deps, tile=128):
    rows, width = dy_near.shape
    units = gate_w.shape[1]

    def row(cols):
        return pl.BlockSpec((tile, cols), lambda i, expert: (i, 0))

    def whole(array):
        return pl.BlockSpec(array.shape, lambda i, expert: (0, 0), pipeline_mode=pl.Buffered(1))

    wide = near.shape[1]
    outs = [wide] * 2 + [units] * 6 + [width] * 2
    return pl.pallas_call(
        functools.partial(expert_kernel, kinds),
        grid_spec=pltpu.PrefetchScalarGridSpec(
            num_scalar_prefetch=1,
            grid=(rows // tile,),
            in_specs=[row(wide), row(wide), row(width), row(width), whole(gate_w), whole(up_w), whole(down_w)]
            + [pl.BlockSpec(memory_space=pl.ANY)] * len(deps),
            out_specs=[row(cols) for cols in outs],
        ),
        out_shape=[jax.ShapeDtypeStruct((rows, cols), BF) for cols in outs],
        compiler_params=pltpu.CompilerParams(vmem_limit_bytes=56 * 2**20),
        cost_estimate=pl.CostEstimate(
            flops=24 * rows * width * units,
            bytes_accessed=16 * rows * width,
            transcendentals=2 * rows * units,
        ),
    )(expert, near, far, dy_near, dy_far, gate_w, up_w, down_w, *deps)


def contract_kernel(count, *refs):
    total = 0.0
    for left, right in zip(refs[:count], refs[count : 2 * count]):
        total += contract_rows(left[...], right[...])
    refs[-1][...] = total


def contract_many(lefts, rights, rows, cols, dep, tile=256):
    count = len(lefts)
    depth = lefts[0].shape[0]
    tall = rows >= cols
    strip = pl.BlockSpec((depth, tile), lambda i: (0, i))
    held = pl.BlockSpec((depth, min(rows, cols)), lambda i: (0, 0), pipeline_mode=pl.Buffered(1))
    return pl.pallas_call(
        functools.partial(contract_kernel, count),
        grid=(max(rows, cols) // tile,),
        in_specs=[strip if tall else held] * count
        + [held if tall else strip] * count
        + [pl.BlockSpec(memory_space=pl.ANY)],
        out_specs=pl.BlockSpec((tile, cols), lambda i: (i, 0)) if tall else pl.BlockSpec((rows, tile), lambda i: (0, i)),
        out_shape=jax.ShapeDtypeStruct((rows, cols), F32),
        compiler_params=pltpu.CompilerParams(vmem_limit_bytes=56 * 2**20),
        cost_estimate=pl.CostEstimate(
            flops=2 * depth * count * rows * cols,
            bytes_accessed=2 * depth * count * (rows + cols) + 4 * rows * cols,
            transcendentals=0,
        ),
    )(*lefts, *rights, dep)


def columns(rows):
    count = rows.shape[1] // 128
    return jnp.concatenate([column(rows[:, n * 128 : (n + 1) * 128]) for n in range(count)], axis=0)


def as_rows(cols):
    count = cols.shape[0] // 128
    return jnp.concatenate([as_row(cols[n * 128 : (n + 1) * 128]) for n in range(count)], axis=1)


def norm_kernel(place_ref, near, far, gain, out):
    n = pl.program_id(0)
    steps = pl.num_programs(0)
    rows = jnp.where(place_ref[n] < steps // 2, near[...], far[...]).astype(F32)
    out[...] = (rows * inverse_rms(rows) * gain[...]).astype(BF)


def norm_in_order(place, near, far, gain, half):
    steps = place.shape[0]
    width = near.shape[1]
    return pl.pallas_call(
        norm_kernel,
        grid_spec=pltpu.PrefetchScalarGridSpec(
            num_scalar_prefetch=1,
            grid=(steps,),
            in_specs=[
                pl.BlockSpec((half, width), lambda n, place: (jnp.minimum(place[n], steps // 2 - 1), 0)),
                pl.BlockSpec((half, width), lambda n, place: (jnp.maximum(place[n] - steps // 2, 0), 0)),
                pl.BlockSpec((1, width), lambda n, place: (0, 0)),
            ],
            out_specs=pl.BlockSpec((half, width), lambda n, place: (n, 0)),
        ),
        out_shape=jax.ShapeDtypeStruct((steps * half, width), BF),
        compiler_params=pltpu.CompilerParams(vmem_limit_bytes=16 * 2**20),
        cost_estimate=pl.CostEstimate(
            flops=4 * steps * half * width, bytes_accessed=6 * steps * half * width, transcendentals=0
        ),
    )(place, near, far, gain)


def project_kernel(count, cols, layer_ref, rows, *refs):
    total = 0.0
    for n in range(count):
        depth = refs[n].shape[0]
        start = pl.multiple_of(layer_ref[n] * depth, depth)
        total += dot(rows[:, pl.ds(start, depth)], refs[n][...])
    out, squares = refs[count:]
    out[...] = total
    for n in range(2):
        part = total[:, n * cols : (n + 1) * cols]
        squares[n : n + 1] = as_rows(jnp.sum(part * part, axis=-1, keepdims=True))


def project(layers, rows, weights, cols, tile=256):
    count = len(weights)
    total, width = rows.shape
    wide = weights[0].shape[1]
    held = pl.BlockSpec(weights[0].shape, lambda n, layers: (0, 0), pipeline_mode=pl.Buffered(1))
    return pl.pallas_call(
        functools.partial(project_kernel, count, cols),
        grid_spec=pltpu.PrefetchScalarGridSpec(
            num_scalar_prefetch=1,
            grid=(total // tile,),
            in_specs=[pl.BlockSpec((tile, width), lambda n, layers: (n, 0))] + [held] * count,
            out_specs=[
                pl.BlockSpec((tile, wide), lambda n, layers: (n, 0)),
                pl.BlockSpec((2, tile), lambda n, layers: (0, n)),
            ],
        ),
        out_shape=[jax.ShapeDtypeStruct((total, wide), F32), jax.ShapeDtypeStruct((2, total), F32)],
        compiler_params=pltpu.CompilerParams(vmem_limit_bytes=40 * 2**20),
        cost_estimate=pl.CostEstimate(
            flops=2 * total * width * wide, bytes_accessed=2 * total * width + 6 * total * wide, transcendentals=0
        ),
    )(layers, rows, *weights)


def grad_blocks_kernel(layer_ref, rows, grads, *outs):
    step = pl.program_id(0)
    block = contract_rows(rows[...], grads[...]).astype(BF)
    for n, out in enumerate(outs):

        @pl.when(step == n)
        def _():
            out[...] = block


def grad_blocks(layers, rows, grads):
    total, width = rows.shape
    wide = grads.shape[1]
    count = layers.shape[0]
    depth = width // count
    return pl.pallas_call(
        grad_blocks_kernel,
        grid_spec=pltpu.PrefetchScalarGridSpec(
            num_scalar_prefetch=1,
            grid=(count,),
            in_specs=[
                pl.BlockSpec((total, depth), lambda n, layers: (0, layers[n])),
                pl.BlockSpec((total, wide), lambda n, layers: (0, 0), pipeline_mode=pl.Buffered(1)),
            ],
            out_specs=[pl.BlockSpec((depth, wide), lambda n, layers: (0, 0))] * count,
        ),
        out_shape=[jax.ShapeDtypeStruct((depth, wide), BF)] * count,
        compiler_params=pltpu.CompilerParams(vmem_limit_bytes=48 * 2**20),
        cost_estimate=pl.CostEstimate(
            flops=2 * total * width * wide, bytes_accessed=2 * (total + wide) * width, transcendentals=0
        ),
    )(layers, rows, grads)


def project_back_kernel(count, half, layer_ref, block_ref, grads, *refs):
    near, far = refs[-2:]
    step = pl.program_id(0)
    blocks = near.shape[0] // half
    for side, out in enumerate((near, far)):
        first = (side * pl.num_programs(0) + step) * blocks
        rows = jnp.concatenate(
            [grads[pl.ds(pl.multiple_of(block_ref[first + n] * half, half), half)] for n in range(blocks)], axis=0
        )
        for n in range(count):
            depth = refs[n].shape[0]
            start = pl.multiple_of(layer_ref[n] * depth, depth)
            out[:, pl.ds(start, depth)] = times_transposed(rows, refs[n][...]).astype(BF)


def project_back(layers, blocks, grads, weights, half, dep, tile=256):
    count = len(weights)
    total, wide = grads.shape
    width = count * weights[0].shape[0]
    held = pl.BlockSpec(weights[0].shape, lambda n, *refs: (0, 0), pipeline_mode=pl.Buffered(1))
    out = jax.ShapeDtypeStruct((total // 2, width), BF)
    return pl.pallas_call(
        functools.partial(project_back_kernel, count, half),
        grid_spec=pltpu.PrefetchScalarGridSpec(
            num_scalar_prefetch=2,
            grid=(total // 2 // tile,),
            in_specs=[pl.BlockSpec((total, wide), lambda n, *refs: (0, 0), pipeline_mode=pl.Buffered(1))]
            + [held] * count
            + [pl.BlockSpec(memory_space=pl.ANY)],
            out_specs=[pl.BlockSpec((tile, width), lambda n, *refs: (n, 0))] * 2,
        ),
        out_shape=[out, out],
        compiler_params=pltpu.CompilerParams(vmem_limit_bytes=40 * 2**20),
        cost_estimate=pl.CostEstimate(
            flops=2 * total * width * wide, bytes_accessed=2 * total * (width + wide), transcendentals=0
        ),
    )(layers, blocks, grads, *weights, dep)


def turn(value, cosine, sine):
    return value * cosine + pltpu.roll(value, HEAD_DIM // 2, 1) * sine


def masked_scores(queries, keys, first, score_scale):
    scores = times_transposed(queries, keys) * score_scale
    row = lax.broadcasted_iota(jnp.int32, scores.shape, 0) + first
    col = lax.broadcasted_iota(jnp.int32, scores.shape, 1)
    return scores, col <= row


def attention_kernel(
    half, tile, score_scale, place_ref, q_pre, k_pre, v_pre, inv, gains, cosine, sine,
    sent, attended, lse, query_rot, key_rot, value,
):
    rows = q_pre.shape[0]
    cos, sin = cosine[...], sine[...]
    query_rot[...] = turn(q_pre[...] * columns(inv[0:1]) * gains[0:1], cos, sin).astype(BF)
    key_rot[...] = turn(k_pre[...] * columns(inv[1:2]) * gains[1:2], cos, sin).astype(BF)
    value[...] = v_pre[...].astype(BF)
    for n in range(rows // tile):
        first = n * tile
        end = first + tile
        scores, allowed = masked_scores(query_rot[first:end], key_rot[:end], first, score_scale)
        scores = jnp.where(allowed, scores, NEG_LARGE)
        top = jnp.max(scores, axis=-1, keepdims=True)
        probs = jnp.exp(scores - top)
        total = jnp.sum(probs, axis=-1, keepdims=True)
        lse[first:end] = jnp.broadcast_to(top + jnp.log(total), (tile, HEAD_DIM))
        attended[first:end] = dot((probs / total).astype(BF), value[:end])
    for n in range(rows // half):
        place = pl.multiple_of(place_ref[n] * half, half)
        sent[pl.ds(place, half)] = attended[n * half : (n + 1) * half].astype(BF)


def attention_grad_kernel(
    half, tile, score_scale, place_ref, sent_grad, attended, lse, query_rot, key_rot, value, q_pre, k_pre, inv, gains,
    cosine, sine, scaled_q, scaled_k, grad_value, dots, grad_gains, grad_heads, key_sum, value_sum, query_sum,
):
    rows = q_pre.shape[0]
    for n in range(rows // half):
        place = pl.multiple_of(place_ref[n] * half, half)
        grad_heads[n * half : (n + 1) * half] = sent_grad[pl.ds(place, half)]
    key_sum[...] = jnp.zeros_like(key_sum)
    value_sum[...] = jnp.zeros_like(value_sum)
    for n in range(rows // tile):
        first = n * tile
        end = first + tile
        grads = grad_heads[first:end]
        queries = query_rot[first:end]
        delta = jnp.sum(grads.astype(F32) * attended[first:end], axis=-1, keepdims=True)
        scores, allowed = masked_scores(queries, key_rot[:end], first, score_scale)
        probs = jnp.where(allowed, jnp.exp(scores - lse[first:end][:, :1]), 0.0)
        grad_scores = (probs * (times_transposed(grads, value[:end]) - delta)).astype(BF)
        query_sum[first:end] = dot(grad_scores, key_rot[:end])
        key_sum[:end] += contract_rows(grad_scores, queries)
        value_sum[:end] += contract_rows(probs.astype(BF), grads)
    grad_value[...] = value_sum[...].astype(BF)
    cos, sin = cosine[...], -sine[...]
    for n, (total, pre, scaled) in enumerate(((query_sum, q_pre, scaled_q), (key_sum, k_pre, scaled_k))):
        grad = turn(total[...] * score_scale, cos, sin)
        grad_gains[n : n + 1] = jnp.sum(grad * pre[...] * columns(inv[n : n + 1]), axis=0, keepdims=True)
        grad = grad * gains[n : n + 1]
        scaled[...] = grad
        dots[n : n + 1] = as_rows(jnp.sum(grad * pre[...], axis=-1, keepdims=True))


class Attention:
    def __init__(self, rows, half, hpd):
        self.rows, self.half, self.hpd = rows, half, hpd
        self.tile = min(256, rows)
        position = np.arange(rows, dtype=np.float32)
        freq = np.exp(np.arange(HEAD_DIM // 2, dtype=np.float32) * np.float32(-2.0 * math.log(10000.0) / HEAD_DIM))
        angles = position[:, None] * freq[None, :].astype(np.float32)
        self.cosine = jnp.asarray(np.concatenate([np.cos(angles)] * 2, axis=1), F32)
        self.sine = jnp.asarray(np.concatenate([-np.sin(angles), np.sin(angles)], axis=1), F32)
        self.head = pl.BlockSpec((rows, HEAD_DIM), lambda h, place: (0, h))
        self.keys = pl.BlockSpec((rows, HEAD_DIM), lambda h, place: (0, h + hpd))
        self.values = pl.BlockSpec((rows, HEAD_DIM), lambda h, place: (0, h + 2 * hpd))
        self.stat = pl.BlockSpec((2, rows), lambda h, place: (0, 0))
        self.gain = pl.BlockSpec((2, HEAD_DIM), lambda h, place: (0, h))
        self.table = pl.BlockSpec((rows, HEAD_DIM), lambda h, place: (0, 0))
        self.args = (half, self.tile, 1.0 / math.sqrt(HEAD_DIM))
        self.params = pltpu.CompilerParams(vmem_limit_bytes=60 * 2**20)

    def shape(self, dtype):
        return jax.ShapeDtypeStruct((self.rows, self.hpd * HEAD_DIM), dtype)

    def cost(self, products):
        area = self.hpd * self.rows * self.rows
        return pl.CostEstimate(
            flops=products * area * HEAD_DIM, bytes_accessed=self.hpd * self.rows * HEAD_DIM * 24, transcendentals=area
        )

    def call(self, kernel, ins, outs, shapes, scratch, products):
        return pl.pallas_call(
            functools.partial(kernel, *self.args),
            grid_spec=pltpu.PrefetchScalarGridSpec(
                num_scalar_prefetch=1, grid=(self.hpd,), in_specs=ins, out_specs=outs, scratch_shapes=scratch
            ),
            out_shape=shapes,
            compiler_params=self.params,
            cost_estimate=self.cost(products),
        )

    def forward(self, places, qkv, inv, gains):
        ins = [self.head, self.keys, self.values, self.stat, self.gain, self.table, self.table]
        shapes = [self.shape(t) for t in (BF, F32, F32, BF, BF, BF)]
        run = self.call(attention_kernel, ins, [self.head] * 6, shapes, [], 3)
        return run(places, qkv, qkv, qkv, inv, gains, self.cosine, self.sine)

    def backward(self, places, sent_grad, kept, qkv, inv, gains):
        rows, hpd = self.rows, self.hpd
        line = pl.BlockSpec((None, 2, rows), lambda h, place: (h, 0, 0))
        ins = [self.head] * 6 + [self.head, self.keys, self.stat, self.gain, self.table, self.table]
        shapes = [self.shape(F32), self.shape(F32), self.shape(BF)]
        shapes += [jax.ShapeDtypeStruct((hpd, 2, rows), F32), jax.ShapeDtypeStruct((2, hpd * HEAD_DIM), F32)]
        scratch = [pltpu.VMEM((rows, HEAD_DIM), BF)] + [pltpu.VMEM((rows, HEAD_DIM), F32)] * 3
        run = self.call(attention_grad_kernel, ins, [self.head] * 3 + [line, self.gain], shapes, scratch, 6)
        return run(places, sent_grad, *kept, qkv, qkv, inv, gains, self.cosine, self.sine)


class Gathered:
    def __init__(self, lay, routes, expert_count, capacity, width):
        self.lay, self.kinds, self.capacity, self.width = lay, expert_count, capacity, width
        self.tok_rows = routes.shape[0]
        chosen = routes[:, :, None] == jnp.arange(expert_count, dtype=jnp.int32)
        self.chosen = jnp.any(chosen, axis=1)
        first = lay.dz * (lay.nc // 2)
        flipped = first + (lay.cx ^ jnp.array([0] + lay.flips, jnp.int32)) // 2
        self.flipped = flipped.astype(jnp.int32)
        self.own = self.flipped[:1]
        self.straight = (first + jnp.arange(lay.nc // 2)).astype(jnp.int32)

    def noted(self, rows, *notes):
        notes = [self.chosen.astype(BF)] + list(notes)
        rest = NOTES - self.kinds * len(notes)
        return jnp.concatenate([rows] + notes + [jnp.zeros((self.tok_rows, rest), BF)], axis=1)

    def offer(self, block, width=None):
        return pick_rows(block, self.straight, self.capacity, width or block.shape[1])

    def exchange(self, offered):
        groups = [list(range(core, self.lay.nc, 2)) for core in (0, 1)]
        return lax.all_to_all(
            offered, "ctx", split_axis=0, concat_axis=0, tiled=True, axis_index_groups=groups
        )

    def send_back(self, sums):
        chip = self.lay.cx // 2
        parts = [
            lax.dynamic_slice_in_dim(sums, (chip ^ n) * self.capacity, self.capacity, 0)
            for n in range(self.lay.nc // 2)
        ]
        return [parts[0]] + [self.lay.swap(p, flip) for p, flip in zip(parts[1:], self.lay.flips)]

    def spread(self, step, parts, total):
        experts = self.flipped if len(parts) > 1 else self.straight
        return spread_rows(self.blocks[step], experts, parts, total, self.capacity)

    def straighten(self, parts):
        chip = self.lay.cx // 2
        whole = jnp.zeros((len(parts) * self.capacity, parts[0].shape[1]), parts[0].dtype)
        for n, part in enumerate(parts):
            whole = lax.dynamic_update_slice_in_dim(whole, part, (chip ^ n) * self.capacity, 0)
        return whole

    def run(self, block, dy, dy_last, gate_w, up_w, down_w):
        lay, nz = self.lay, self.lay.nz
        self.blocks = blocks = [block]
        self.rows, self.done, self.dy = rows, done, dy = [], [], dy
        back, far_sums = {}, {}
        near = self.exchange(self.offer(block))
        coming = lay.ring_step(block)
        coming, near = sync(coming, near)
        for step in range(nz):
            far = lay.swap(near, 1)
            rows += [near, far]
            if step:
                far_sums[step - 1] = lay.swap(done[-1][1], 1)
            if step + 1 < nz:
                blocks.append(coming)
                near = self.exchange(self.offer(coming))
                if step + 2 < nz:
                    coming = lay.ring_step(coming)
            if step == 0:
                late = self.send_back(dy_last)
            if step == nz - 2:
                last_dy = self.straighten(late)
                dy.append([last_dy, lay.swap(last_dy, 1)])
            sent, deps = [], []
            if step == nz - 1:
                for n in range(1, nz - 1):
                    deps.append(add_rows(done[n][0], far_sums[n]))
                    back[n] = [self.exchange(deps[-1])] if n == 1 else self.send_back(deps[-1])
                    sent += back[n]
            made = list(
                expert_chunk(self.kinds, self.own, *rows[-2:], *dy[step], gate_w, up_w, down_w, *deps)
            )
            held = [made[1], coming] + ([near] if step + 1 < nz else [])
            held += sent[:1] + (late[1:] if step == 1 else []) + (dy[-1][1:] if step == nz - 2 else [])
            held = list(sync(*held))
            made[1], coming = held[:2]
            if step + 1 < nz:
                near = held[2]
            if step == 1:
                late[1:] = held[3:]
            if step == nz - 2:
                dy[-1][1] = held[3]
            if step == nz - 1:
                back[1] = held[2:]
            done.append(made)
        self.grads = {}
        total = self.spread(1, back[1], None)
        far_sums[nz - 1] = lay.swap(done[-1][1], 1)
        for n, step in enumerate(list(range(2, nz)) + [0]):
            coming = lay.ring_step(total)
            if step not in back:
                sums = add_rows(done[step][0], far_sums[step])
                back[step] = [self.exchange(sums)] if step == nz - 1 else self.send_back(sums)
            beside = list(back[step])
            if n < 3:
                self.grads[n] = self.weight_grads(n, total)
                beside.append(self.grads[n])
            if n == 0:
                beside.append(far_sums[nz - 1])
            coming, *beside = sync(coming, *beside)
            if n == 0:
                far_sums[nz - 1] = beside.pop()
            if n < 3:
                self.grads[n] = beside.pop()
            if step == nz - 1:
                beside[0], far_sums[0] = sync(beside[0], far_sums[0])
            total = self.spread(step, beside, coming)
        return total[:, : self.width].astype(F32), total[:, self.width : self.width + self.kinds].astype(F32)

    def out_sum(self, step, *deps):
        near, far = self.done[step][-2:]
        return add_rows(near, self.lay.swap(far, 1), *deps)

    def weight_grads(self, which, dep):
        near = 2 + 2 * which
        mids = [d[k] for d in self.done for k in (near, near + 1)]
        units = mids[0].shape[1]
        if which == 0:
            return contract_many(mids, [d for pair in self.dy for d in pair], units, self.width, dep)
        return contract_many(self.rows, mids, self.width, units, dep)


def experts_sent(lay, mlp_normed, routes, router_probs, grad_result, gate_w, up_w, down_w):
    tok_rows, width = mlp_normed.shape
    expert_count = router_probs.shape[1]
    capacity = 3 * tok_rows * TOP // (2 * expert_count)
    flat_routes = routes.reshape(tok_rows * TOP)
    onehot = (flat_routes[:, None] == jnp.arange(expert_count, dtype=jnp.int32)[None, :]).astype(
        jnp.int32
    )
    slot_index = jnp.sum((jnp.cumsum(onehot, axis=0) - onehot) * onehot, axis=1)
    chosen = onehot.reshape(tok_rows, TOP, expert_count).astype(F32)
    gate_values = jnp.einsum("tke,te->tk", chosen, router_probs)

    def dispatch(rows_in):
        sent = jnp.zeros((expert_count, capacity, width), BF).at[flat_routes, slot_index].set(rows_in)
        return a2a(jnp.repeat(sent, 2, axis=0), ALL)

    def collect(buffer):
        even_rows = buffer[2 * flat_routes, slot_index].astype(F32)
        odd_rows = buffer[2 * flat_routes + 1, slot_index].astype(F32)
        return (even_rows + odd_rows).reshape(tok_rows, TOP, width)

    received = dispatch(jnp.repeat(mlp_normed, TOP, axis=0))
    flat_in = received.reshape(-1, width)
    gate_pre = dot(flat_in, gate_w)
    up_pre = dot(flat_in, up_w)
    hidden = (jax.nn.silu(gate_pre) * up_pre).astype(BF)
    half_out = dot(hidden, down_w).astype(BF).reshape(received.shape)
    expert_rows = collect(a2a(half_out, ALL))
    mixture = jnp.einsum("tk,tkd->td", gate_values, expert_rows)
    grad_gates = jnp.einsum("td,tkd->tk", grad_result, expert_rows)
    grad_rows = (
        (gate_values[:, :, None] * grad_result[:, None, :])
        .astype(BF)
        .reshape(tok_rows * TOP, width)
    )
    grad_flat = dispatch(grad_rows).reshape(-1, width)
    grad_down_w = contract_rows(hidden, grad_flat)
    grad_hidden = times_transposed(grad_flat, down_w)
    sigmoid_val = jax.nn.sigmoid(gate_pre)
    grad_gate_pre = (
        grad_hidden * up_pre * sigmoid_val * (1.0 + gate_pre * (1.0 - sigmoid_val))
    ).astype(BF)
    grad_up_pre = (grad_hidden * jax.nn.silu(gate_pre)).astype(BF)
    grad_gate_w = contract_rows(flat_in, grad_gate_pre)
    grad_up_w = contract_rows(flat_in, grad_up_pre)
    grad_copy = (
        (times_transposed(grad_gate_pre, gate_w) + times_transposed(grad_up_pre, up_w))
        .astype(BF)
        .reshape(received.shape)
    )
    grad_sum = jnp.sum(collect(a2a(grad_copy, ALL)), axis=1)
    weighted = router_probs * jnp.einsum("tk,tke->te", grad_gates, chosen)
    return (mixture, grad_sum, weighted, (grad_down_w, grad_gate_w, grad_up_w))


def body(
    tokens,
    routes,
    cotangent,
    attn_gain,
    query_weight,
    key_weight,
    value_weight,
    query_gain,
    key_gain,
    out_weight,
    mlp_gain,
    router_weight,
    gate_weight,
    up_weight,
    down_weight,
):
    rb = query_weight.shape[0]
    lay = Layout(rb)
    nz, nc, cx = lay.nz, lay.nc, lay.cx
    tok_rows = tokens.shape[1]
    width = tokens.shape[2]
    half = tok_rows // 2
    seq_rows = tok_rows * nc
    expert_count = router_weight.shape[1]
    hpd, cols = lay.hpd, lay.cols
    devices = nz * nc
    capacity = 3 * tok_rows * TOP // (2 * expert_count)
    gathered = (
        nz > 3
        and devices * tok_rows <= 4 * expert_count * capacity
        and 3 * expert_count <= NOTES
        and capacity % 16 == 0
    )

    sent = jnp.concatenate(
        [lay.head_blocks(w) for w in (query_weight, key_weight, value_weight)], axis=-1
    )
    kinds = expert_count + 4
    small = jnp.concatenate(
        [router_weight] + [g[:, None] for g in (query_gain, key_gain, mlp_gain, attn_gain)], axis=1
    )
    small = jnp.broadcast_to(small.T.reshape(1, kinds * rb), (devices, kinds * rb))
    block = a2a(sent, "ctx").reshape(nc * rb, 3 * cols)
    parts = [tokens[0]] + [lay.swap(tokens[0], flip) for flip in lay.flips]
    places = lay.arrival_place()
    places = jnp.concatenate([places * 2, (places * 2 + 1)[::-1]]).astype(jnp.int32)
    if gathered:
        moe = Gathered(lay, routes[0], expert_count, capacity, width)
        dy_blocks = [moe.noted(cotangent[0])]
        dy_blocks.append(lay.ring_step(dy_blocks[0]))
        offered = moe.offer(dy_blocks[0], width)
    out_blocks = [out_weight, lay.ring_step(out_weight)]
    if gathered:
        block, out_blocks[1], dy_blocks[1], offered, *parts[1:3] = sync(
            block, out_blocks[1], dy_blocks[1], offered, *parts[1:3]
        )
    ring, dy = [block], []
    for step in range(1, nz):
        block = lay.ring_step(block)
        beside = []
        if step == 1:
            beside = [a2a(small, ALL)] + parts[1:]
        elif step == 2:
            seq_near = jnp.concatenate(parts, axis=0)
            beside = [lay.swap(seq_near, 1)]
        elif step == 3:
            beside = [norm_in_order(places, seq_near, seq_far, attn_gain_f[None], half)]
            if nz == 4:
                beside.append(lay.head_weights(out_blocks))
        if gathered and step > 1:
            dy.append([moe.exchange(offered)])
            beside.append(dy[-1][0])
            if step == 2:
                offered = moe.offer(dy_blocks[1], width)
                beside.append(offered)
        if step + 1 < nz:
            beside.append(lay.ring_step(out_blocks[-1]))
        block, out_blocks[-1], *beside = sync(block, out_blocks[-1], *beside)
        if step + 1 < nz:
            out_blocks.append(beside.pop())
        if step == 1:
            small, parts[1:] = beside[0], beside[1:]
            small = small.reshape(devices, kinds, rb).transpose(1, 0, 2).reshape(kinds, width)
            router_t = small[:expert_count]
            qgain_f, kgain_f, mlp_gain_f, attn_gain_f = (small[expert_count + k].astype(F32) for k in range(4))
        elif step == 2:
            seq_far = beside[0]
        elif step == 3:
            normed = beside[0]
            if nz == 4:
                out_rows = beside.pop(1)
        if gathered and step > 1:
            dy[-1][0] = beside[1]
            if step == 2:
                offered = beside[2]
        ring.append(block)
    if nz < 4:
        normed = norm_in_order(places, seq_near, seq_far, attn_gain_f[None], half)
    if nz != 4:
        out_rows = lay.head_weights(out_blocks)
    if gathered:
        dy_blocks.append(lay.ring_step(after(dy_blocks[1], ring[-1])))
    layers = jnp.stack([lay.layer_at(step) for step in range(nz)]).astype(jnp.int32)
    qkv, squares = project(layers, normed, ring, cols)
    query_pre, key_pre = qkv[:, :cols], qkv[:, cols : 2 * cols]

    def sum_heads(stats):
        stats = lax.all_gather(stats.reshape(2 * seq_rows // 128, 128), "ctx", axis=0).sum(0)
        return stats.reshape(2, seq_rows) / width

    inv = lax.rsqrt(sum_heads(squares) + EPSILON)
    own_gains = jnp.stack([lay.own_heads(qgain_f), lay.own_heads(kgain_f)])
    attention = Attention(seq_rows, half, hpd)
    if gathered:
        inv, dy_blocks[2] = sync(inv, dy_blocks[2])
        dy_blocks.append(lay.ring_step(dy_blocks[2]))
        dy.append([moe.exchange(moe.offer(dy_blocks[2], width))])
        for pair in dy[:2]:
            pair.append(lay.swap(pair[0], 1))
    attended_b, *kept = attention.forward(places, qkv, inv, own_gains)
    if gathered:
        attended_b, out_rows, dy_blocks[3], dy[2][0], dy[0][1], dy[1][1] = sync(
            attended_b, out_rows, dy_blocks[3], dy[2][0], dy[0][1], dy[1][1]
        )
    near, far = (dot(attended_b[part], out_rows).astype(BF) for part in (slice(0, seq_rows // 2), slice(seq_rows // 2, None)))
    branch = near.astype(F32) + lay.swap(far, 1).astype(F32)
    if gathered:
        offered = moe.offer(dy_blocks[3], width)
        branch, offered = sync(branch.astype(BF), offered)
        dy[2].append(lay.swap(dy[2][0], 1))
    branch = lay.reduce_chips(branch.astype(BF))
    if gathered:
        branch, dy[2][1], offered = sync(branch, dy[2][1], offered)
    inputs_f = tokens[0].astype(F32)
    middle = inputs_f + branch.astype(F32)
    mlp_inv = inverse_rms(middle)
    mlp_normed = (middle * mlp_inv * mlp_gain_f).astype(BF)
    router_probs = jax.nn.softmax(times_transposed(mlp_normed, router_t), axis=-1)
    grad_result = cotangent[0].astype(F32)
    if gathered:
        combine = jnp.where(moe.chosen, router_probs, 0.0)
        high = combine.astype(BF)
        block = moe.noted(mlp_normed, high, (combine - high.astype(F32)).astype(BF))
        grad_mlp_normed, weighted = moe.run(
            block, dy, offered, gate_weight[0], up_weight[0], down_weight[0]
        )
    else:
        mixture, grad_mlp_normed, weighted, weight_grads = experts_sent(
            lay, mlp_normed, routes[0], router_probs, grad_result, gate_weight[0], up_weight[0], down_weight[0]
        )
    grad_logits = (weighted - router_probs * jnp.sum(weighted, axis=-1, keepdims=True)).astype(BF)
    grad_router_t = contract_rows(grad_logits, mlp_normed)
    grad_mlp_normed = grad_mlp_normed + dot(grad_logits, router_t)
    grad_middle_norm, grad_mlp_gain = norm_backward(middle, mlp_inv, mlp_gain_f, grad_mlp_normed)
    grad_middle = grad_result + grad_middle_norm
    grad_branch = grad_middle.astype(BF)
    branch_near = lay.gather_near(grad_branch)
    if gathered:
        branch_near, first = sync(branch_near, moe.out_sum(1))
        first = moe.exchange(first)
    branch_far = lay.swap(branch_near, 1)
    grad_heads = jnp.concatenate(
        [times_transposed(part, out_rows).astype(BF) for part in (branch_near, branch_far)], axis=0
    )
    scaled_q, scaled_k, grad_value, dots, grad_gains = attention.backward(places, grad_heads, kept, qkv, inv, own_gains)
    packed = jnp.concatenate(
        [grad_router_t]
        + [g[None] for g in (lay.all_heads(grad_gains[0]), lay.all_heads(grad_gains[1]), grad_mlp_gain)],
        axis=0,
    )
    kinds = expert_count + 3
    packed = packed.reshape(kinds, devices, rb).transpose(1, 0, 2).reshape(devices, kinds * rb)
    if gathered:
        dots, first, packed = sync(dots, first, packed)
        mixture = lay.ring_step(moe.spread(1, [first], None))
    packed = a2a(packed, ALL)
    dots = sum_heads(dots.sum(0))
    if gathered:
        dots, packed, mixture = sync(dots, packed, mixture)

    def through_norm(scaled, pre, n):
        inverse = inv[n][:, None]
        return (inverse * scaled - pre * (inverse * inverse * inverse) * dots[n][:, None]).astype(BF)

    grad_pre = jnp.concatenate(
        [through_norm(scaled_q, query_pre, 0), through_norm(scaled_k, key_pre, 1), grad_value], axis=-1
    )
    grad_qkv = grad_blocks(layers, normed, grad_pre)
    halves = jnp.stack([lay.arrival(), 2 * nc - 1 - lay.arrival()], axis=1).reshape(-1).astype(jnp.int32)
    share = cx % lay.group

    def out_terms(near, far):
        grad_out = contract_rows(attended_b[: seq_rows // 2], near) + contract_rows(attended_b[seq_rows // 2 :], far)
        grad_out = grad_out.astype(BF).reshape(hpd, lay.group, rb, width)
        terms = []
        for k in range(lay.group):
            term = lax.dynamic_index_in_dim(grad_out, share ^ k, 1, keepdims=False)
            terms.append(lay.swap(term, k) if k else term)
        return jnp.stack(terms)

    def out_part(terms, step):
        layer = lay.layer_at(step)
        return terms[(layer // hpd) ^ share, layer % hpd]

    total = grad_qkv[1]
    if not gathered:
        mixture = mixture.astype(BF)
    for n, step in enumerate(list(range(2, nz)) + [0]):
        ready = total
        total = lay.ring_step(total)
        if n == 0:
            near, far = project_back(layers, halves, grad_pre, ring, half, ready)
            total, near, far, branch_near = sync(total, near, far, branch_near)
        elif n == 1:
            far = lay.swap(far, 1)
            if gathered:
                part = moe.exchange(moe.out_sum(2, ready))
                total, far, part = sync(total, far, part)
        elif n == 2:
            terms = out_terms(branch_near, branch_far)
            grad_normed = lay.reduce_chips((near.astype(F32) + far.astype(F32)).astype(BF))
            if gathered:
                mixture = lay.ring_step(moe.spread(2, [part], mixture))
                part = moe.exchange(moe.out_sum(3, ready))
                total, terms, grad_normed, mixture, part = sync(total, terms, grad_normed, mixture, part)
                mixture = lay.ring_step(moe.spread(3, [part], mixture))
                last = moe.send_back(moe.out_sum(0, total))
            out_total = lay.ring_step(out_part(terms, 1))
        total = (total.astype(F32) + grad_qkv[step].astype(F32)).astype(BF)
    grad_qkv = a2a(total.reshape(nc, rb, 3 * cols), "ctx")
    for step in list(range(2, nz)) + [0]:
        out_total = (out_total.astype(F32) + out_part(terms, step).astype(F32)).astype(BF)
        if step:
            out_total = lay.ring_step(out_total)
    grad_out_w = out_total.astype(F32)
    if gathered:
        weight_grads = [moe.grads[n] for n in range(3)]
    if gathered:
        mixture = moe.spread(0, last, mixture)
    grad_down_w, grad_gate_w, grad_up_w = weight_grads
    result = middle + mixture.astype(F32)
    grad_query_w, grad_key_w, grad_value_w, grad_attn_gain = lay.weight_rows(
        grad_qkv, (query_weight, key_weight, value_weight), attn_gain
    )
    grad_attn_gain = grad_attn_gain[0]
    attn_inv = inverse_rms(inputs_f)
    scaled = grad_normed.astype(F32) * attn_gain_f
    grad_inputs = (
        grad_middle
        + attn_inv * scaled
        - inputs_f * (attn_inv * attn_inv * attn_inv) * jnp.mean(scaled * inputs_f, axis=-1, keepdims=True)
    )
    packed = packed.sum(0).reshape(kinds, rb)
    gains = [grad_attn_gain] + [packed[expert_count + k] for k in range(3)]
    return (
        result.astype(BF)[None],
        grad_inputs.astype(BF)[None],
        gains[0],
        grad_query_w,
        grad_key_w,
        grad_value_w,
        gains[1],
        gains[2],
        grad_out_w,
        gains[3],
        packed[:expert_count].T,
        grad_gate_w[None],
        grad_up_w[None],
        grad_down_w[None],
    )


def solution(mesh):
    both = ("dp", "ctx")
    in_specs = (
        P("dp", "ctx", None),
        P("dp", "ctx", None),
        P("dp", "ctx", None),
        P(both),
        P(both, None),
        P(both, None),
        P(both, None),
        P(both),
        P(both),
        P(both, None),
        P(both),
        P(both, None),
        P(both, None, None),
        P(both, None, None),
        P(both, None, None),
    )
    out_specs = (
        P("dp", "ctx", None),
        P("dp", "ctx", None),
        P(both),
        P(both, None),
        P(both, None),
        P(both, None),
        P(both),
        P(both),
        P(both, None),
        P(both),
        P(both, None),
        P(both, None, None),
        P(both, None, None),
        P(both, None, None),
    )
    return jax.shard_map(body, mesh=mesh, in_specs=in_specs, out_specs=out_specs, check_vma=False)
```

```python
import functools
import math

import jax
import jax.numpy as jnp
import numpy as np
from jax import lax
from jax.experimental import pallas as pl
from jax.experimental.pallas import tpu as pltpu
from jax.sharding import PartitionSpec as P

HEADS = 16
HEAD_DIM = 128
TOP = 8

EPSILON = 1e-05
NEG_LARGE = -1e30
NOTES = 128
BF = jnp.bfloat16
F32 = jnp.float32
ALL = ("dp", "ctx")


def dot(left, right):
    return jnp.dot(left, right, preferred_element_type=F32)


def contract_rows(left, right):
    return lax.dot_general(left, right, (((0,), (0,)), ((), ())), preferred_element_type=F32)


def times_transposed(left, right):
    return lax.dot_general(left, right, (((1,), (1,)), ((), ())), preferred_element_type=F32)


def inverse_rms(tensor):
    return lax.rsqrt(jnp.mean(tensor * tensor, axis=-1, keepdims=True) + EPSILON)


def norm_backward(tensor, inverse, gain_vec, grad_in):
    scaled = grad_in * gain_vec
    grad_gain = jnp.sum(grad_in * tensor * inverse, axis=0)
    grad_tensor = inverse * scaled - tensor * (inverse * inverse * inverse) * jnp.mean(
        scaled * tensor, axis=-1, keepdims=True
    )
    return (grad_tensor, grad_gain)


class Layout:
    def __init__(self, rb):
        self.nz = lax.axis_size("dp")
        self.nc = lax.axis_size("ctx")
        self.dz = lax.axis_index("dp")
        self.cx = lax.axis_index("ctx")
        nz, nc = self.nz, self.nc
        order = [0] + list(range(1, nz, 2)) + list(range(nz - 2 + nz % 2, 0, -2))
        self.ring = [(order[i], order[(i + 1) % nz]) for i in range(nz)]
        odd = self.dz % 2 == 1
        self.pos = jnp.where(odd, (self.dz + 1) // 2, jnp.where(self.dz == 0, 0, nz - self.dz // 2))
        self.bits = [1 << b for b in range(1, (nc - 1).bit_length())]
        self.flips = list(range(2, nc, 2))
        self.hpd = HEADS // nc
        self.cols = self.hpd * HEAD_DIM
        self.group = HEAD_DIM // rb
        self.rb = rb

    def swap(self, value, bit):
        return lax.ppermute(value, "ctx", [(i, i ^ bit) for i in range(self.nc)])

    def ring_step(self, value):
        return lax.ppermute(value, "dp", self.ring)

    def layer_at(self, step):
        place = (self.pos - step) % self.nz
        back = jnp.where(place == 0, 0, 2 * (self.nz - place))
        return jnp.where((place > 0) & (place <= self.nz // 2), 2 * place - 1, back)

    def gather_ring(self, block):
        blocks = [block]
        for _ in range(self.nz - 1):
            blocks.append(self.ring_step(blocks[-1]))
        return blocks

    def gather_near(self, value):
        return jnp.concatenate([value] + [self.swap(value, flip) for flip in self.flips], axis=0)

    def gather_ctx(self, value):
        near = self.gather_near(value)
        return (near, self.swap(near, 1))

    def reduce_ctx(self, near, far):
        total = (near.astype(F32) + self.swap(far, 1).astype(F32)).astype(BF)
        return self.reduce_chips(total)

    def reduce_chips(self, total):
        blocks = total.reshape((self.nc // 2, -1) + total.shape[1:])
        half = blocks.shape[1] // 2
        outs = []
        for color in (0, 1):
            part = blocks[:, color * half : (color + 1) * half]
            held = list(range(self.nc // 2))
            for bit in self.bits[::-1] if color == 0 else self.bits:
                keep = np.array([n for n, h in enumerate(held) if not 2 * h & bit])
                send = np.array([n for n, h in enumerate(held) if 2 * h & bit])
                other = self.swap(jnp.stack([part[n] for n in send]), bit)
                part = (jnp.stack([part[n] for n in keep]).astype(F32) + other.astype(F32)).astype(BF)
                held = [held[n] for n in keep]
            outs.append(part[0])
        return jnp.concatenate(outs, axis=0)

    def reduce_ring(self, parts):
        total = parts(1)
        for step in list(range(2, self.nz)) + [0]:
            total = (self.ring_step(total).astype(F32) + parts(step).astype(F32)).astype(BF)
        return total

    def arrival(self):
        flips = np.array([2 * n + core for core in (0, 1) for n in range(self.nc // 2)], np.int32)
        return jnp.asarray(flips) ^ self.cx

    def arrival_place(self):
        flips = jnp.arange(self.nc) ^ self.cx
        return (flips % 2) * (self.nc // 2) + flips // 2

    def head_blocks(self, value):
        rows = value.shape[0]
        split = value.reshape(rows, self.group, self.hpd, self.nc // self.group, HEAD_DIM)
        return split.transpose(3, 1, 0, 2, 4).reshape(self.nc, rows, self.cols)

    def head_rows(self, value):
        rows = value.shape[1]
        split = value.reshape(self.nc // self.group, self.group, rows, self.hpd, HEAD_DIM)
        return split.transpose(2, 1, 3, 0, 4).reshape(rows, self.nc * self.cols)

    def head_at(self, device, n):
        return ((device % self.group) * self.hpd + n) * (self.nc // self.group) + device // self.group

    def weight_rows(self, grads, weights, gain):
        count, rows = len(weights), weights[0].shape[0]
        width = weights[0].shape[1]

        def kernel(gain, grads, *refs):
            sums = 0.0
            gain_col = column(gain[...])
            for device in range(self.nc):
                for w in range(count):
                    for n in range(self.hpd):
                        head = slice(self.head_at(device, n) * HEAD_DIM, (self.head_at(device, n) + 1) * HEAD_DIM)
                        start = w * self.cols + n * HEAD_DIM
                        part = grads[device, :, start : start + HEAD_DIM].astype(F32)
                        refs[count + w][:, head] = part
                        sums += part * refs[w][:, head].astype(F32)
            refs[-1][...] = as_row(jnp.sum(sums, axis=-1, keepdims=True) / gain_col)

        shape = jax.ShapeDtypeStruct((rows, width), F32)
        return pl.pallas_call(
            kernel,
            out_shape=[shape] * count + [jax.ShapeDtypeStruct((1, rows), F32)],
            compiler_params=pltpu.CompilerParams(vmem_limit_bytes=24 * 2**20),
        )(gain.astype(F32)[None], grads, *weights)

    def slot_of(self, layer):
        place = jnp.where(layer % 2 == 1, (layer + 1) // 2, jnp.where(layer == 0, 0, self.nz - layer // 2))
        return (self.pos - place) % self.nz

    def head_weights(self, blocks):
        blocks = jnp.stack(blocks)
        share = self.cx % self.group
        rows = jnp.zeros((self.hpd, self.group) + blocks.shape[1:], blocks.dtype)
        for k in range(self.group):
            other = share ^ k
            part = jnp.stack(
                [
                    lax.dynamic_index_in_dim(blocks, self.slot_of(other * self.hpd + n), 0, keepdims=False)
                    for n in range(self.hpd)
                ]
            )
            part = self.swap(part, k) if k else part
            rows = lax.dynamic_update_slice(rows, part[:, None], (0, other, 0, 0))
        return rows.reshape(self.cols, blocks.shape[-1])

    def own_heads(self, vector):
        return self.head_blocks(vector[None])[self.cx, 0]

    def all_heads(self, vector):
        whole = jnp.zeros((self.nc, 1, self.cols), vector.dtype)
        whole = lax.dynamic_update_slice(whole, vector[None, None], (self.cx, 0, 0))
        return self.head_rows(whole)[0]


def sync(*values):
    return lax.optimization_barrier(values)


def after(value, *deps):
    return lax.optimization_barrier((value,) + deps)[0]


def a2a(value, axes):
    return lax.all_to_all(value, axes, split_axis=0, concat_axis=0, tiled=True)


def column(row):
    return jnp.broadcast_to(row, (row.shape[1], row.shape[1])).T[:, :1]


def as_row(col):
    return jnp.broadcast_to(col, (col.shape[0], col.shape[0])).T[:1]


def lane_pick(notes, *lanes):
    lane = lax.broadcasted_iota(jnp.int32, notes.shape, 1)
    keep = functools.reduce(jnp.logical_or, [lane == n for n in lanes])
    return jnp.sum(jnp.where(keep, notes.astype(F32), 0.0), axis=-1, keepdims=True)


def pick_kernel(capacity, count, expert_ref, block, out):
    rows = block.shape[0]
    width = out.shape[1]
    start = block.shape[1] - NOTES
    before = lax.broadcasted_iota(jnp.int32, (rows, rows), 0) < lax.broadcasted_iota(jnp.int32, (rows, rows), 1)
    before = jnp.where(before, 1.0, 0.0).astype(BF)
    for n in range(count):
        named = lane_pick(block[:, start:], expert_ref[n])
        named = jnp.broadcast_to(named, (rows, rows)).T[:capacity]
        slot = dot(named.astype(BF), before)
        mine = lax.broadcasted_iota(jnp.int32, slot.shape, 0).astype(F32)
        choose = jnp.where((slot == mine) & (named > 0.5), 1.0, 0.0).astype(BF)
        out[n * capacity : (n + 1) * capacity] = dot(choose, block[:, :width]).astype(BF)


def pick_rows(block, experts, capacity, width):
    rows, wide = block.shape
    count = experts.shape[0]
    return pl.pallas_call(
        functools.partial(pick_kernel, capacity, count),
        grid_spec=pltpu.PrefetchScalarGridSpec(
            num_scalar_prefetch=1,
            grid=(1,),
            in_specs=[pl.BlockSpec((rows, wide), lambda n, experts: (0, 0))],
            out_specs=pl.BlockSpec((count * capacity, width), lambda n, experts: (0, 0)),
        ),
        out_shape=jax.ShapeDtypeStruct((count * capacity, width), BF),
        compiler_params=pltpu.CompilerParams(vmem_limit_bytes=24 * 2**20),
        cost_estimate=pl.CostEstimate(
            flops=2 * count * rows * capacity * width, bytes_accessed=4 * count * rows * width, transcendentals=0
        ),
    )(experts, block)


def add_kernel(left, right, *refs):
    refs[-1][...] = (left[...].astype(F32) + right[...].astype(F32)).astype(BF)


def add_rows(left, right, *deps, tile=96):
    rows, width = left.shape
    row = pl.BlockSpec((tile, width), lambda n: (n, 0))
    return pl.pallas_call(
        add_kernel,
        grid=(rows // tile,),
        in_specs=[row, row] + [pl.BlockSpec(memory_space=pl.ANY)] * len(deps),
        out_specs=row,
        out_shape=jax.ShapeDtypeStruct((rows, width), BF),
        compiler_params=pltpu.CompilerParams(vmem_limit_bytes=40 * 2**20),
        cost_estimate=pl.CostEstimate(flops=rows * width, bytes_accessed=6 * rows * width, transcendentals=0),
    )(left, right, *deps)


def spread_kernel(capacity, has_sum, expert_ref, notes, *refs):
    out = refs[-1]
    parts = refs[: -2 if has_sum else -1]
    rows = notes.shape[0]
    after_it = lax.broadcasted_iota(jnp.int32, (rows, rows), 1) < lax.broadcasted_iota(jnp.int32, (rows, rows), 0)
    after_it = jnp.where(after_it, 1.0, 0.0).astype(BF)
    total = refs[-2][...].astype(F32) if has_sum else 0.0
    n = 0
    for part in parts:
        for place in range(0, part.shape[0], capacity):
            named = jnp.broadcast_to(lane_pick(notes[...], expert_ref[n]), (rows, capacity))
            slot = dot(after_it, named.astype(BF))
            mine = lax.broadcasted_iota(jnp.int32, slot.shape, 1).astype(F32)
            choose = jnp.where((slot == mine) & (named > 0.5), 1.0, 0.0).astype(BF)
            total += dot(choose, part[place : place + capacity])
            n += 1
    out[...] = total.astype(BF)


def spread_rows(block, experts, parts, total, capacity):
    rows = block.shape[0]
    width = parts[0].shape[1]
    place = block.shape[1] // NOTES - 1
    row = pl.BlockSpec((rows, width), lambda n, experts: (0, 0))
    return pl.pallas_call(
        functools.partial(spread_kernel, capacity, total is not None),
        grid_spec=pltpu.PrefetchScalarGridSpec(
            num_scalar_prefetch=1,
            grid=(1,),
            in_specs=[pl.BlockSpec((rows, NOTES), lambda n, experts: (0, place))]
            + [pl.BlockSpec(p.shape, lambda n, experts: (0, 0)) for p in parts]
            + ([row] if total is not None else []),
            out_specs=row,
        ),
        out_shape=jax.ShapeDtypeStruct((rows, width), BF),
        compiler_params=pltpu.CompilerParams(vmem_limit_bytes=24 * 2**20),
        cost_estimate=pl.CostEstimate(
            flops=8 * rows * rows * width, bytes_accessed=16 * rows * width, transcendentals=0
        ),
    )(experts, block, *parts, *([total] if total is not None else []))


def expert_kernel(
    kinds, expert_ref, near, far, dy_near, dy_far, gate_w, up_w, down_w, *refs,
):
    sides, mids, outs = refs[-10:-8], refs[-8:-2], refs[-2:]
    tile = near.shape[0]
    width = dy_near.shape[1]
    expert = expert_ref[0]
    rows = jnp.concatenate([near[:, :width], far[:, :width]], axis=0)
    notes = jnp.concatenate([near[:, width:], far[:, width:]], axis=0)
    dy = jnp.concatenate([dy_near[...], dy_far[...]], axis=0)

    def put(pair, start, value):
        pair[0][:, start : start + value.shape[1]] = value[:tile]
        pair[1][:, start : start + value.shape[1]] = value[tile:]

    gate_col = lane_pick(notes, expert + kinds, expert + 2 * kinds)
    gate_pre = dot(rows, gate_w[...])
    up_pre = dot(rows, up_w[...])
    sigmoid_val = jax.nn.sigmoid(gate_pre)
    silu = gate_pre * sigmoid_val
    hidden_f = silu * up_pre
    put(outs, 0, (dot(hidden_f.astype(BF), down_w[...]) * gate_col).astype(BF))
    grad_hidden = times_transposed(dy, down_w[...])
    weighted = jnp.sum(grad_hidden * hidden_f, axis=-1, keepdims=True) * gate_col
    lane = lax.broadcasted_iota(jnp.int32, (2 * tile, NOTES), 1)
    put(sides, width, jnp.where(lane == expert, weighted, 0.0).astype(BF))
    grad_hidden = grad_hidden * gate_col
    grad_gate_pre = (
        grad_hidden * up_pre * (sigmoid_val * (1.0 + gate_pre * (1.0 - sigmoid_val)))
    ).astype(BF)
    grad_up_pre = (grad_hidden * silu).astype(BF)
    for n, mid in enumerate(((hidden_f * gate_col).astype(BF), grad_gate_pre, grad_up_pre)):
        mids[2 * n][...] = mid[:tile]
        mids[2 * n + 1][...] = mid[tile:]
    put(
        sides,
        0,
        (
            times_transposed(grad_gate_pre, gate_w[...]) + times_transposed(grad_up_pre, up_w[...])
        ).astype(BF),
    )


def expert_chunk(kinds, expert, near, far, dy_near, dy_far, gate_w, up_w, down_w, *deps, tile=128):
    rows, width = dy_near.shape
    units = gate_w.shape[1]

    def row(cols):
        return pl.BlockSpec((tile, cols), lambda i, expert: (i, 0))

    def whole(array):
        return pl.BlockSpec(array.shape, lambda i, expert: (0, 0), pipeline_mode=pl.Buffered(1))

    wide = near.shape[1]
    outs = [wide] * 2 + [units] * 6 + [width] * 2
    return pl.pallas_call(
        functools.partial(expert_kernel, kinds),
        grid_spec=pltpu.PrefetchScalarGridSpec(
            num_scalar_prefetch=1,
            grid=(rows // tile,),
            in_specs=[row(wide), row(wide), row(width), row(width), whole(gate_w), whole(up_w), whole(down_w)]
            + [pl.BlockSpec(memory_space=pl.ANY)] * len(deps),
            out_specs=[row(cols) for cols in outs],
        ),
        out_shape=[jax.ShapeDtypeStruct((rows, cols), BF) for cols in outs],
        compiler_params=pltpu.CompilerParams(vmem_limit_bytes=56 * 2**20),
        cost_estimate=pl.CostEstimate(
            flops=24 * rows * width * units,
            bytes_accessed=16 * rows * width,
            transcendentals=2 * rows * units,
        ),
    )(expert, near, far, dy_near, dy_far, gate_w, up_w, down_w, *deps)


def contract_kernel(count, *refs):
    total = 0.0
    for left, right in zip(refs[:count], refs[count : 2 * count]):
        total += contract_rows(left[...], right[...])
    refs[-1][...] = total


def contract_many(lefts, rights, rows, cols, dep, tile=256):
    count = len(lefts)
    depth = lefts[0].shape[0]
    tall = rows >= cols
    strip = pl.BlockSpec((depth, tile), lambda i: (0, i))
    held = pl.BlockSpec((depth, min(rows, cols)), lambda i: (0, 0), pipeline_mode=pl.Buffered(1))
    return pl.pallas_call(
        functools.partial(contract_kernel, count),
        grid=(max(rows, cols) // tile,),
        in_specs=[strip if tall else held] * count
        + [held if tall else strip] * count
        + [pl.BlockSpec(memory_space=pl.ANY)],
        out_specs=pl.BlockSpec((tile, cols), lambda i: (i, 0)) if tall else pl.BlockSpec((rows, tile), lambda i: (0, i)),
        out_shape=jax.ShapeDtypeStruct((rows, cols), F32),
        compiler_params=pltpu.CompilerParams(vmem_limit_bytes=56 * 2**20),
        cost_estimate=pl.CostEstimate(
            flops=2 * depth * count * rows * cols,
            bytes_accessed=2 * depth * count * (rows + cols) + 4 * rows * cols,
            transcendentals=0,
        ),
    )(*lefts, *rights, dep)


def columns(rows):
    count = rows.shape[1] // 128
    return jnp.concatenate([column(rows[:, n * 128 : (n + 1) * 128]) for n in range(count)], axis=0)


def as_rows(cols):
    count = cols.shape[0] // 128
    return jnp.concatenate([as_row(cols[n * 128 : (n + 1) * 128]) for n in range(count)], axis=1)


def norm_kernel(place_ref, near, far, gain, out):
    n = pl.program_id(0)
    steps = pl.num_programs(0)
    rows = jnp.where(place_ref[n] < steps // 2, near[...], far[...]).astype(F32)
    out[...] = (rows * inverse_rms(rows) * gain[...]).astype(BF)


def norm_in_order(place, near, far, gain, half):
    steps = place.shape[0]
    width = near.shape[1]
    return pl.pallas_call(
        norm_kernel,
        grid_spec=pltpu.PrefetchScalarGridSpec(
            num_scalar_prefetch=1,
            grid=(steps,),
            in_specs=[
                pl.BlockSpec((half, width), lambda n, place: (jnp.minimum(place[n], steps // 2 - 1), 0)),
                pl.BlockSpec((half, width), lambda n, place: (jnp.maximum(place[n] - steps // 2, 0), 0)),
                pl.BlockSpec((1, width), lambda n, place: (0, 0)),
            ],
            out_specs=pl.BlockSpec((half, width), lambda n, place: (n, 0)),
        ),
        out_shape=jax.ShapeDtypeStruct((steps * half, width), BF),
        compiler_params=pltpu.CompilerParams(vmem_limit_bytes=16 * 2**20),
        cost_estimate=pl.CostEstimate(
            flops=4 * steps * half * width, bytes_accessed=6 * steps * half * width, transcendentals=0
        ),
    )(place, near, far, gain)


def project_kernel(count, cols, layer_ref, rows, *refs):
    total = 0.0
    for n in range(count):
        depth = refs[n].shape[0]
        start = pl.multiple_of(layer_ref[n] * depth, depth)
        total += dot(rows[:, pl.ds(start, depth)], refs[n][...])
    out, squares = refs[count:]
    out[...] = total
    for n in range(2):
        part = total[:, n * cols : (n + 1) * cols]
        squares[n : n + 1] = as_rows(jnp.sum(part * part, axis=-1, keepdims=True))


def project(layers, rows, weights, cols, tile=256):
    count = len(weights)
    total, width = rows.shape
    wide = weights[0].shape[1]
    held = pl.BlockSpec(weights[0].shape, lambda n, layers: (0, 0), pipeline_mode=pl.Buffered(1))
    return pl.pallas_call(
        functools.partial(project_kernel, count, cols),
        grid_spec=pltpu.PrefetchScalarGridSpec(
            num_scalar_prefetch=1,
            grid=(total // tile,),
            in_specs=[pl.BlockSpec((tile, width), lambda n, layers: (n, 0))] + [held] * count,
            out_specs=[
                pl.BlockSpec((tile, wide), lambda n, layers: (n, 0)),
                pl.BlockSpec((2, tile), lambda n, layers: (0, n)),
            ],
        ),
        out_shape=[jax.ShapeDtypeStruct((total, wide), F32), jax.ShapeDtypeStruct((2, total), F32)],
        compiler_params=pltpu.CompilerParams(vmem_limit_bytes=60 * 2**20),
        cost_estimate=pl.CostEstimate(
            flops=2 * total * width * wide, bytes_accessed=2 * total * width + 6 * total * wide, transcendentals=0
        ),
    )(layers, rows, *weights)


def grad_blocks_kernel(layer_ref, rows, grads, *outs):
    step = pl.program_id(0)
    block = contract_rows(rows[...], grads[...]).astype(BF)
    for n, out in enumerate(outs):

        @pl.when(step == n)
        def _():
            out[...] = block


def grad_blocks(layers, rows, grads):
    total, width = rows.shape
    wide = grads.shape[1]
    count = layers.shape[0]
    depth = width // count
    return pl.pallas_call(
        grad_blocks_kernel,
        grid_spec=pltpu.PrefetchScalarGridSpec(
            num_scalar_prefetch=1,
            grid=(count,),
            in_specs=[
                pl.BlockSpec((total, depth), lambda n, layers: (0, layers[n])),
                pl.BlockSpec((total, wide), lambda n, layers: (0, 0), pipeline_mode=pl.Buffered(1)),
            ],
            out_specs=[pl.BlockSpec((depth, wide), lambda n, layers: (0, 0))] * count,
        ),
        out_shape=[jax.ShapeDtypeStruct((depth, wide), BF)] * count,
        compiler_params=pltpu.CompilerParams(vmem_limit_bytes=48 * 2**20),
        cost_estimate=pl.CostEstimate(
            flops=2 * total * width * wide, bytes_accessed=2 * (total + wide) * width, transcendentals=0
        ),
    )(layers, rows, grads)


def project_back_kernel(count, half, layer_ref, block_ref, grads, *refs):
    near, far = refs[-2:]
    step = pl.program_id(0)
    blocks = near.shape[0] // half
    for side, out in enumerate((near, far)):
        first = (side * pl.num_programs(0) + step) * blocks
        rows = jnp.concatenate(
            [grads[pl.ds(pl.multiple_of(block_ref[first + n] * half, half), half)] for n in range(blocks)], axis=0
        )
        for n in range(count):
            depth = refs[n].shape[0]
            start = pl.multiple_of(layer_ref[n] * depth, depth)
            out[:, pl.ds(start, depth)] = times_transposed(rows, refs[n][...]).astype(BF)


def project_back(layers, blocks, grads, weights, half, dep, tile=256):
    count = len(weights)
    total, wide = grads.shape
    width = count * weights[0].shape[0]
    held = pl.BlockSpec(weights[0].shape, lambda n, *refs: (0, 0), pipeline_mode=pl.Buffered(1))
    out = jax.ShapeDtypeStruct((total // 2, width), BF)
    return pl.pallas_call(
        functools.partial(project_back_kernel, count, half),
        grid_spec=pltpu.PrefetchScalarGridSpec(
            num_scalar_prefetch=2,
            grid=(total // 2 // tile,),
            in_specs=[pl.BlockSpec((total, wide), lambda n, *refs: (0, 0), pipeline_mode=pl.Buffered(1))]
            + [held] * count
            + [pl.BlockSpec(memory_space=pl.ANY)],
            out_specs=[pl.BlockSpec((tile, width), lambda n, *refs: (n, 0))] * 2,
        ),
        out_shape=[out, out],
        compiler_params=pltpu.CompilerParams(vmem_limit_bytes=40 * 2**20),
        cost_estimate=pl.CostEstimate(
            flops=2 * total * width * wide, bytes_accessed=2 * total * (width + wide), transcendentals=0
        ),
    )(layers, blocks, grads, *weights, dep)


def turn(value, cosine, sine):
    return value * cosine + pltpu.roll(value, HEAD_DIM // 2, 1) * sine


def masked_scores(queries, keys, first, score_scale):
    scores = times_transposed(queries, keys) * score_scale
    row = lax.broadcasted_iota(jnp.int32, scores.shape, 0) + first
    col = lax.broadcasted_iota(jnp.int32, scores.shape, 1)
    return scores, col <= row


def attention_kernel(
    half, tile, score_scale, place_ref, q_pre, k_pre, v_pre, inv, gains, cosine, sine,
    sent, attended, lse, query_rot, key_rot, value,
):
    rows = q_pre.shape[0]
    cos, sin = cosine[...], sine[...]
    query_rot[...] = turn(q_pre[...] * columns(inv[0:1]) * gains[0:1], cos, sin).astype(BF)
    key_rot[...] = turn(k_pre[...] * columns(inv[1:2]) * gains[1:2], cos, sin).astype(BF)
    value[...] = v_pre[...].astype(BF)
    for n in range(rows // tile):
        first = n * tile
        end = first + tile
        scores, allowed = masked_scores(query_rot[first:end], key_rot[:end], first, score_scale)
        scores = jnp.where(allowed, scores, NEG_LARGE)
        top = jnp.max(scores, axis=-1, keepdims=True)
        probs = jnp.exp(scores - top)
        total = jnp.sum(probs, axis=-1, keepdims=True)
        lse[first:end] = jnp.broadcast_to(top + jnp.log(total), (tile, HEAD_DIM))
        attended[first:end] = dot((probs / total).astype(BF), value[:end])
    for n in range(rows // half):
        place = pl.multiple_of(place_ref[n] * half, half)
        sent[pl.ds(place, half)] = attended[n * half : (n + 1) * half].astype(BF)


def attention_grad_kernel(
    half, tile, score_scale, place_ref, sent_grad, attended, lse, query_rot, key_rot, value, q_pre, k_pre, inv, gains,
    cosine, sine, scaled_q, scaled_k, grad_value, dots, grad_gains, grad_heads, key_sum, value_sum, query_sum,
):
    rows = q_pre.shape[0]
    for n in range(rows // half):
        place = pl.multiple_of(place_ref[n] * half, half)
        grad_heads[n * half : (n + 1) * half] = sent_grad[pl.ds(place, half)]
    key_sum[...] = jnp.zeros_like(key_sum)
    value_sum[...] = jnp.zeros_like(value_sum)
    for n in range(rows // tile):
        first = n * tile
        end = first + tile
        grads = grad_heads[first:end]
        queries = query_rot[first:end]
        delta = jnp.sum(grads.astype(F32) * attended[first:end], axis=-1, keepdims=True)
        scores, allowed = masked_scores(queries, key_rot[:end], first, score_scale)
        probs = jnp.where(allowed, jnp.exp(scores - lse[first:end][:, :1]), 0.0)
        grad_scores = (probs * (times_transposed(grads, value[:end]) - delta)).astype(BF)
        query_sum[first:end] = dot(grad_scores, key_rot[:end])
        key_sum[:end] += contract_rows(grad_scores, queries)
        value_sum[:end] += contract_rows(probs.astype(BF), grads)
    grad_value[...] = value_sum[...].astype(BF)
    cos, sin = cosine[...], -sine[...]
    for n, (total, pre, scaled) in enumerate(((query_sum, q_pre, scaled_q), (key_sum, k_pre, scaled_k))):
        grad = turn(total[...] * score_scale, cos, sin)
        grad_gains[n : n + 1] = jnp.sum(grad * pre[...] * columns(inv[n : n + 1]), axis=0, keepdims=True)
        grad = grad * gains[n : n + 1]
        scaled[...] = grad
        dots[n : n + 1] = as_rows(jnp.sum(grad * pre[...], axis=-1, keepdims=True))


class Attention:
    def __init__(self, rows, half, hpd):
        self.rows, self.half, self.hpd = rows, half, hpd
        self.tile = min(256, rows)
        position = np.arange(rows, dtype=np.float32)
        freq = np.exp(np.arange(HEAD_DIM // 2, dtype=np.float32) * np.float32(-2.0 * math.log(10000.0) / HEAD_DIM))
        angles = position[:, None] * freq[None, :].astype(np.float32)
        self.cosine = jnp.asarray(np.concatenate([np.cos(angles)] * 2, axis=1), F32)
        self.sine = jnp.asarray(np.concatenate([-np.sin(angles), np.sin(angles)], axis=1), F32)
        self.head = pl.BlockSpec((rows, HEAD_DIM), lambda h, place: (0, h))
        self.keys = pl.BlockSpec((rows, HEAD_DIM), lambda h, place: (0, h + hpd))
        self.values = pl.BlockSpec((rows, HEAD_DIM), lambda h, place: (0, h + 2 * hpd))
        self.stat = pl.BlockSpec((2, rows), lambda h, place: (0, 0))
        self.gain = pl.BlockSpec((2, HEAD_DIM), lambda h, place: (0, h))
        self.table = pl.BlockSpec((rows, HEAD_DIM), lambda h, place: (0, 0))
        self.args = (half, self.tile, 1.0 / math.sqrt(HEAD_DIM))
        self.params = pltpu.CompilerParams(vmem_limit_bytes=60 * 2**20)

    def shape(self, dtype):
        return jax.ShapeDtypeStruct((self.rows, self.hpd * HEAD_DIM), dtype)

    def cost(self, products):
        area = self.hpd * self.rows * self.rows
        return pl.CostEstimate(
            flops=products * area * HEAD_DIM, bytes_accessed=self.hpd * self.rows * HEAD_DIM * 24, transcendentals=area
        )

    def call(self, kernel, ins, outs, shapes, scratch, products):
        return pl.pallas_call(
            functools.partial(kernel, *self.args),
            grid_spec=pltpu.PrefetchScalarGridSpec(
                num_scalar_prefetch=1, grid=(self.hpd,), in_specs=ins, out_specs=outs, scratch_shapes=scratch
            ),
            out_shape=shapes,
            compiler_params=self.params,
            cost_estimate=self.cost(products),
        )

    def forward(self, places, qkv, inv, gains):
        ins = [self.head, self.keys, self.values, self.stat, self.gain, self.table, self.table]
        shapes = [self.shape(t) for t in (BF, F32, F32, BF, BF, BF)]
        run = self.call(attention_kernel, ins, [self.head] * 6, shapes, [], 3)
        return run(places, qkv, qkv, qkv, inv, gains, self.cosine, self.sine)

    def backward(self, places, sent_grad, kept, qkv, inv, gains):
        rows, hpd = self.rows, self.hpd
        line = pl.BlockSpec((None, 2, rows), lambda h, place: (h, 0, 0))
        ins = [self.head] * 6 + [self.head, self.keys, self.stat, self.gain, self.table, self.table]
        shapes = [self.shape(F32), self.shape(F32), self.shape(BF)]
        shapes += [jax.ShapeDtypeStruct((hpd, 2, rows), F32), jax.ShapeDtypeStruct((2, hpd * HEAD_DIM), F32)]
        scratch = [pltpu.VMEM((rows, HEAD_DIM), BF)] + [pltpu.VMEM((rows, HEAD_DIM), F32)] * 3
        run = self.call(attention_grad_kernel, ins, [self.head] * 3 + [line, self.gain], shapes, scratch, 6)
        return run(places, sent_grad, *kept, qkv, qkv, inv, gains, self.cosine, self.sine)


class Gathered:
    def __init__(self, lay, routes, expert_count, capacity, width):
        self.lay, self.kinds, self.capacity, self.width = lay, expert_count, capacity, width
        self.tok_rows = routes.shape[0]
        chosen = routes[:, :, None] == jnp.arange(expert_count, dtype=jnp.int32)
        self.chosen = jnp.any(chosen, axis=1)
        first = lay.dz * (lay.nc // 2)
        flipped = first + (lay.cx ^ jnp.array([0] + lay.flips, jnp.int32)) // 2
        self.flipped = flipped.astype(jnp.int32)
        self.own = self.flipped[:1]
        self.straight = (first + jnp.arange(lay.nc // 2)).astype(jnp.int32)

    def noted(self, rows, *notes):
        notes = [self.chosen.astype(BF)] + list(notes)
        rest = NOTES - self.kinds * len(notes)
        return jnp.concatenate([rows] + notes + [jnp.zeros((self.tok_rows, rest), BF)], axis=1)

    def offer(self, block, width=None):
        return pick_rows(block, self.straight, self.capacity, width or block.shape[1])

    def exchange(self, offered):
        groups = [list(range(core, self.lay.nc, 2)) for core in (0, 1)]
        return lax.all_to_all(
            offered, "ctx", split_axis=0, concat_axis=0, tiled=True, axis_index_groups=groups
        )

    def send_back(self, sums):
        chip = self.lay.cx // 2
        parts = [
            lax.dynamic_slice_in_dim(sums, (chip ^ n) * self.capacity, self.capacity, 0)
            for n in range(self.lay.nc // 2)
        ]
        return [parts[0]] + [self.lay.swap(p, flip) for p, flip in zip(parts[1:], self.lay.flips)]

    def spread(self, step, parts, total):
        experts = self.flipped if len(parts) > 1 else self.straight
        return spread_rows(self.blocks[step], experts, parts, total, self.capacity)

    def straighten(self, parts):
        chip = self.lay.cx // 2
        whole = jnp.zeros((len(parts) * self.capacity, parts[0].shape[1]), parts[0].dtype)
        for n, part in enumerate(parts):
            whole = lax.dynamic_update_slice_in_dim(whole, part, (chip ^ n) * self.capacity, 0)
        return whole

    def run(self, block, dy, dy_last, gate_w, up_w, down_w):
        lay, nz = self.lay, self.lay.nz
        self.blocks = blocks = [block]
        self.rows, self.done, self.dy = rows, done, dy = [], [], dy
        back, far_sums = {}, {}
        near = self.exchange(self.offer(block))
        coming = lay.ring_step(block)
        coming, near = sync(coming, near)
        for step in range(nz):
            far = lay.swap(near, 1)
            rows += [near, far]
            if step:
                far_sums[step - 1] = lay.swap(done[-1][1], 1)
            if step + 1 < nz:
                blocks.append(coming)
                near = self.exchange(self.offer(coming))
                if step + 2 < nz:
                    coming = lay.ring_step(coming)
            if step == 0:
                late = self.send_back(dy_last)
            if step == nz - 2:
                last_dy = self.straighten(late)
                dy.append([last_dy, lay.swap(last_dy, 1)])
            sent, deps = [], []
            if step == nz - 1:
                for n in range(1, nz - 1):
                    deps.append(add_rows(done[n][0], far_sums[n]))
                    back[n] = [self.exchange(deps[-1])] if n == 1 else self.send_back(deps[-1])
                    sent += back[n]
            made = list(
                expert_chunk(self.kinds, self.own, *rows[-2:], *dy[step], gate_w, up_w, down_w, *deps)
            )
            held = [made[1], coming] + ([near] if step + 1 < nz else [])
            held += sent[:1] + (late[1:] if step == 1 else []) + (dy[-1][1:] if step == nz - 2 else [])
            held += [far_sums[0]] if step == nz - 1 else []
            held = list(sync(*held))
            made[1], coming = held[:2]
            if step + 1 < nz:
                near = held[2]
            if step == 1:
                late[1:] = held[3:]
            if step == nz - 2:
                dy[-1][1] = held[3]
            if step == nz - 1:
                back[1], far_sums[0] = held[2:3], held[3]
            done.append(made)
        self.grads = {}
        total = self.spread(1, back[1], None)
        far_sums[nz - 1] = lay.swap(done[-1][1], 1)
        for n, step in enumerate(list(range(2, nz)) + [0]):
            coming = lay.ring_step(total)
            if step not in back:
                sums = add_rows(done[step][0], far_sums[step])
                back[step] = [self.exchange(sums)] if step == nz - 1 else self.send_back(sums)
            beside = list(back[step])
            if n < 3:
                self.grads[n] = self.weight_grads(n, total)
                beside.append(self.grads[n])
            if n == 0:
                beside.append(far_sums[nz - 1])
            coming, *beside = sync(coming, *beside)
            if n == 0:
                far_sums[nz - 1] = beside.pop()
            if n < 3:
                self.grads[n] = beside.pop()
            if step == nz - 1:
                beside[0], far_sums[0] = sync(beside[0], far_sums[0])
            total = self.spread(step, beside, coming)
        return total[:, : self.width].astype(F32), total[:, self.width : self.width + self.kinds].astype(F32)

    def out_sum(self, step, *deps):
        near, far = self.done[step][-2:]
        return add_rows(near, self.lay.swap(far, 1), *deps)

    def weight_grads(self, which, dep):
        near = 2 + 2 * which
        mids = [d[k] for d in self.done for k in (near, near + 1)]
        units = mids[0].shape[1]
        if which == 0:
            return contract_many(mids, [d for pair in self.dy for d in pair], units, self.width, dep)
        return contract_many(self.rows, mids, self.width, units, dep)


def experts_sent(lay, mlp_normed, routes, router_probs, grad_result, gate_w, up_w, down_w):
    tok_rows, width = mlp_normed.shape
    expert_count = router_probs.shape[1]
    capacity = 3 * tok_rows * TOP // (2 * expert_count)
    flat_routes = routes.reshape(tok_rows * TOP)
    onehot = (flat_routes[:, None] == jnp.arange(expert_count, dtype=jnp.int32)[None, :]).astype(
        jnp.int32
    )
    slot_index = jnp.sum((jnp.cumsum(onehot, axis=0) - onehot) * onehot, axis=1)
    chosen = onehot.reshape(tok_rows, TOP, expert_count).astype(F32)
    gate_values = jnp.einsum("tke,te->tk", chosen, router_probs)

    def dispatch(rows_in):
        sent = jnp.zeros((expert_count, capacity, width), BF).at[flat_routes, slot_index].set(rows_in)
        return a2a(jnp.repeat(sent, 2, axis=0), ALL)

    def collect(buffer):
        even_rows = buffer[2 * flat_routes, slot_index].astype(F32)
        odd_rows = buffer[2 * flat_routes + 1, slot_index].astype(F32)
        return (even_rows + odd_rows).reshape(tok_rows, TOP, width)

    received = dispatch(jnp.repeat(mlp_normed, TOP, axis=0))
    flat_in = received.reshape(-1, width)
    gate_pre = dot(flat_in, gate_w)
    up_pre = dot(flat_in, up_w)
    hidden = (jax.nn.silu(gate_pre) * up_pre).astype(BF)
    half_out = dot(hidden, down_w).astype(BF).reshape(received.shape)
    expert_rows = collect(a2a(half_out, ALL))
    mixture = jnp.einsum("tk,tkd->td", gate_values, expert_rows)
    grad_gates = jnp.einsum("td,tkd->tk", grad_result, expert_rows)
    grad_rows = (
        (gate_values[:, :, None] * grad_result[:, None, :])
        .astype(BF)
        .reshape(tok_rows * TOP, width)
    )
    grad_flat = dispatch(grad_rows).reshape(-1, width)
    grad_down_w = contract_rows(hidden, grad_flat)
    grad_hidden = times_transposed(grad_flat, down_w)
    sigmoid_val = jax.nn.sigmoid(gate_pre)
    grad_gate_pre = (
        grad_hidden * up_pre * sigmoid_val * (1.0 + gate_pre * (1.0 - sigmoid_val))
    ).astype(BF)
    grad_up_pre = (grad_hidden * jax.nn.silu(gate_pre)).astype(BF)
    grad_gate_w = contract_rows(flat_in, grad_gate_pre)
    grad_up_w = contract_rows(flat_in, grad_up_pre)
    grad_copy = (
        (times_transposed(grad_gate_pre, gate_w) + times_transposed(grad_up_pre, up_w))
        .astype(BF)
        .reshape(received.shape)
    )
    grad_sum = jnp.sum(collect(a2a(grad_copy, ALL)), axis=1)
    weighted = router_probs * jnp.einsum("tk,tke->te", grad_gates, chosen)
    return (mixture, grad_sum, weighted, (grad_down_w, grad_gate_w, grad_up_w))


def body(
    tokens,
    routes,
    cotangent,
    attn_gain,
    query_weight,
    key_weight,
    value_weight,
    query_gain,
    key_gain,
    out_weight,
    mlp_gain,
    router_weight,
    gate_weight,
    up_weight,
    down_weight,
):
    rb = query_weight.shape[0]
    lay = Layout(rb)
    nz, nc, cx = lay.nz, lay.nc, lay.cx
    tok_rows = tokens.shape[1]
    width = tokens.shape[2]
    half = tok_rows // 2
    seq_rows = tok_rows * nc
    expert_count = router_weight.shape[1]
    hpd, cols = lay.hpd, lay.cols
    devices = nz * nc
    capacity = 3 * tok_rows * TOP // (2 * expert_count)
    gathered = (
        nz > 3
        and devices * tok_rows <= 4 * expert_count * capacity
        and 3 * expert_count <= NOTES
        and capacity % 16 == 0
    )

    sent = jnp.concatenate(
        [lay.head_blocks(w) for w in (query_weight, key_weight, value_weight)], axis=-1
    )
    kinds = expert_count + 4
    small = jnp.concatenate(
        [router_weight] + [g[:, None] for g in (query_gain, key_gain, mlp_gain, attn_gain)], axis=1
    )
    small = jnp.broadcast_to(small.T.reshape(1, kinds * rb), (devices, kinds * rb))
    block = a2a(sent, "ctx").reshape(nc * rb, 3 * cols)
    parts = [tokens[0]] + [lay.swap(tokens[0], flip) for flip in lay.flips]
    places = lay.arrival_place()
    places = jnp.concatenate([places * 2, (places * 2 + 1)[::-1]]).astype(jnp.int32)
    if gathered:
        moe = Gathered(lay, routes[0], expert_count, capacity, width)
        dy_blocks = [moe.noted(cotangent[0])]
        dy_blocks.append(lay.ring_step(dy_blocks[0]))
        offered = moe.offer(dy_blocks[0], width)
    out_blocks = [out_weight, lay.ring_step(out_weight)]
    if gathered:
        block, out_blocks[1], dy_blocks[1], offered, *parts[1:3] = sync(
            block, out_blocks[1], dy_blocks[1], offered, *parts[1:3]
        )
    ring, dy = [block], []
    for step in range(1, nz):
        block = lay.ring_step(block)
        beside = []
        if step == 1:
            beside = [a2a(small, ALL)] + parts[1:]
        elif step == 2:
            seq_near = jnp.concatenate(parts, axis=0)
            beside = [lay.swap(seq_near, 1)]
        elif step == 3:
            beside = [norm_in_order(places, seq_near, seq_far, attn_gain_f[None], half)]
            if nz == 4:
                beside.append(lay.head_weights(out_blocks))
        if gathered and step > 1:
            dy.append([moe.exchange(offered)])
            beside.append(dy[-1][0])
            if step == 2:
                offered = moe.offer(dy_blocks[1], width)
                beside.append(offered)
        if step + 1 < nz:
            beside.append(lay.ring_step(out_blocks[-1]))
        block, out_blocks[-1], *beside = sync(block, out_blocks[-1], *beside)
        if step + 1 < nz:
            out_blocks.append(beside.pop())
        if step == 1:
            small, parts[1:] = beside[0], beside[1:]
            small = small.reshape(devices, kinds, rb).transpose(1, 0, 2).reshape(kinds, width)
            router_t = small[:expert_count]
            qgain_f, kgain_f, mlp_gain_f, attn_gain_f = (small[expert_count + k].astype(F32) for k in range(4))
        elif step == 2:
            seq_far = beside[0]
        elif step == 3:
            normed = beside[0]
            if nz == 4:
                out_rows = beside.pop(1)
        if gathered and step > 1:
            dy[-1][0] = beside[1]
            if step == 2:
                offered = beside[2]
        ring.append(block)
    if nz < 4:
        normed = norm_in_order(places, seq_near, seq_far, attn_gain_f[None], half)
    if nz != 4:
        out_rows = lay.head_weights(out_blocks)
    if gathered:
        dy_blocks.append(lay.ring_step(after(dy_blocks[1], ring[-1])))
    layers = jnp.stack([lay.layer_at(step) for step in range(nz)]).astype(jnp.int32)
    qkv, squares = project(layers, normed, ring, cols)
    query_pre, key_pre = qkv[:, :cols], qkv[:, cols : 2 * cols]

    def sum_heads(stats):
        stats = lax.all_gather(stats.reshape(2 * seq_rows // 128, 128), "ctx", axis=0).sum(0)
        return stats.reshape(2, seq_rows) / width

    inv = lax.rsqrt(sum_heads(squares) + EPSILON)
    own_gains = jnp.stack([lay.own_heads(qgain_f), lay.own_heads(kgain_f)])
    attention = Attention(seq_rows, half, hpd)
    if gathered:
        inv, dy_blocks[2] = sync(inv, dy_blocks[2])
        dy_blocks.append(lay.ring_step(dy_blocks[2]))
        dy.append([moe.exchange(moe.offer(dy_blocks[2], width))])
        for pair in dy[:2]:
            pair.append(lay.swap(pair[0], 1))
    attended_b, *kept = attention.forward(places, qkv, inv, own_gains)
    if gathered:
        attended_b, out_rows, dy_blocks[3], dy[2][0], dy[0][1], dy[1][1] = sync(
            attended_b, out_rows, dy_blocks[3], dy[2][0], dy[0][1], dy[1][1]
        )
    near, far = (dot(attended_b[part], out_rows).astype(BF) for part in (slice(0, seq_rows // 2), slice(seq_rows // 2, None)))
    branch = near.astype(F32) + lay.swap(far, 1).astype(F32)
    if gathered:
        offered = moe.offer(dy_blocks[3], width)
        branch, offered = sync(branch.astype(BF), offered)
        dy[2].append(lay.swap(dy[2][0], 1))
    branch = lay.reduce_chips(branch.astype(BF))
    if gathered:
        branch, dy[2][1], offered = sync(branch, dy[2][1], offered)
    inputs_f = tokens[0].astype(F32)
    middle = inputs_f + branch.astype(F32)
    mlp_inv = inverse_rms(middle)
    mlp_normed = (middle * mlp_inv * mlp_gain_f).astype(BF)
    router_probs = jax.nn.softmax(times_transposed(mlp_normed, router_t), axis=-1)
    grad_result = cotangent[0].astype(F32)
    if gathered:
        combine = jnp.where(moe.chosen, router_probs, 0.0)
        high = combine.astype(BF)
        block = moe.noted(mlp_normed, high, (combine - high.astype(F32)).astype(BF))
        grad_mlp_normed, weighted = moe.run(
            block, dy, offered, gate_weight[0], up_weight[0], down_weight[0]
        )
    else:
        mixture, grad_mlp_normed, weighted, weight_grads = experts_sent(
            lay, mlp_normed, routes[0], router_probs, grad_result, gate_weight[0], up_weight[0], down_weight[0]
        )
    grad_logits = (weighted - router_probs * jnp.sum(weighted, axis=-1, keepdims=True)).astype(BF)
    grad_router_t = contract_rows(grad_logits, mlp_normed)
    grad_mlp_normed = grad_mlp_normed + dot(grad_logits, router_t)
    grad_middle_norm, grad_mlp_gain = norm_backward(middle, mlp_inv, mlp_gain_f, grad_mlp_normed)
    grad_middle = grad_result + grad_middle_norm
    grad_branch = grad_middle.astype(BF)
    branch_near = lay.gather_near(grad_branch)
    if gathered:
        branch_near, first, *out_sums = sync(branch_near, *(moe.out_sum(n) for n in (1, 2, 3, 0)))
        first, second = moe.exchange(first), moe.send_back(out_sums.pop(0))
    branch_far = lay.swap(branch_near, 1)
    grad_heads = jnp.concatenate(
        [times_transposed(part, out_rows).astype(BF) for part in (branch_near, branch_far)], axis=0
    )
    scaled_q, scaled_k, grad_value, dots, grad_gains = attention.backward(places, grad_heads, kept, qkv, inv, own_gains)
    packed = jnp.concatenate(
        [grad_router_t]
        + [g[None] for g in (lay.all_heads(grad_gains[0]), lay.all_heads(grad_gains[1]), grad_mlp_gain)],
        axis=0,
    )
    kinds = expert_count + 3
    packed = packed.reshape(kinds, devices, rb).transpose(1, 0, 2).reshape(devices, kinds * rb)
    if gathered:
        dots, first, packed = sync(dots, first, packed)
        mixture = lay.ring_step(moe.spread(1, [first], None))
    packed = a2a(packed, ALL)
    dots = sum_heads(dots.sum(0))
    if gathered:
        dots, packed, mixture = sync(dots, packed, mixture)

    def through_norm(scaled, pre, n):
        inverse = inv[n][:, None]
        return (inverse * scaled - pre * (inverse * inverse * inverse) * dots[n][:, None]).astype(BF)

    grad_pre = jnp.concatenate(
        [through_norm(scaled_q, query_pre, 0), through_norm(scaled_k, key_pre, 1), grad_value], axis=-1
    )
    grad_qkv = grad_blocks(layers, normed, grad_pre)
    halves = jnp.stack([lay.arrival(), 2 * nc - 1 - lay.arrival()], axis=1).reshape(-1).astype(jnp.int32)
    share = cx % lay.group

    def out_terms(near, far):
        grad_out = contract_rows(attended_b[: seq_rows // 2], near) + contract_rows(attended_b[seq_rows // 2 :], far)
        grad_out = grad_out.astype(BF).reshape(hpd, lay.group, rb, width)
        terms = []
        for k in range(lay.group):
            term = lax.dynamic_index_in_dim(grad_out, share ^ k, 1, keepdims=False)
            terms.append(lay.swap(term, k) if k else term)
        return jnp.stack(terms)

    def out_part(terms, step):
        layer = lay.layer_at(step)
        return terms[(layer // hpd) ^ share, layer % hpd]

    total = grad_qkv[1]
    if not gathered:
        mixture = mixture.astype(BF)
    for n, step in enumerate(list(range(2, nz)) + [0]):
        ready = total
        total = lay.ring_step(total)
        if n == 0:
            near, far = project_back(layers, halves, grad_pre, ring, half, ready)
            beside = second + out_sums if gathered else []
            total, near, far, branch_near, *beside = sync(total, near, far, branch_near, *beside)
        elif n == 1:
            terms = out_terms(branch_near, branch_far)
            grad_normed = lay.reduce_ctx(near, far)
            if gathered:
                mixture = lay.ring_step(moe.spread(2, beside[:-2], mixture))
                part = moe.exchange(beside[-2])
                beside = [mixture, part, beside[-1]]
            total, terms, grad_normed, *beside = sync(total, terms, grad_normed, *beside)
        elif n == 2:
            out_total = lay.ring_step(out_part(terms, 1))
            if gathered:
                mixture, part, last = beside
                mixture = moe.spread(3, [part], mixture)
                last = moe.exchange(last)
                total, out_total, mixture, last = sync(total, out_total, mixture, last)
                mixture = lay.ring_step(mixture)
        total = (total.astype(F32) + grad_qkv[step].astype(F32)).astype(BF)
        if n == 0:
            total, near, far, branch_near, *beside = sync(total, near, far, branch_near, *beside)
        elif n == 1:
            total, terms, *beside = sync(total, terms, *beside)
    grad_qkv = a2a(total.reshape(nc, rb, 3 * cols), "ctx")
    for step in list(range(2, nz)) + [0]:
        out_total = (out_total.astype(F32) + out_part(terms, step).astype(F32)).astype(BF)
        if step:
            out_total = lay.ring_step(out_total)
    grad_out_w = out_total.astype(F32)
    if gathered:
        weight_grads = [moe.grads[n] for n in range(3)]
    if gathered:
        mixture = moe.spread(0, [last], mixture)
    grad_down_w, grad_gate_w, grad_up_w = weight_grads
    result = middle + mixture.astype(F32)
    grad_query_w, grad_key_w, grad_value_w, grad_attn_gain = lay.weight_rows(
        grad_qkv, (query_weight, key_weight, value_weight), attn_gain
    )
    grad_attn_gain = grad_attn_gain[0]
    attn_inv = inverse_rms(inputs_f)
    scaled = grad_normed.astype(F32) * attn_gain_f
    grad_inputs = (
        grad_middle
        + attn_inv * scaled
        - inputs_f * (attn_inv * attn_inv * attn_inv) * jnp.mean(scaled * inputs_f, axis=-1, keepdims=True)
    )
    packed = packed.sum(0).reshape(kinds, rb)
    gains = [grad_attn_gain] + [packed[expert_count + k] for k in range(3)]
    return (
        result.astype(BF)[None],
        grad_inputs.astype(BF)[None],
        gains[0],
        grad_query_w,
        grad_key_w,
        grad_value_w,
        gains[1],
        gains[2],
        grad_out_w,
        gains[3],
        packed[:expert_count].T,
        grad_gate_w[None],
        grad_up_w[None],
        grad_down_w[None],
    )


def solution(mesh):
    both = ("dp", "ctx")
    in_specs = (
        P("dp", "ctx", None),
        P("dp", "ctx", None),
        P("dp", "ctx", None),
        P(both),
        P(both, None),
        P(both, None),
        P(both, None),
        P(both),
        P(both),
        P(both, None),
        P(both),
        P(both, None),
        P(both, None, None),
        P(both, None, None),
        P(both, None, None),
    )
    out_specs = (
        P("dp", "ctx", None),
        P("dp", "ctx", None),
        P(both),
        P(both, None),
        P(both, None),
        P(both, None),
        P(both),
        P(both),
        P(both, None),
        P(both),
        P(both, None),
        P(both, None, None),
        P(both, None, None),
        P(both, None, None),
    )
    return jax.shard_map(body, mesh=mesh, in_specs=in_specs, out_specs=out_specs, check_vma=False)
```

```python
import functools
import math

import jax
import jax.numpy as jnp
import numpy as np
from jax import lax
from jax.experimental import pallas as pl
from jax.experimental.pallas import tpu as pltpu
from jax.sharding import PartitionSpec as P

HEADS = 16
HEAD_DIM = 128
TOP = 8

EPSILON = 1e-05
NEG_LARGE = -1e30
NOTES = 128
BF = jnp.bfloat16
F32 = jnp.float32
ALL = ("dp", "ctx")


def dot(left, right):
    return jnp.dot(left, right, preferred_element_type=F32)


def contract_rows(left, right):
    return lax.dot_general(left, right, (((0,), (0,)), ((), ())), preferred_element_type=F32)


def times_transposed(left, right):
    return lax.dot_general(left, right, (((1,), (1,)), ((), ())), preferred_element_type=F32)


def inverse_rms(tensor):
    return lax.rsqrt(jnp.mean(tensor * tensor, axis=-1, keepdims=True) + EPSILON)


def norm_backward(tensor, inverse, gain_vec, grad_in):
    scaled = grad_in * gain_vec
    grad_gain = jnp.sum(grad_in * tensor * inverse, axis=0)
    grad_tensor = inverse * scaled - tensor * (inverse * inverse * inverse) * jnp.mean(
        scaled * tensor, axis=-1, keepdims=True
    )
    return (grad_tensor, grad_gain)


class Layout:
    def __init__(self, rb):
        self.nz = lax.axis_size("dp")
        self.nc = lax.axis_size("ctx")
        self.dz = lax.axis_index("dp")
        self.cx = lax.axis_index("ctx")
        nz, nc = self.nz, self.nc
        order = [0] + list(range(1, nz, 2)) + list(range(nz - 2 + nz % 2, 0, -2))
        self.ring = [(order[i], order[(i + 1) % nz]) for i in range(nz)]
        odd = self.dz % 2 == 1
        self.pos = jnp.where(odd, (self.dz + 1) // 2, jnp.where(self.dz == 0, 0, nz - self.dz // 2))
        self.bits = [1 << b for b in range(1, (nc - 1).bit_length())]
        self.flips = list(range(2, nc, 2))
        self.hpd = HEADS // nc
        self.cols = self.hpd * HEAD_DIM
        self.group = HEAD_DIM // rb
        self.rb = rb

    def swap(self, value, bit):
        return lax.ppermute(value, "ctx", [(i, i ^ bit) for i in range(self.nc)])

    def ring_step(self, value):
        return lax.ppermute(value, "dp", self.ring)

    def layer_at(self, step):
        place = (self.pos - step) % self.nz
        back = jnp.where(place == 0, 0, 2 * (self.nz - place))
        return jnp.where((place > 0) & (place <= self.nz // 2), 2 * place - 1, back)

    def gather_ring(self, block):
        blocks = [block]
        for _ in range(self.nz - 1):
            blocks.append(self.ring_step(blocks[-1]))
        return blocks

    def gather_near(self, value):
        return jnp.concatenate([value] + [self.swap(value, flip) for flip in self.flips], axis=0)

    def gather_ctx(self, value):
        near = self.gather_near(value)
        return (near, self.swap(near, 1))

    def reduce_ctx(self, near, far):
        total = (near.astype(F32) + self.swap(far, 1).astype(F32)).astype(BF)
        return self.reduce_chips(total)

    def reduce_chips(self, total):
        blocks = total.reshape((self.nc // 2, -1) + total.shape[1:])
        half = blocks.shape[1] // 2
        outs = []
        for color in (0, 1):
            part = blocks[:, color * half : (color + 1) * half]
            held = list(range(self.nc // 2))
            for bit in self.bits[::-1] if color == 0 else self.bits:
                keep = np.array([n for n, h in enumerate(held) if not 2 * h & bit])
                send = np.array([n for n, h in enumerate(held) if 2 * h & bit])
                other = self.swap(jnp.stack([part[n] for n in send]), bit)
                part = (jnp.stack([part[n] for n in keep]).astype(F32) + other.astype(F32)).astype(BF)
                held = [held[n] for n in keep]
            outs.append(part[0])
        return jnp.concatenate(outs, axis=0)

    def reduce_ring(self, parts):
        total = parts(1)
        for step in list(range(2, self.nz)) + [0]:
            total = (self.ring_step(total).astype(F32) + parts(step).astype(F32)).astype(BF)
        return total

    def arrival(self):
        flips = np.array([2 * n + core for core in (0, 1) for n in range(self.nc // 2)], np.int32)
        return jnp.asarray(flips) ^ self.cx

    def arrival_place(self):
        flips = jnp.arange(self.nc) ^ self.cx
        return (flips % 2) * (self.nc // 2) + flips // 2

    def head_blocks(self, value):
        rows = value.shape[0]
        split = value.reshape(rows, self.group, self.hpd, self.nc // self.group, HEAD_DIM)
        return split.transpose(3, 1, 0, 2, 4).reshape(self.nc, rows, self.cols)

    def head_rows(self, value):
        rows = value.shape[1]
        split = value.reshape(self.nc // self.group, self.group, rows, self.hpd, HEAD_DIM)
        return split.transpose(2, 1, 3, 0, 4).reshape(rows, self.nc * self.cols)

    def head_at(self, device, n):
        return ((device % self.group) * self.hpd + n) * (self.nc // self.group) + device // self.group

    def weight_rows(self, grads, weights, gain):
        count, rows = len(weights), weights[0].shape[0]
        width = weights[0].shape[1]

        def kernel(gain, grads, *refs):
            sums = 0.0
            gain_col = column(gain[...])
            for device in range(self.nc):
                for w in range(count):
                    for n in range(self.hpd):
                        head = slice(self.head_at(device, n) * HEAD_DIM, (self.head_at(device, n) + 1) * HEAD_DIM)
                        start = w * self.cols + n * HEAD_DIM
                        part = grads[device, :, start : start + HEAD_DIM].astype(F32)
                        refs[count + w][:, head] = part
                        sums += part * refs[w][:, head].astype(F32)
            refs[-1][...] = as_row(jnp.sum(sums, axis=-1, keepdims=True) / gain_col)

        shape = jax.ShapeDtypeStruct((rows, width), F32)
        return pl.pallas_call(
            kernel,
            out_shape=[shape] * count + [jax.ShapeDtypeStruct((1, rows), F32)],
            compiler_params=pltpu.CompilerParams(vmem_limit_bytes=24 * 2**20),
        )(gain.astype(F32)[None], grads, *weights)

    def slot_of(self, layer):
        place = jnp.where(layer % 2 == 1, (layer + 1) // 2, jnp.where(layer == 0, 0, self.nz - layer // 2))
        return (self.pos - place) % self.nz

    def head_weights(self, blocks):
        blocks = jnp.stack(blocks)
        share = self.cx % self.group
        rows = jnp.zeros((self.hpd, self.group) + blocks.shape[1:], blocks.dtype)
        for k in range(self.group):
            other = share ^ k
            part = jnp.stack(
                [
                    lax.dynamic_index_in_dim(blocks, self.slot_of(other * self.hpd + n), 0, keepdims=False)
                    for n in range(self.hpd)
                ]
            )
            part = self.swap(part, k) if k else part
            rows = lax.dynamic_update_slice(rows, part[:, None], (0, other, 0, 0))
        return rows.reshape(self.cols, blocks.shape[-1])

    def own_heads(self, vector):
        return self.head_blocks(vector[None])[self.cx, 0]

    def all_heads(self, vector):
        whole = jnp.zeros((self.nc, 1, self.cols), vector.dtype)
        whole = lax.dynamic_update_slice(whole, vector[None, None], (self.cx, 0, 0))
        return self.head_rows(whole)[0]


def sync(*values):
    return lax.optimization_barrier(values)


def after(value, *deps):
    return lax.optimization_barrier((value,) + deps)[0]


def a2a(value, axes):
    return lax.all_to_all(value, axes, split_axis=0, concat_axis=0, tiled=True)


def column(row):
    return jnp.broadcast_to(row, (row.shape[1], row.shape[1])).T[:, :1]


def as_row(col):
    return jnp.broadcast_to(col, (col.shape[0], col.shape[0])).T[:1]


def lane_pick(notes, *lanes):
    lane = lax.broadcasted_iota(jnp.int32, notes.shape, 1)
    keep = functools.reduce(jnp.logical_or, [lane == n for n in lanes])
    return jnp.sum(jnp.where(keep, notes.astype(F32), 0.0), axis=-1, keepdims=True)


def pick_kernel(capacity, count, expert_ref, block, out):
    rows = block.shape[0]
    width = out.shape[1]
    start = block.shape[1] - NOTES
    before = lax.broadcasted_iota(jnp.int32, (rows, rows), 0) < lax.broadcasted_iota(jnp.int32, (rows, rows), 1)
    before = jnp.where(before, 1.0, 0.0).astype(BF)
    for n in range(count):
        named = lane_pick(block[:, start:], expert_ref[n])
        named = jnp.broadcast_to(named, (rows, rows)).T[:capacity]
        slot = dot(named.astype(BF), before)
        mine = lax.broadcasted_iota(jnp.int32, slot.shape, 0).astype(F32)
        choose = jnp.where((slot == mine) & (named > 0.5), 1.0, 0.0).astype(BF)
        out[n * capacity : (n + 1) * capacity] = dot(choose, block[:, :width]).astype(BF)


def pick_rows(block, experts, capacity, width):
    rows, wide = block.shape
    count = experts.shape[0]
    return pl.pallas_call(
        functools.partial(pick_kernel, capacity, count),
        grid_spec=pltpu.PrefetchScalarGridSpec(
            num_scalar_prefetch=1,
            grid=(1,),
            in_specs=[pl.BlockSpec((rows, wide), lambda n, experts: (0, 0))],
            out_specs=pl.BlockSpec((count * capacity, width), lambda n, experts: (0, 0)),
        ),
        out_shape=jax.ShapeDtypeStruct((count * capacity, width), BF),
        compiler_params=pltpu.CompilerParams(vmem_limit_bytes=24 * 2**20),
        cost_estimate=pl.CostEstimate(
            flops=2 * count * rows * capacity * width, bytes_accessed=4 * count * rows * width, transcendentals=0
        ),
    )(experts, block)


def add_kernel(left, right, *refs):
    refs[-1][...] = (left[...].astype(F32) + right[...].astype(F32)).astype(BF)


def add_rows(left, right, *deps, tile=96):
    rows, width = left.shape
    row = pl.BlockSpec((tile, width), lambda n: (n, 0))
    return pl.pallas_call(
        add_kernel,
        grid=(rows // tile,),
        in_specs=[row, row] + [pl.BlockSpec(memory_space=pl.ANY)] * len(deps),
        out_specs=row,
        out_shape=jax.ShapeDtypeStruct((rows, width), BF),
        compiler_params=pltpu.CompilerParams(vmem_limit_bytes=40 * 2**20),
        cost_estimate=pl.CostEstimate(flops=rows * width, bytes_accessed=6 * rows * width, transcendentals=0),
    )(left, right, *deps)


def spread_kernel(capacity, has_sum, expert_ref, notes, *refs):
    out = refs[-1]
    parts = refs[: -2 if has_sum else -1]
    rows = notes.shape[0]
    after_it = lax.broadcasted_iota(jnp.int32, (rows, rows), 1) < lax.broadcasted_iota(jnp.int32, (rows, rows), 0)
    after_it = jnp.where(after_it, 1.0, 0.0).astype(BF)
    total = refs[-2][...].astype(F32) if has_sum else 0.0
    n = 0
    for part in parts:
        for place in range(0, part.shape[0], capacity):
            named = jnp.broadcast_to(lane_pick(notes[...], expert_ref[n]), (rows, capacity))
            slot = dot(after_it, named.astype(BF))
            mine = lax.broadcasted_iota(jnp.int32, slot.shape, 1).astype(F32)
            choose = jnp.where((slot == mine) & (named > 0.5), 1.0, 0.0).astype(BF)
            total += dot(choose, part[place : place + capacity])
            n += 1
    out[...] = total.astype(BF)


def spread_rows(block, experts, parts, total, capacity):
    rows = block.shape[0]
    width = parts[0].shape[1]
    place = block.shape[1] // NOTES - 1
    row = pl.BlockSpec((rows, width), lambda n, experts: (0, 0))
    return pl.pallas_call(
        functools.partial(spread_kernel, capacity, total is not None),
        grid_spec=pltpu.PrefetchScalarGridSpec(
            num_scalar_prefetch=1,
            grid=(1,),
            in_specs=[pl.BlockSpec((rows, NOTES), lambda n, experts: (0, place))]
            + [pl.BlockSpec(p.shape, lambda n, experts: (0, 0)) for p in parts]
            + ([row] if total is not None else []),
            out_specs=row,
        ),
        out_shape=jax.ShapeDtypeStruct((rows, width), BF),
        compiler_params=pltpu.CompilerParams(vmem_limit_bytes=24 * 2**20),
        cost_estimate=pl.CostEstimate(
            flops=8 * rows * rows * width, bytes_accessed=16 * rows * width, transcendentals=0
        ),
    )(experts, block, *parts, *([total] if total is not None else []))


def expert_kernel(
    kinds, expert_ref, near, far, dy_near, dy_far, gate_w, up_w, down_w, *refs,
):
    sides, mids, outs = refs[-10:-8], refs[-8:-2], refs[-2:]
    tile = near.shape[0]
    width = dy_near.shape[1]
    expert = expert_ref[0]
    rows = jnp.concatenate([near[:, :width], far[:, :width]], axis=0)
    notes = jnp.concatenate([near[:, width:], far[:, width:]], axis=0)
    dy = jnp.concatenate([dy_near[...], dy_far[...]], axis=0)

    def put(pair, start, value):
        pair[0][:, start : start + value.shape[1]] = value[:tile]
        pair[1][:, start : start + value.shape[1]] = value[tile:]

    gate_col = lane_pick(notes, expert + kinds, expert + 2 * kinds)
    gate_pre = dot(rows, gate_w[...])
    up_pre = dot(rows, up_w[...])
    sigmoid_val = jax.nn.sigmoid(gate_pre)
    silu = gate_pre * sigmoid_val
    hidden_f = silu * up_pre
    put(outs, 0, (dot(hidden_f.astype(BF), down_w[...]) * gate_col).astype(BF))
    grad_hidden = times_transposed(dy, down_w[...])
    weighted = jnp.sum(grad_hidden * hidden_f, axis=-1, keepdims=True) * gate_col
    lane = lax.broadcasted_iota(jnp.int32, (2 * tile, NOTES), 1)
    put(sides, width, jnp.where(lane == expert, weighted, 0.0).astype(BF))
    grad_hidden = grad_hidden * gate_col
    grad_gate_pre = (
        grad_hidden * up_pre * (sigmoid_val * (1.0 + gate_pre * (1.0 - sigmoid_val)))
    ).astype(BF)
    grad_up_pre = (grad_hidden * silu).astype(BF)
    for n, mid in enumerate(((hidden_f * gate_col).astype(BF), grad_gate_pre, grad_up_pre)):
        mids[2 * n][...] = mid[:tile]
        mids[2 * n + 1][...] = mid[tile:]
    put(
        sides,
        0,
        (
            times_transposed(grad_gate_pre, gate_w[...]) + times_transposed(grad_up_pre, up_w[...])
        ).astype(BF),
    )


def expert_chunk(kinds, expert, near, far, dy_near, dy_far, gate_w, up_w, down_w, *deps, tile=128):
    rows, width = dy_near.shape
    units = gate_w.shape[1]

    def row(cols):
        return pl.BlockSpec((tile, cols), lambda i, expert: (i, 0))

    def whole(array):
        return pl.BlockSpec(array.shape, lambda i, expert: (0, 0), pipeline_mode=pl.Buffered(1))

    wide = near.shape[1]
    outs = [wide] * 2 + [units] * 6 + [width] * 2
    return pl.pallas_call(
        functools.partial(expert_kernel, kinds),
        grid_spec=pltpu.PrefetchScalarGridSpec(
            num_scalar_prefetch=1,
            grid=(rows // tile,),
            in_specs=[row(wide), row(wide), row(width), row(width), whole(gate_w), whole(up_w), whole(down_w)]
            + [pl.BlockSpec(memory_space=pl.ANY)] * len(deps),
            out_specs=[row(cols) for cols in outs],
        ),
        out_shape=[jax.ShapeDtypeStruct((rows, cols), BF) for cols in outs],
        compiler_params=pltpu.CompilerParams(vmem_limit_bytes=56 * 2**20),
        cost_estimate=pl.CostEstimate(
            flops=24 * rows * width * units,
            bytes_accessed=16 * rows * width,
            transcendentals=2 * rows * units,
        ),
    )(expert, near, far, dy_near, dy_far, gate_w, up_w, down_w, *deps)


def contract_kernel(count, *refs):
    total = 0.0
    for left, right in zip(refs[:count], refs[count : 2 * count]):
        total += contract_rows(left[...], right[...])
    refs[-1][...] = total


def contract_many(lefts, rights, rows, cols, dep, tile=256):
    count = len(lefts)
    depth = lefts[0].shape[0]
    tall = rows >= cols
    strip = pl.BlockSpec((depth, tile), lambda i: (0, i))
    held = pl.BlockSpec((depth, min(rows, cols)), lambda i: (0, 0), pipeline_mode=pl.Buffered(1))
    return pl.pallas_call(
        functools.partial(contract_kernel, count),
        grid=(max(rows, cols) // tile,),
        in_specs=[strip if tall else held] * count
        + [held if tall else strip] * count
        + [pl.BlockSpec(memory_space=pl.ANY)],
        out_specs=pl.BlockSpec((tile, cols), lambda i: (i, 0)) if tall else pl.BlockSpec((rows, tile), lambda i: (0, i)),
        out_shape=jax.ShapeDtypeStruct((rows, cols), F32),
        compiler_params=pltpu.CompilerParams(vmem_limit_bytes=56 * 2**20),
        cost_estimate=pl.CostEstimate(
            flops=2 * depth * count * rows * cols,
            bytes_accessed=2 * depth * count * (rows + cols) + 4 * rows * cols,
            transcendentals=0,
        ),
    )(*lefts, *rights, dep)


def columns(rows):
    count = rows.shape[1] // 128
    return jnp.concatenate([column(rows[:, n * 128 : (n + 1) * 128]) for n in range(count)], axis=0)


def as_rows(cols):
    count = cols.shape[0] // 128
    return jnp.concatenate([as_row(cols[n * 128 : (n + 1) * 128]) for n in range(count)], axis=1)


def norm_kernel(place_ref, near, far, gain, out):
    n = pl.program_id(0)
    steps = pl.num_programs(0)
    rows = jnp.where(place_ref[n] < steps // 2, near[...], far[...]).astype(F32)
    out[...] = (rows * inverse_rms(rows) * gain[...]).astype(BF)


def norm_in_order(place, near, far, gain, half):
    steps = place.shape[0]
    width = near.shape[1]
    return pl.pallas_call(
        norm_kernel,
        grid_spec=pltpu.PrefetchScalarGridSpec(
            num_scalar_prefetch=1,
            grid=(steps,),
            in_specs=[
                pl.BlockSpec((half, width), lambda n, place: (jnp.minimum(place[n], steps // 2 - 1), 0)),
                pl.BlockSpec((half, width), lambda n, place: (jnp.maximum(place[n] - steps // 2, 0), 0)),
                pl.BlockSpec((1, width), lambda n, place: (0, 0)),
            ],
            out_specs=pl.BlockSpec((half, width), lambda n, place: (n, 0)),
        ),
        out_shape=jax.ShapeDtypeStruct((steps * half, width), BF),
        compiler_params=pltpu.CompilerParams(vmem_limit_bytes=16 * 2**20),
        cost_estimate=pl.CostEstimate(
            flops=4 * steps * half * width, bytes_accessed=6 * steps * half * width, transcendentals=0
        ),
    )(place, near, far, gain)


def project_kernel(count, cols, layer_ref, rows, *refs):
    total = 0.0
    for n in range(count):
        depth = refs[n].shape[0]
        start = pl.multiple_of(layer_ref[n] * depth, depth)
        total += dot(rows[:, pl.ds(start, depth)], refs[n][...])
    out, squares = refs[count:]
    out[...] = total
    for n in range(2):
        part = total[:, n * cols : (n + 1) * cols]
        squares[n : n + 1] = as_rows(jnp.sum(part * part, axis=-1, keepdims=True))


def project(layers, rows, weights, cols, tile=256):
    count = len(weights)
    total, width = rows.shape
    wide = weights[0].shape[1]
    held = pl.BlockSpec(weights[0].shape, lambda n, layers: (0, 0), pipeline_mode=pl.Buffered(1))
    return pl.pallas_call(
        functools.partial(project_kernel, count, cols),
        grid_spec=pltpu.PrefetchScalarGridSpec(
            num_scalar_prefetch=1,
            grid=(total // tile,),
            in_specs=[pl.BlockSpec((tile, width), lambda n, layers: (n, 0))] + [held] * count,
            out_specs=[
                pl.BlockSpec((tile, wide), lambda n, layers: (n, 0)),
                pl.BlockSpec((2, tile), lambda n, layers: (0, n)),
            ],
        ),
        out_shape=[jax.ShapeDtypeStruct((total, wide), F32), jax.ShapeDtypeStruct((2, total), F32)],
        compiler_params=pltpu.CompilerParams(vmem_limit_bytes=60 * 2**20),
        cost_estimate=pl.CostEstimate(
            flops=2 * total * width * wide, bytes_accessed=2 * total * width + 6 * total * wide, transcendentals=0
        ),
    )(layers, rows, *weights)


def grad_blocks_kernel(layer_ref, rows, grads, *outs):
    step = pl.program_id(0)
    block = contract_rows(rows[...], grads[...]).astype(BF)
    for n, out in enumerate(outs):

        @pl.when(step == n)
        def _():
            out[...] = block


def grad_blocks(layers, rows, grads):
    total, width = rows.shape
    wide = grads.shape[1]
    count = layers.shape[0]
    depth = width // count
    return pl.pallas_call(
        grad_blocks_kernel,
        grid_spec=pltpu.PrefetchScalarGridSpec(
            num_scalar_prefetch=1,
            grid=(count,),
            in_specs=[
                pl.BlockSpec((total, depth), lambda n, layers: (0, layers[n])),
                pl.BlockSpec((total, wide), lambda n, layers: (0, 0), pipeline_mode=pl.Buffered(1)),
            ],
            out_specs=[pl.BlockSpec((depth, wide), lambda n, layers: (0, 0))] * count,
        ),
        out_shape=[jax.ShapeDtypeStruct((depth, wide), BF)] * count,
        compiler_params=pltpu.CompilerParams(vmem_limit_bytes=48 * 2**20),
        cost_estimate=pl.CostEstimate(
            flops=2 * total * width * wide, bytes_accessed=2 * (total + wide) * width, transcendentals=0
        ),
    )(layers, rows, grads)


def project_back_kernel(count, half, layer_ref, block_ref, grads, *refs):
    near, far = refs[-2:]
    step = pl.program_id(0)
    blocks = near.shape[0] // half
    for side, out in enumerate((near, far)):
        first = (side * pl.num_programs(0) + step) * blocks
        rows = jnp.concatenate(
            [grads[pl.ds(pl.multiple_of(block_ref[first + n] * half, half), half)] for n in range(blocks)], axis=0
        )
        for n in range(count):
            depth = refs[n].shape[0]
            start = pl.multiple_of(layer_ref[n] * depth, depth)
            out[:, pl.ds(start, depth)] = times_transposed(rows, refs[n][...]).astype(BF)


def project_back(layers, blocks, grads, weights, half, dep, tile=256):
    count = len(weights)
    total, wide = grads.shape
    width = count * weights[0].shape[0]
    held = pl.BlockSpec(weights[0].shape, lambda n, *refs: (0, 0), pipeline_mode=pl.Buffered(1))
    out = jax.ShapeDtypeStruct((total // 2, width), BF)
    return pl.pallas_call(
        functools.partial(project_back_kernel, count, half),
        grid_spec=pltpu.PrefetchScalarGridSpec(
            num_scalar_prefetch=2,
            grid=(total // 2 // tile,),
            in_specs=[pl.BlockSpec((total, wide), lambda n, *refs: (0, 0), pipeline_mode=pl.Buffered(1))]
            + [held] * count
            + [pl.BlockSpec(memory_space=pl.ANY)],
            out_specs=[pl.BlockSpec((tile, width), lambda n, *refs: (n, 0))] * 2,
        ),
        out_shape=[out, out],
        compiler_params=pltpu.CompilerParams(vmem_limit_bytes=40 * 2**20),
        cost_estimate=pl.CostEstimate(
            flops=2 * total * width * wide, bytes_accessed=2 * total * (width + wide), transcendentals=0
        ),
    )(layers, blocks, grads, *weights, dep)


def turn(value, cosine, sine):
    return value * cosine + pltpu.roll(value, HEAD_DIM // 2, 1) * sine


def masked_scores(queries, keys, first, score_scale):
    scores = times_transposed(queries, keys) * score_scale
    row = lax.broadcasted_iota(jnp.int32, scores.shape, 0) + first
    col = lax.broadcasted_iota(jnp.int32, scores.shape, 1)
    return scores, col <= row


def attention_kernel(
    half, tile, score_scale, place_ref, q_pre, k_pre, v_pre, inv, gains, cosine, sine,
    sent, attended, lse, query_rot, key_rot, value,
):
    rows = q_pre.shape[0]
    cos, sin = cosine[...], sine[...]
    query_rot[...] = turn(q_pre[...] * columns(inv[0:1]) * gains[0:1], cos, sin).astype(BF)
    key_rot[...] = turn(k_pre[...] * columns(inv[1:2]) * gains[1:2], cos, sin).astype(BF)
    value[...] = v_pre[...].astype(BF)
    for n in range(rows // tile):
        first = n * tile
        end = first + tile
        scores, allowed = masked_scores(query_rot[first:end], key_rot[:end], first, score_scale)
        scores = jnp.where(allowed, scores, NEG_LARGE)
        top = jnp.max(scores, axis=-1, keepdims=True)
        probs = jnp.exp(scores - top)
        total = jnp.sum(probs, axis=-1, keepdims=True)
        lse[first:end] = jnp.broadcast_to(top + jnp.log(total), (tile, HEAD_DIM))
        attended[first:end] = dot((probs / total).astype(BF), value[:end])
    for n in range(rows // half):
        place = pl.multiple_of(place_ref[n] * half, half)
        sent[pl.ds(place, half)] = attended[n * half : (n + 1) * half].astype(BF)


def attention_grad_kernel(
    half, tile, score_scale, place_ref, sent_grad, attended, lse, query_rot, key_rot, value, q_pre, k_pre, inv, gains,
    cosine, sine, scaled_q, scaled_k, grad_value, dots, grad_gains, grad_heads, key_sum, value_sum, query_sum,
):
    rows = q_pre.shape[0]
    for n in range(rows // half):
        place = pl.multiple_of(place_ref[n] * half, half)
        grad_heads[n * half : (n + 1) * half] = sent_grad[pl.ds(place, half)]
    key_sum[...] = jnp.zeros_like(key_sum)
    value_sum[...] = jnp.zeros_like(value_sum)
    for n in range(rows // tile):
        first = n * tile
        end = first + tile
        grads = grad_heads[first:end]
        queries = query_rot[first:end]
        delta = jnp.sum(grads.astype(F32) * attended[first:end], axis=-1, keepdims=True)
        scores, allowed = masked_scores(queries, key_rot[:end], first, score_scale)
        probs = jnp.where(allowed, jnp.exp(scores - lse[first:end][:, :1]), 0.0)
        grad_scores = (probs * (times_transposed(grads, value[:end]) - delta)).astype(BF)
        query_sum[first:end] = dot(grad_scores, key_rot[:end])
        key_sum[:end] += contract_rows(grad_scores, queries)
        value_sum[:end] += contract_rows(probs.astype(BF), grads)
    grad_value[...] = value_sum[...].astype(BF)
    cos, sin = cosine[...], -sine[...]
    for n, (total, pre, scaled) in enumerate(((query_sum, q_pre, scaled_q), (key_sum, k_pre, scaled_k))):
        grad = turn(total[...] * score_scale, cos, sin)
        grad_gains[n : n + 1] = jnp.sum(grad * pre[...] * columns(inv[n : n + 1]), axis=0, keepdims=True)
        grad = grad * gains[n : n + 1]
        scaled[...] = grad
        dots[n : n + 1] = as_rows(jnp.sum(grad * pre[...], axis=-1, keepdims=True))


class Attention:
    def __init__(self, rows, half, hpd):
        self.rows, self.half, self.hpd = rows, half, hpd
        self.tile = min(256, rows)
        position = np.arange(rows, dtype=np.float32)
        freq = np.exp(np.arange(HEAD_DIM // 2, dtype=np.float32) * np.float32(-2.0 * math.log(10000.0) / HEAD_DIM))
        angles = position[:, None] * freq[None, :].astype(np.float32)
        self.cosine = jnp.asarray(np.concatenate([np.cos(angles)] * 2, axis=1), F32)
        self.sine = jnp.asarray(np.concatenate([-np.sin(angles), np.sin(angles)], axis=1), F32)
        self.head = pl.BlockSpec((rows, HEAD_DIM), lambda h, place: (0, h))
        self.keys = pl.BlockSpec((rows, HEAD_DIM), lambda h, place: (0, h + hpd))
        self.values = pl.BlockSpec((rows, HEAD_DIM), lambda h, place: (0, h + 2 * hpd))
        self.stat = pl.BlockSpec((2, rows), lambda h, place: (0, 0))
        self.gain = pl.BlockSpec((2, HEAD_DIM), lambda h, place: (0, h))
        self.table = pl.BlockSpec((rows, HEAD_DIM), lambda h, place: (0, 0))
        self.args = (half, self.tile, 1.0 / math.sqrt(HEAD_DIM))
        self.params = pltpu.CompilerParams(vmem_limit_bytes=60 * 2**20)

    def shape(self, dtype):
        return jax.ShapeDtypeStruct((self.rows, self.hpd * HEAD_DIM), dtype)

    def cost(self, products):
        area = self.hpd * self.rows * self.rows
        return pl.CostEstimate(
            flops=products * area * HEAD_DIM, bytes_accessed=self.hpd * self.rows * HEAD_DIM * 24, transcendentals=area
        )

    def call(self, kernel, ins, outs, shapes, scratch, products):
        return pl.pallas_call(
            functools.partial(kernel, *self.args),
            grid_spec=pltpu.PrefetchScalarGridSpec(
                num_scalar_prefetch=1, grid=(self.hpd,), in_specs=ins, out_specs=outs, scratch_shapes=scratch
            ),
            out_shape=shapes,
            compiler_params=self.params,
            cost_estimate=self.cost(products),
        )

    def forward(self, places, qkv, inv, gains):
        ins = [self.head, self.keys, self.values, self.stat, self.gain, self.table, self.table]
        shapes = [self.shape(t) for t in (BF, F32, F32, BF, BF, BF)]
        run = self.call(attention_kernel, ins, [self.head] * 6, shapes, [], 3)
        return run(places, qkv, qkv, qkv, inv, gains, self.cosine, self.sine)

    def backward(self, places, sent_grad, kept, qkv, inv, gains):
        rows, hpd = self.rows, self.hpd
        line = pl.BlockSpec((None, 2, rows), lambda h, place: (h, 0, 0))
        ins = [self.head] * 6 + [self.head, self.keys, self.stat, self.gain, self.table, self.table]
        shapes = [self.shape(F32), self.shape(F32), self.shape(BF)]
        shapes += [jax.ShapeDtypeStruct((hpd, 2, rows), F32), jax.ShapeDtypeStruct((2, hpd * HEAD_DIM), F32)]
        scratch = [pltpu.VMEM((rows, HEAD_DIM), BF)] + [pltpu.VMEM((rows, HEAD_DIM), F32)] * 3
        run = self.call(attention_grad_kernel, ins, [self.head] * 3 + [line, self.gain], shapes, scratch, 6)
        return run(places, sent_grad, *kept, qkv, qkv, inv, gains, self.cosine, self.sine)


class Gathered:
    def __init__(self, lay, routes, expert_count, capacity, width):
        self.lay, self.kinds, self.capacity, self.width = lay, expert_count, capacity, width
        self.tok_rows = routes.shape[0]
        chosen = routes[:, :, None] == jnp.arange(expert_count, dtype=jnp.int32)
        self.chosen = jnp.any(chosen, axis=1)
        first = lay.dz * (lay.nc // 2)
        flipped = first + (lay.cx ^ jnp.array([0] + lay.flips, jnp.int32)) // 2
        self.flipped = flipped.astype(jnp.int32)
        self.own = self.flipped[:1]
        self.straight = (first + jnp.arange(lay.nc // 2)).astype(jnp.int32)

    def noted(self, rows, *notes):
        notes = [self.chosen.astype(BF)] + list(notes)
        rest = NOTES - self.kinds * len(notes)
        return jnp.concatenate([rows] + notes + [jnp.zeros((self.tok_rows, rest), BF)], axis=1)

    def offer(self, block, width=None):
        return pick_rows(block, self.straight, self.capacity, width or block.shape[1])

    def exchange(self, offered):
        groups = [list(range(core, self.lay.nc, 2)) for core in (0, 1)]
        return lax.all_to_all(
            offered, "ctx", split_axis=0, concat_axis=0, tiled=True, axis_index_groups=groups
        )

    def send_back(self, sums):
        chip = self.lay.cx // 2
        parts = [
            lax.dynamic_slice_in_dim(sums, (chip ^ n) * self.capacity, self.capacity, 0)
            for n in range(self.lay.nc // 2)
        ]
        return [parts[0]] + [self.lay.swap(p, flip) for p, flip in zip(parts[1:], self.lay.flips)]

    def spread(self, step, parts, total):
        experts = self.flipped if len(parts) > 1 else self.straight
        return spread_rows(self.blocks[step], experts, parts, total, self.capacity)

    def straighten(self, parts):
        chip = self.lay.cx // 2
        whole = jnp.zeros((len(parts) * self.capacity, parts[0].shape[1]), parts[0].dtype)
        for n, part in enumerate(parts):
            whole = lax.dynamic_update_slice_in_dim(whole, part, (chip ^ n) * self.capacity, 0)
        return whole

    def run(self, block, dy, dy_last, gate_w, up_w, down_w):
        lay, nz = self.lay, self.lay.nz
        self.blocks = blocks = [block]
        self.rows, self.done, self.dy = rows, done, dy = [], [], dy
        back, far_sums = {}, {}
        near = self.exchange(self.offer(block))
        coming = lay.ring_step(block)
        coming, near = sync(coming, near)
        for step in range(nz):
            far = lay.swap(near, 1)
            rows += [near, far]
            if step:
                far_sums[step - 1] = lay.swap(done[-1][1], 1)
            if step + 1 < nz:
                blocks.append(coming)
                near = self.exchange(self.offer(coming))
                if step + 2 < nz:
                    coming = lay.ring_step(coming)
            if step == 0:
                late = self.send_back(dy_last)
            if step == nz - 2:
                last_dy = self.straighten(late)
                dy.append([last_dy, lay.swap(last_dy, 1)])
            sent, deps = [], []
            if step == nz - 1:
                for n in range(1, nz - 1):
                    deps.append(add_rows(done[n][0], far_sums[n]))
                    back[n] = [self.exchange(deps[-1])] if n == 1 else self.send_back(deps[-1])
                    sent += back[n]
            made = list(
                expert_chunk(self.kinds, self.own, *rows[-2:], *dy[step], gate_w, up_w, down_w, *deps)
            )
            held = [made[1], coming] + ([near] if step + 1 < nz else [])
            held += sent[:1] + (late[1:] if step == 1 else []) + (dy[-1][1:] if step == nz - 2 else [])
            held += [far_sums[0]] if step == nz - 1 else []
            held = list(sync(*held))
            made[1], coming = held[:2]
            if step + 1 < nz:
                near = held[2]
            if step == 1:
                late[1:] = held[3:]
            if step == nz - 2:
                dy[-1][1] = held[3]
            if step == nz - 1:
                back[1], far_sums[0] = held[2:3], held[3]
            done.append(made)
        self.grads = {}
        total = self.spread(1, back[1], None)
        far_sums[nz - 1] = lay.swap(done[-1][1], 1)
        for n, step in enumerate(list(range(2, nz)) + [0]):
            coming = lay.ring_step(total)
            if step not in back:
                sums = add_rows(done[step][0], far_sums[step])
                back[step] = [self.exchange(sums)] if step == nz - 1 else self.send_back(sums)
            beside = list(back[step])
            if n < 3:
                self.grads[n] = self.weight_grads(n, total)
                beside.append(self.grads[n])
            if n == 0:
                beside.append(far_sums[nz - 1])
            coming, *beside = sync(coming, *beside)
            if n == 0:
                far_sums[nz - 1] = beside.pop()
            if n < 3:
                self.grads[n] = beside.pop()
            if step == nz - 1:
                beside[0], far_sums[0] = sync(beside[0], far_sums[0])
            total = self.spread(step, beside, coming)
        return total[:, : self.width].astype(F32), total[:, self.width : self.width + self.kinds].astype(F32)

    def out_sum(self, step, *deps):
        near, far = self.done[step][-2:]
        return add_rows(near, self.lay.swap(far, 1), *deps)

    def weight_grads(self, which, dep):
        near = 2 + 2 * which
        mids = [d[k] for d in self.done for k in (near, near + 1)]
        units = mids[0].shape[1]
        if which == 0:
            return contract_many(mids, [d for pair in self.dy for d in pair], units, self.width, dep)
        return contract_many(self.rows, mids, self.width, units, dep)


def experts_sent(lay, mlp_normed, routes, router_probs, grad_result, gate_w, up_w, down_w):
    tok_rows, width = mlp_normed.shape
    expert_count = router_probs.shape[1]
    capacity = 3 * tok_rows * TOP // (2 * expert_count)
    flat_routes = routes.reshape(tok_rows * TOP)
    onehot = (flat_routes[:, None] == jnp.arange(expert_count, dtype=jnp.int32)[None, :]).astype(
        jnp.int32
    )
    slot_index = jnp.sum((jnp.cumsum(onehot, axis=0) - onehot) * onehot, axis=1)
    chosen = onehot.reshape(tok_rows, TOP, expert_count).astype(F32)
    gate_values = jnp.einsum("tke,te->tk", chosen, router_probs)

    def dispatch(rows_in):
        sent = jnp.zeros((expert_count, capacity, width), BF).at[flat_routes, slot_index].set(rows_in)
        return a2a(jnp.repeat(sent, 2, axis=0), ALL)

    def collect(buffer):
        even_rows = buffer[2 * flat_routes, slot_index].astype(F32)
        odd_rows = buffer[2 * flat_routes + 1, slot_index].astype(F32)
        return (even_rows + odd_rows).reshape(tok_rows, TOP, width)

    received = dispatch(jnp.repeat(mlp_normed, TOP, axis=0))
    flat_in = received.reshape(-1, width)
    gate_pre = dot(flat_in, gate_w)
    up_pre = dot(flat_in, up_w)
    hidden = (jax.nn.silu(gate_pre) * up_pre).astype(BF)
    half_out = dot(hidden, down_w).astype(BF).reshape(received.shape)
    expert_rows = collect(a2a(half_out, ALL))
    mixture = jnp.einsum("tk,tkd->td", gate_values, expert_rows)
    grad_gates = jnp.einsum("td,tkd->tk", grad_result, expert_rows)
    grad_rows = (
        (gate_values[:, :, None] * grad_result[:, None, :])
        .astype(BF)
        .reshape(tok_rows * TOP, width)
    )
    grad_flat = dispatch(grad_rows).reshape(-1, width)
    grad_down_w = contract_rows(hidden, grad_flat)
    grad_hidden = times_transposed(grad_flat, down_w)
    sigmoid_val = jax.nn.sigmoid(gate_pre)
    grad_gate_pre = (
        grad_hidden * up_pre * sigmoid_val * (1.0 + gate_pre * (1.0 - sigmoid_val))
    ).astype(BF)
    grad_up_pre = (grad_hidden * jax.nn.silu(gate_pre)).astype(BF)
    grad_gate_w = contract_rows(flat_in, grad_gate_pre)
    grad_up_w = contract_rows(flat_in, grad_up_pre)
    grad_copy = (
        (times_transposed(grad_gate_pre, gate_w) + times_transposed(grad_up_pre, up_w))
        .astype(BF)
        .reshape(received.shape)
    )
    grad_sum = jnp.sum(collect(a2a(grad_copy, ALL)), axis=1)
    weighted = router_probs * jnp.einsum("tk,tke->te", grad_gates, chosen)
    return (mixture, grad_sum, weighted, (grad_down_w, grad_gate_w, grad_up_w))


def body(
    tokens,
    routes,
    cotangent,
    attn_gain,
    query_weight,
    key_weight,
    value_weight,
    query_gain,
    key_gain,
    out_weight,
    mlp_gain,
    router_weight,
    gate_weight,
    up_weight,
    down_weight,
):
    rb = query_weight.shape[0]
    lay = Layout(rb)
    nz, nc, cx = lay.nz, lay.nc, lay.cx
    tok_rows = tokens.shape[1]
    width = tokens.shape[2]
    half = tok_rows // 2
    seq_rows = tok_rows * nc
    expert_count = router_weight.shape[1]
    hpd, cols = lay.hpd, lay.cols
    devices = nz * nc
    capacity = 3 * tok_rows * TOP // (2 * expert_count)
    gathered = (
        nz > 3
        and devices * tok_rows <= 4 * expert_count * capacity
        and 3 * expert_count <= NOTES
        and capacity % 16 == 0
    )

    sent = jnp.concatenate(
        [lay.head_blocks(w) for w in (query_weight, key_weight, value_weight)], axis=-1
    )
    kinds = expert_count + 4
    small = jnp.concatenate(
        [router_weight] + [g[:, None] for g in (query_gain, key_gain, mlp_gain, attn_gain)], axis=1
    )
    small = jnp.broadcast_to(small.T.reshape(1, kinds * rb), (devices, kinds * rb))
    block = a2a(sent, "ctx").reshape(nc * rb, 3 * cols)
    parts = [tokens[0]] + [lay.swap(tokens[0], flip) for flip in lay.flips]
    places = lay.arrival_place()
    places = jnp.concatenate([places * 2, (places * 2 + 1)[::-1]]).astype(jnp.int32)
    if gathered:
        moe = Gathered(lay, routes[0], expert_count, capacity, width)
        dy_blocks = [moe.noted(cotangent[0])]
        dy_blocks.append(lay.ring_step(dy_blocks[0]))
        offered = moe.offer(dy_blocks[0], width)
    out_blocks = [out_weight, lay.ring_step(out_weight)]
    if gathered:
        block, out_blocks[1], dy_blocks[1], offered, *parts[1:3] = sync(
            block, out_blocks[1], dy_blocks[1], offered, *parts[1:3]
        )
    ring, dy = [block], []
    for step in range(1, nz):
        block = lay.ring_step(block)
        beside = []
        if step == 1:
            beside = [a2a(small, ALL)] + parts[1:]
        elif step == 2:
            seq_near = jnp.concatenate(parts, axis=0)
            beside = [lay.swap(seq_near, 1)]
        elif step == 3:
            beside = [norm_in_order(places, seq_near, seq_far, attn_gain_f[None], half)]
            if nz == 4:
                beside.append(lay.head_weights(out_blocks))
        if gathered and step > 1:
            dy.append([moe.exchange(offered)])
            beside.append(dy[-1][0])
            if step == 2:
                offered = moe.offer(dy_blocks[1], width)
                beside.append(offered)
        if step + 1 < nz:
            beside.append(lay.ring_step(out_blocks[-1]))
        block, out_blocks[-1], *beside = sync(block, out_blocks[-1], *beside)
        if step + 1 < nz:
            out_blocks.append(beside.pop())
        if step == 1:
            small, parts[1:] = beside[0], beside[1:]
            small = small.reshape(devices, kinds, rb).transpose(1, 0, 2).reshape(kinds, width)
            router_t = small[:expert_count]
            qgain_f, kgain_f, mlp_gain_f, attn_gain_f = (small[expert_count + k].astype(F32) for k in range(4))
        elif step == 2:
            seq_far = beside[0]
        elif step == 3:
            normed = beside[0]
            if nz == 4:
                out_rows = beside.pop(1)
        if gathered and step > 1:
            dy[-1][0] = beside[1]
            if step == 2:
                offered = beside[2]
        ring.append(block)
    if nz < 4:
        normed = norm_in_order(places, seq_near, seq_far, attn_gain_f[None], half)
    if nz != 4:
        out_rows = lay.head_weights(out_blocks)
    if gathered:
        dy_blocks.append(lay.ring_step(after(dy_blocks[1], ring[-1])))
    layers = jnp.stack([lay.layer_at(step) for step in range(nz)]).astype(jnp.int32)
    qkv, squares = project(layers, normed, ring, cols)
    query_pre, key_pre = qkv[:, :cols], qkv[:, cols : 2 * cols]

    def sum_heads(stats):
        stats = lax.all_gather(stats.reshape(2 * seq_rows // 128, 128), "ctx", axis=0).sum(0)
        return stats.reshape(2, seq_rows) / width

    inv = lax.rsqrt(sum_heads(squares) + EPSILON)
    own_gains = jnp.stack([lay.own_heads(qgain_f), lay.own_heads(kgain_f)])
    attention = Attention(seq_rows, half, hpd)
    if gathered:
        inv, dy_blocks[2] = sync(inv, dy_blocks[2])
        dy_blocks.append(lay.ring_step(dy_blocks[2]))
        dy.append([moe.exchange(moe.offer(dy_blocks[2], width))])
        for pair in dy[:2]:
            pair.append(lay.swap(pair[0], 1))
    attended_b, *kept = attention.forward(places, qkv, inv, own_gains)
    if gathered:
        attended_b, out_rows, dy_blocks[3], dy[2][0], dy[0][1], dy[1][1] = sync(
            attended_b, out_rows, dy_blocks[3], dy[2][0], dy[0][1], dy[1][1]
        )
    near, far = (dot(attended_b[part], out_rows).astype(BF) for part in (slice(0, seq_rows // 2), slice(seq_rows // 2, None)))
    branch = near.astype(F32) + lay.swap(far, 1).astype(F32)
    if gathered:
        offered = moe.offer(dy_blocks[3], width)
        branch, offered = sync(branch.astype(BF), offered)
        dy[2].append(lay.swap(dy[2][0], 1))
    branch = lay.reduce_chips(branch.astype(BF))
    if gathered:
        branch, dy[2][1], offered = sync(branch, dy[2][1], offered)
    inputs_f = tokens[0].astype(F32)
    middle = inputs_f + branch.astype(F32)
    mlp_inv = inverse_rms(middle)
    mlp_normed = (middle * mlp_inv * mlp_gain_f).astype(BF)
    router_probs = jax.nn.softmax(times_transposed(mlp_normed, router_t), axis=-1)
    grad_result = cotangent[0].astype(F32)
    if gathered:
        combine = jnp.where(moe.chosen, router_probs, 0.0)
        high = combine.astype(BF)
        block = moe.noted(mlp_normed, high, (combine - high.astype(F32)).astype(BF))
        grad_mlp_normed, weighted = moe.run(
            block, dy, offered, gate_weight[0], up_weight[0], down_weight[0]
        )
    else:
        mixture, grad_mlp_normed, weighted, weight_grads = experts_sent(
            lay, mlp_normed, routes[0], router_probs, grad_result, gate_weight[0], up_weight[0], down_weight[0]
        )
    grad_logits = (weighted - router_probs * jnp.sum(weighted, axis=-1, keepdims=True)).astype(BF)
    grad_router_t = contract_rows(grad_logits, mlp_normed)
    grad_mlp_normed = grad_mlp_normed + dot(grad_logits, router_t)
    grad_middle_norm, grad_mlp_gain = norm_backward(middle, mlp_inv, mlp_gain_f, grad_mlp_normed)
    grad_middle = grad_result + grad_middle_norm
    grad_branch = grad_middle.astype(BF)
    branch_near = lay.gather_near(grad_branch)
    if gathered:
        branch_near, first, *out_sums = sync(branch_near, *(moe.out_sum(n) for n in (1, 2, 3, 0)))
        first, second = moe.exchange(first), moe.send_back(out_sums.pop(0))
    branch_far = lay.swap(branch_near, 1)
    grad_heads = jnp.concatenate(
        [times_transposed(part, out_rows).astype(BF) for part in (branch_near, branch_far)], axis=0
    )
    scaled_q, scaled_k, grad_value, dots, grad_gains = attention.backward(places, grad_heads, kept, qkv, inv, own_gains)
    packed = jnp.concatenate(
        [grad_router_t]
        + [g[None] for g in (lay.all_heads(grad_gains[0]), lay.all_heads(grad_gains[1]), grad_mlp_gain)],
        axis=0,
    )
    kinds = expert_count + 3
    packed = packed.reshape(kinds, devices, rb).transpose(1, 0, 2).reshape(devices, kinds * rb)
    if gathered:
        dots, first, packed = sync(dots, first, packed)
        mixture = lay.ring_step(moe.spread(1, [first], None))
    packed = a2a(packed, ALL)
    dots = sum_heads(dots.sum(0))
    if gathered:
        dots, packed, mixture = sync(dots, packed, mixture)

    def through_norm(scaled, pre, n):
        inverse = inv[n][:, None]
        return (inverse * scaled - pre * (inverse * inverse * inverse) * dots[n][:, None]).astype(BF)

    grad_pre = jnp.concatenate(
        [through_norm(scaled_q, query_pre, 0), through_norm(scaled_k, key_pre, 1), grad_value], axis=-1
    )
    grad_qkv = grad_blocks(layers, normed, grad_pre)
    halves = jnp.stack([lay.arrival(), 2 * nc - 1 - lay.arrival()], axis=1).reshape(-1).astype(jnp.int32)
    share = cx % lay.group

    def out_terms(near, far):
        grad_out = contract_rows(attended_b[: seq_rows // 2], near) + contract_rows(attended_b[seq_rows // 2 :], far)
        grad_out = grad_out.astype(BF).reshape(hpd, lay.group, rb, width)
        terms = []
        for k in range(lay.group):
            term = lax.dynamic_index_in_dim(grad_out, share ^ k, 1, keepdims=False)
            terms.append(lay.swap(term, k) if k else term)
        return jnp.stack(terms)

    def out_part(terms, step):
        layer = lay.layer_at(step)
        return terms[(layer // hpd) ^ share, layer % hpd]

    total = grad_qkv[1]
    if not gathered:
        mixture = mixture.astype(BF)
    for n, step in enumerate(list(range(2, nz)) + [0]):
        ready = total
        total = lay.ring_step(total)
        if n == 0:
            near, far = project_back(layers, halves, grad_pre, ring, half, ready)
            beside = second + out_sums if gathered else []
            total, near, far, branch_near, *beside = sync(total, near, far, branch_near, *beside)
        elif n == 1:
            terms = out_terms(branch_near, branch_far)
            grad_normed = lay.reduce_chips(both)
            if gathered:
                mixture = lay.ring_step(moe.spread(2, beside[:-2], mixture))
                part = moe.exchange(beside[-2])
                beside = [mixture, part, beside[-1]]
            total, terms, grad_normed, *beside = sync(total, terms, grad_normed, *beside)
        elif n == 2:
            out_total = lay.ring_step(out_part(terms, 1))
            if gathered:
                mixture, part, last = beside
                mixture = moe.spread(3, [part], mixture)
                last = moe.exchange(last)
                total, out_total, mixture, last = sync(total, out_total, mixture, last)
                mixture = lay.ring_step(mixture)
        total = (total.astype(F32) + grad_qkv[step].astype(F32)).astype(BF)
        if n == 0:
            both = (near.astype(F32) + lay.swap(far, 1).astype(F32)).astype(BF)
            both, branch_near, *beside = sync(both, branch_near, *beside)
        elif n == 1:
            total, terms, *beside = sync(total, terms, *beside)
    grad_qkv = a2a(total.reshape(nc, rb, 3 * cols), "ctx")
    for step in list(range(2, nz)) + [0]:
        out_total = (out_total.astype(F32) + out_part(terms, step).astype(F32)).astype(BF)
        if step:
            out_total = lay.ring_step(out_total)
    grad_out_w = out_total.astype(F32)
    if gathered:
        weight_grads = [moe.grads[n] for n in range(3)]
    if gathered:
        mixture = moe.spread(0, [last], mixture)
    grad_down_w, grad_gate_w, grad_up_w = weight_grads
    result = middle + mixture.astype(F32)
    grad_query_w, grad_key_w, grad_value_w, grad_attn_gain = lay.weight_rows(
        grad_qkv, (query_weight, key_weight, value_weight), attn_gain
    )
    grad_attn_gain = grad_attn_gain[0]
    attn_inv = inverse_rms(inputs_f)
    scaled = grad_normed.astype(F32) * attn_gain_f
    grad_inputs = (
        grad_middle
        + attn_inv * scaled
        - inputs_f * (attn_inv * attn_inv * attn_inv) * jnp.mean(scaled * inputs_f, axis=-1, keepdims=True)
    )
    packed = packed.sum(0).reshape(kinds, rb)
    gains = [grad_attn_gain] + [packed[expert_count + k] for k in range(3)]
    return (
        result.astype(BF)[None],
        grad_inputs.astype(BF)[None],
        gains[0],
        grad_query_w,
        grad_key_w,
        grad_value_w,
        gains[1],
        gains[2],
        grad_out_w,
        gains[3],
        packed[:expert_count].T,
        grad_gate_w[None],
        grad_up_w[None],
        grad_down_w[None],
    )


def solution(mesh):
    both = ("dp", "ctx")
    in_specs = (
        P("dp", "ctx", None),
        P("dp", "ctx", None),
        P("dp", "ctx", None),
        P(both),
        P(both, None),
        P(both, None),
        P(both, None),
        P(both),
        P(both),
        P(both, None),
        P(both),
        P(both, None),
        P(both, None, None),
        P(both, None, None),
        P(both, None, None),
    )
    out_specs = (
        P("dp", "ctx", None),
        P("dp", "ctx", None),
        P(both),
        P(both, None),
        P(both, None),
        P(both, None),
        P(both),
        P(both),
        P(both, None),
        P(both),
        P(both, None),
        P(both, None, None),
        P(both, None, None),
        P(both, None, None),
    )
    return jax.shard_map(body, mesh=mesh, in_specs=in_specs, out_specs=out_specs, check_vma=False)
```
